512 devices in a mesh: blk: 128 (over y_lo, x, z), feat: 4 (over y_hi, core).
Axes of the slice: x: 4, y: 4 (y_hi: 2, y_lo: 2; y = y_hi * 2 + y_lo), z: 16, core: 2. Of those that a mesh axis runs over, the one named last changes fastest.
Arguments:
- series: bfloat16 [131072, 2048], P('blk', 'feat'), may hold values from -12 to 12
- scales: bfloat16 [131072], P('blk'), may hold values from 0.69921875 to 1.3984375
- width: float32 [1], replicated, may hold values from 2 to 4
Outputs:
- kernel_same: float32 [131072, 1024], P(('blk', 'feat'))
- kernel_next: float32 [131072, 1024], P(('blk', 'feat'))
- kernel_prev: float32 [131072, 1024], P(('blk', 'feat'))
The draws below stay inside these ranges and needn't reach their ends.
All inputs are finite; a program needn't handle non-finite values.
Results may differ from the reference program's by a relative error of at most 0.0003.
Values may be sent and summed in bfloat16 or wider, within the bound.
A program may use at most 64 MiB of HBM per device.

```python
import math
import jax
import jax.numpy as jnp
from jax import lax

D = 2048
BLOCK = 1024
LAGS = 24
SNAPSHOTS = 131072
N_BLK = 128


def mode_waves(freq_key, phase_key, count_modes):
    slow_key = jax.random.fold_in(freq_key, 1)
    middle_key = jax.random.fold_in(freq_key, 2)
    quick_key = jax.random.fold_in(freq_key, 3)
    slow = jax.random.randint(slow_key, (2,), 1, 5, jnp.int32)
    middle = jax.random.randint(middle_key, (2,), max(1, N_BLK // 4), 2 * N_BLK + 1, jnp.int32)
    quick = N_BLK * jax.random.randint(quick_key, (count_modes - 4,), 2, 9, jnp.int32)
    freqs = jnp.concatenate([slow, middle, quick], axis=0)
    times = jnp.arange(SNAPSHOTS, dtype=jnp.int32)
    cycle = times[:, None] * freqs[None, :] % SNAPSHOTS
    phases = jax.random.uniform(phase_key, (count_modes,), jnp.float32, 0.0, 2.0 * math.pi)
    return jnp.cos(2.0 * math.pi * cycle.astype(jnp.float32) / SNAPSHOTS + phases[None, :])


def draw_series(key, part):
    key = jax.random.fold_in(key, 11)
    noise_key = jax.random.fold_in(key, 1)
    level_key = jax.random.fold_in(key, 2)
    freq_key = jax.random.fold_in(key, 3)
    phase_key = jax.random.fold_in(key, 4)
    amp_key = jax.random.fold_in(key, 5)
    pattern_key = jax.random.fold_in(key, 6)
    count_modes = 6
    waves = mode_waves(freq_key, phase_key, count_modes)
    patterns = jax.random.uniform(pattern_key, (count_modes, D), jnp.float32, -1.732, 1.732)
    levels = jnp.exp(jax.random.uniform(level_key, (SNAPSHOTS, 1), jnp.float32, math.log(0.7), math.log(1.3)))
    noise = jnp.clip(jax.random.normal(noise_key, (SNAPSHOTS, D), jnp.float32), -4.0, 4.0)
    amps = jnp.exp(jax.random.uniform(amp_key, (count_modes,), jnp.float32, math.log(0.35), math.log(0.6)))
    mixed = noise + 0.8 * jnp.roll(noise, 1, axis=0) + 0.5 * jnp.roll(noise, 2, axis=0)
    total = 0.6 * levels * mixed / 1.37
    for mode in range(count_modes):
        total = total + amps[mode] * waves[:, mode:mode + 1] * patterns[mode][None, :]
    return total.astype(jnp.bfloat16)


def level_of(stream_key, shape, pieces, low, high):
    level = 1.0
    for position, parts in pieces:
        draws = jax.random.uniform(jax.random.fold_in(jax.random.fold_in(stream_key, 6), position), (parts,), jnp.float32, low / len(pieces), high / len(pieces))
        level = level * jnp.repeat(jnp.exp(draws), shape[position] // parts).reshape((-1,) + (1,) * (len(shape) - 1 - position))
    return level


def setup_inputs(seed: int = 0) -> dict:
    arg_keys = jax.random.split(jax.random.key(seed), 4)
    series = draw_series(jax.random.fold_in(arg_keys[3], 71), 0)
    scales = jnp.clip(jnp.exp(math.log(1.3984375) - 0.6931472 * jax.random.uniform(arg_keys[1], (SNAPSHOTS,), jnp.float32) ** level_of(arg_keys[1], (SNAPSHOTS,), ((0, 128),), -0.2, 0.2)), 0.69921875, 1.3984375).astype(jnp.bfloat16)
    width = jnp.clip(jax.random.uniform(arg_keys[2], (1,), jnp.float32, 2.0, 4.0), 2.0, 4.0)
    return dict(series=series, scales=scales, width=width)


def kernel_tile(rows_ext, cols_ext, row_scales, col_scales, width):
    nrows = rows_ext.shape[0] - (LAGS - 1)
    ncols = cols_ext.shape[0] - (LAGS - 1)
    gram = jnp.dot(rows_ext, cols_ext.T, precision=lax.Precision.HIGHEST)
    row_sq = jnp.sum(rows_ext * rows_ext, axis=1)
    col_sq = jnp.sum(cols_ext * cols_ext, axis=1)
    spread = row_sq[:, None] + col_sq[None, :] - 2.0 * gram
    total = spread[LAGS - 1:LAGS - 1 + nrows, LAGS - 1:LAGS - 1 + ncols]
    for lag in range(1, LAGS):
        total = total + spread[LAGS - 1 - lag:LAGS - 1 - lag + nrows, LAGS - 1 - lag:LAGS - 1 - lag + ncols]
    dist = total / (LAGS * D)
    denom = width[0] * row_scales.astype(jnp.float32)[:, None] * col_scales.astype(jnp.float32)[None, :]
    return jnp.exp(-dist / denom)


def reference(series, scales, width):
    data = series.astype(jnp.float32)
    padded = jnp.concatenate([data[SNAPSHOTS - (LAGS - 1):], data], axis=0)

    def tiles(index):
        start = (index * BLOCK).astype(jnp.int32)
        later = (((index + 1) % N_BLK) * BLOCK).astype(jnp.int32)
        own = lax.dynamic_slice_in_dim(padded, start, BLOCK + LAGS - 1, 0)
        after = lax.dynamic_slice_in_dim(padded, later, BLOCK + LAGS - 1, 0)
        own_scales = lax.dynamic_slice_in_dim(scales, start, BLOCK, 0)
        after_scales = lax.dynamic_slice_in_dim(scales, later, BLOCK, 0)
        same = kernel_tile(own, own, own_scales, own_scales, width)
        following = kernel_tile(own, after, own_scales, after_scales, width)
        return same, following

    same, following = lax.map(tiles, jnp.arange(N_BLK, dtype=jnp.int32))
    before = jnp.transpose(jnp.roll(following, 1, axis=0), (0, 2, 1))
    return (same.reshape(SNAPSHOTS, BLOCK), following.reshape(SNAPSHOTS, BLOCK), before.reshape(SNAPSHOTS, BLOCK))
```

```python
import functools

import jax
import jax.numpy as jnp
from jax import lax
from jax.experimental import pallas as pl
from jax.experimental.pallas import tpu as pltpu
from jax.sharding import PartitionSpec as P

LAGS = 24
LEAD = 32
LANE = 128
Z_SIZE = 16
PARTS = 4
MESH = pl.DeviceIdType.MESH
CONTRACT_LAST = (((1,), (1,)), ((), ()))


def multiple(value, of):
    return pl.multiple_of(value, of)


def tiles_kernel(
    blocks,
    series_ref,
    inv_ref,
    width_ref,
    same_ref,
    next_ref,
    prev_ref,
    whole,
    rows,
    nrows,
    ninv,
    gram,
    sums,
    norms,
    row_norms,
    row_factor,
    kept,
    turned,
    same_kept,
    local_sem,
    tail_send,
    tail_recv,
    sib_send,
    sib_recv,
    hop,
    turn_hop,
    raw_relay,
    tile_relay,
    hop_send,
    hop_recv,
    far_send,
    far_recv,
    pass_send,
    pass_recv,
    rows_send,
    rows_recv,
    inv_send,
    inv_recv,
    prev_send,
    prev_recv,
    turn_send,
    turn_recv,
    turn_hop_send,
    turn_hop_recv,
    raw_send,
    raw_recv,
    tile_send,
    tile_recv,
):
    block, quarter = series_ref.shape
    dims = 4 * quarter
    share = block // 4
    wide = block + LANE
    past = wide - LEAD

    b, f = lax.axis_index("blk"), lax.axis_index("feat")
    core, chip = lax.rem(f, 2), f // 2
    sib, far, cross = f + 1 - 2 * core, lax.rem(f + 2, 4), 3 - f
    after, before = lax.rem(b + 1, blocks), lax.rem(b + blocks - 1, blocks)
    half = blocks // 2
    pos, first = lax.rem(b, half), (b // half) * half
    over = lax.rem(b + half, blocks)
    near, side_z, side_x, end = first, first + Z_SIZE - 1, first + half - Z_SIZE, first + half - 1
    is_near, is_end = pos == 0, pos == half - 1
    is_side_z, is_side_x = pos == Z_SIZE - 1, pos == half - Z_SIZE
    is_side = jnp.logical_or(is_side_z, is_side_x)
    is_corner = jnp.logical_or(is_side, jnp.logical_or(is_near, is_end))
    others = (sib, far, cross)
    everyone = (f, sib, far, cross)

    barrier = pltpu.get_barrier_semaphore()
    peers = [(b, j) for j in others] + [(n, j) for n in (after, before) for j in everyone]
    peers += [(over, j) for j in (f, far, sib)]
    for peer in peers:
        pl.semaphore_signal(barrier, inc=1, device_id=peer, device_id_type=MESH)

    @pl.when(is_corner)
    def _():
        for corner in (near, side_z, side_x, end):

            @pl.when(corner != b)
            def _():
                pl.semaphore_signal(barrier, inc=1, device_id=(corner, f), device_id_type=MESH)

    @pl.when(is_corner)
    def _():
        pl.semaphore_wait(barrier, len(peers) + 3)

    @pl.when(jnp.logical_not(is_corner))
    def _():
        pl.semaphore_wait(barrier, len(peers))

    sent = []

    def post(src, dst, send_sem, recv_sem, to):
        pltpu.make_async_remote_copy(
            src_ref=src, dst_ref=dst, send_sem=send_sem, recv_sem=recv_sem, device_id=to, device_id_type=MESH
        ).start()

    def leaves(src, send_sem, recv_sem):
        sent.append(
            pltpu.make_async_remote_copy(
                src_ref=src, dst_ref=src, send_sem=send_sem, recv_sem=recv_sem, device_id=(b, sib), device_id_type=MESH
            )
        )

    def send(src, dst, send_sem, recv_sem, to):
        post(src, dst, send_sem, recv_sem, to)
        leaves(src, send_sem, recv_sem)

    def receive(dst, send_sem, recv_sem, sender):
        pltpu.make_async_remote_copy(
            src_ref=dst, dst_ref=dst, send_sem=send_sem, recv_sem=recv_sem, device_id=sender, device_id_type=MESH
        ).wait_recv()

    def cols(q):
        return pl.ds(multiple(q * quarter, quarter), quarter)

    def group(g):
        return pl.ds(multiple(g * share, share), share)

    def chunk(c, k):
        return group(lax.rem(2 * c + k, 4))

    here = pltpu.make_async_copy(series_ref, whole.at[pl.ds(0, block), cols(f)], local_sem.at[0])
    here.start()
    for i, j in enumerate(everyone):
        send(
            series_ref.at[pl.ds(block - LEAD, LEAD), :],
            whole.at[pl.ds(past, LEAD), cols(f)],
            tail_send.at[i],
            tail_recv.at[i],
            (after, j),
        )
    def halved(c, k, s):
        return pl.ds(multiple(lax.rem(2 * c + k, 4) * share + s * (share // 2), share // 2), share // 2)

    def set_out(k):
        for s, j in enumerate((f, far)):
            i = 4 * s + k
            send(
                series_ref.at[halved(1 - chip, k, s), :], hop.at[s, k], hop_send.at[i], hop_recv.at[i], (over, j)
            )

    def hand_over(k):
        for s, j in enumerate((f, far)):
            i = 4 * s + k
            receive(hop.at[s, k], hop_send.at[i], hop_recv.at[i], (over, j))
            c, to = (1 - chip, far) if s == 0 else (chip, f)
            send(hop.at[s, k], whole.at[halved(c, k, s), cols(j)], far_send.at[i], far_recv.at[i], (over, to))

    set_out(0)
    set_out(1)
    send(series_ref, whole.at[pl.ds(0, block), cols(f)], sib_send.at[0], sib_recv.at[0], (b, sib))
    send(inv_ref, ninv, inv_send.at[0], inv_recv.at[0], (before, f))

    def send_rows(q, i, src):
        @pl.when(pos != 0)
        def _():
            post(src, nrows.at[pl.ds(LEAD, share), cols(q)], rows_send.at[i], rows_recv.at[i], (before, f))

        @pl.when(pos == 0)
        def _():
            to = (side_z, side_x, over, end)[i]
            slot = 1 if i == 2 else 0
            post(src, raw_relay.at[slot], rows_send.at[i], raw_recv.at[slot], (to, f))

        leaves(src, rows_send.at[i], rows_recv.at[i])

    def relay_onward(buffer, slot, send_sem, recv_sem, sender, cases):
        receive(buffer.at[slot], send_sem.at[slot], recv_sem.at[slot], sender)
        for here_is, dst, dst_sem, to in cases:

            @pl.when(here_is)
            def _():
                post(buffer.at[slot], dst, send_sem.at[slot], dst_sem, to)

    def row_piece(i):
        return nrows.at[pl.ds(LEAD, share), cols(everyone[i])]

    def raw_out(here_is):
        @pl.when(here_is)
        def _():
            cases = (
                (is_end, row_piece(3), rows_recv.at[3], (over, f)),
                (is_side, raw_relay.at[1], raw_recv.at[1], (over, f)),
            )
            relay_onward(raw_relay, 0, raw_send, raw_recv, (near, f), cases)

    def raw_in(here_is):
        @pl.when(here_is)
        def _():
            cases = (
                (is_near, row_piece(2), rows_recv.at[2], (end, f)),
                (is_side_z, row_piece(0), rows_recv.at[0], (end, f)),
                (is_side_x, row_piece(1), rows_recv.at[1], (end, f)),
            )
            relay_onward(raw_relay, 1, raw_send, raw_recv, (over, f), cases)

    send_rows(f, 0, series_ref.at[group(f), :])
    whole[pl.ds(block, LANE - LEAD), :] = jnp.zeros((LANE - LEAD, dims), whole.dtype)
    gram[pl.ds(0, 8), :] = jnp.zeros((8, wide), jnp.float32)

    receive(whole.at[pl.ds(0, block), cols(sib)], sib_send.at[0], sib_recv.at[0], (b, sib))
    send_rows(sib, 1, whole.at[group(f), cols(sib)])

    def pass_on(k):
        part = chunk(chip, k)
        for s in range(2):
            i = 4 * s + k
            receive(
                whole.at[halved(chip, k, s), cols(far)], far_send.at[i], far_recv.at[i], (over, far if s == 0 else f)
            )
        send(whole.at[part, cols(far)], whole.at[part, cols(far)], pass_send.at[k], pass_recv.at[k], (b, sib))

    def passed(k):
        receive(whole.at[chunk(chip, k), cols(cross)], pass_send.at[k], pass_recv.at[k], (b, sib))

    hand_over(0)
    set_out(2)
    hand_over(1)
    set_out(3)
    pass_on(0)
    raw_out(is_side)
    hand_over(2)
    pass_on(1)
    send_rows(far, 2, whole.at[group(f), cols(far)])
    passed(0)
    passed(1)
    send_rows(cross, 3, whole.at[group(f), cols(cross)])
    raw_in(is_side)
    hand_over(3)
    pass_on(2)
    pass_on(3)
    raw_in(is_near)
    raw_out(is_end)
    passed(2)
    passed(3)
    for i, j in enumerate(everyone):
        receive(whole.at[pl.ds(past, LEAD), cols(j)], tail_send.at[i], tail_recv.at[i], (before, j))
    here.wait()
    lead = multiple(lax.rem(f * share + wide - LEAD, wide), LEAD)
    send(
        whole.at[pl.ds(lead, LEAD), :], nrows.at[pl.ds(0, LEAD), :], rows_send.at[4], rows_recv.at[4], (before, f)
    )

    def squares(x):
        total = jnp.zeros((x.shape[0], LANE), jnp.float32)
        for g in range(dims // LANE):
            piece = x[:, g * LANE : (g + 1) * LANE].astype(jnp.float32)
            total = total + piece * piece
        return total

    def norm_step(j, carry):
        part = pl.ds(multiple(j * LANE, LANE), LANE)
        norms[:, part] = jnp.broadcast_to(jnp.sum(squares(whole[part, :]).T, axis=0, keepdims=True), (8, LANE))
        return carry

    lax.fori_loop(0, wide // LANE, norm_step, 0)

    def lag_sum(x, axis):
        for step in (1, 2, 4):
            x = x + pltpu.roll(x, step, axis)
        return x + pltpu.roll(x, 8, axis) + pltpu.roll(x, 16, axis)

    norms[...] = lag_sum(norms[...], 1)
    inv_row = jnp.concatenate([inv_ref[j : j + 1, :] for j in range(block // LANE)], axis=1)
    width_row = jnp.full((1, LANE), width_ref[0], jnp.float32) * (LAGS * dims)

    def factors(ref):
        for j in range(share // LANE):
            line = ref[pl.ds(f * (share // LANE) + j, 1), :] / width_row
            row_factor[pl.ds(j * LANE, LANE), :] = jnp.broadcast_to(-line, (LANE, LANE)).T

    def tile(source, target, ready):
        def gram_step(j, carry):
            part = pl.ds(multiple(j * 256, 256), 256)
            gram[pl.ds(8, LEAD + share), part] = lax.dot_general(
                source[...], whole[part, :], CONTRACT_LAST, preferred_element_type=jnp.float32
            )
            return carry

        lax.fori_loop(0, block // 256, gram_step, 0)
        gram[pl.ds(8, LEAD + share), pl.ds(block, LANE)] = lax.dot_general(
            source[...], whole[pl.ds(block, LANE), :], CONTRACT_LAST, preferred_element_type=jnp.float32
        )

        def eight_lags(t, carry):
            x = gram[pl.ds(multiple(t * 32, 32), 40), :]
            for step in (1, 2, 4):
                x = x + pltpu.roll(pltpu.roll(x, step, 0), step, 1)
            sums[pl.ds(multiple(t * 32, 32), 32), :] = x[8:, :]
            return carry

        lax.fori_loop(0, (LEAD + share) // 32, eight_lags, 0)

        def finish(t, carry):
            x = sums[pl.ds(multiple(t * 32 + 32, 32), 32), :]
            x = x + pltpu.roll(sums[pl.ds(multiple(t * 32 + 24, 8), 32), :], 8, 1)
            x = x + pltpu.roll(sums[pl.ds(multiple(t * 32 + 16, 8), 32), :], 16, 1)
            part = pl.ds(multiple(t * 32, 32), 32)
            spread = row_norms[part, :][:, :1] + norms[pl.ds(0, 1), pl.ds(0, block)] - 2.0 * x[:, :block]
            target[part, :] = jnp.exp(spread * (row_factor[part, :][:, :1] * inv_row))
            return carry

        per = share // 32 // PARTS
        for h in range(PARTS):
            lax.fori_loop(h * per, (h + 1) * per, finish, 0)
            ready(pl.ds(h * per * 32, per * 32), h)

    for i, j in enumerate(everyone):
        receive(nrows.at[pl.ds(LEAD, share), cols(j)], rows_send.at[i], rows_recv.at[i], (after, f))
    receive(nrows.at[pl.ds(0, LEAD), :], rows_send.at[4], rows_recv.at[4], (after, f))
    receive(ninv, inv_send.at[0], inv_recv.at[0], (after, f))
    factors(ninv)
    lagged = jnp.broadcast_to(jnp.sum(squares(nrows[...]), axis=1, keepdims=True), (LEAD + share, LANE))
    row_norms[...] = lag_sum(lagged, 0)[LEAD:, :]

    def send_prev(part, h):
        @pl.when(pos != half - 1)
        def _():
            post(kept.at[part, :], prev_ref.at[part, :], prev_send.at[h], prev_recv.at[h], (after, f))

        @pl.when(pos == half - 1)
        def _():
            to = (side_z, side_x, near, over)[h]
            slot = 1 if h == 3 else 0
            post(kept.at[part, :], tile_relay.at[slot], prev_send.at[h], tile_recv.at[slot], (to, f))

        leaves(kept.at[part, :], prev_send.at[h], prev_recv.at[h])

    tile(nrows, kept, send_prev)

    def turn_step(j, carry):
        part = pl.ds(multiple(j * LANE, LANE), LANE)
        turned[part, :] = kept[:, part].T
        return carry

    lax.fori_loop(0, block // LANE, turn_step, 0)
    own_columns = pl.ds(multiple(f * share, share), share)
    send(turned.at[group(far), :], turn_hop.at[0], turn_hop_send.at[0], turn_hop_recv.at[0], (over, f))
    send(turned.at[group(cross), :], turn_hop.at[1], turn_hop_send.at[1], turn_hop_recv.at[1], (over, far))
    send(turned.at[group(sib), :], next_ref.at[:, own_columns], turn_send.at[2], turn_recv.at[2], (b, sib))
    own_turned = pltpu.make_async_copy(turned.at[group(f), :], next_ref.at[:, own_columns], local_sem.at[1])
    own_turned.start()

    rows[pl.ds(0, LEAD), :] = whole[pl.ds(lead, LEAD), :]
    rows[pl.ds(LEAD, share), :] = whole[group(f), :]
    factors(inv_ref)
    for j in range(share // LANE):
        line = norms[pl.ds(0, 1), pl.ds(multiple(f * share + j * LANE, LANE), LANE)]
        row_norms[pl.ds(j * LANE, LANE), :] = jnp.broadcast_to(line, (LANE, LANE)).T
    tile(rows, same_kept, lambda part, h: None)
    own_same = pltpu.make_async_copy(same_kept, same_ref, local_sem.at[2])
    own_same.start()

    for s, j, to in ((0, f, far), (1, far, sib)):
        receive(turn_hop.at[s], turn_hop_send.at[s], turn_hop_recv.at[s], (over, j))
        send(turn_hop.at[s], next_ref.at[:, group(j)], turn_send.at[s], turn_recv.at[s], (over, to))

    def piece(h):
        return pl.ds(h * (share // PARTS), share // PARTS)

    def tile_piece(h):
        return prev_ref.at[piece(h), :]

    @pl.when(jnp.logical_or(is_near, is_side))
    def _():
        cases = (
            (is_near, tile_piece(2), prev_recv.at[2], (over, f)),
            (is_side, tile_relay.at[1], tile_recv.at[1], (over, f)),
        )
        relay_onward(tile_relay, 0, tile_send, tile_recv, (end, f), cases)

    @pl.when(jnp.logical_or(is_end, is_side))
    def _():
        cases = (
            (is_end, tile_piece(3), prev_recv.at[3], (near, f)),
            (is_side_z, tile_piece(0), prev_recv.at[0], (near, f)),
            (is_side_x, tile_piece(1), prev_recv.at[1], (near, f)),
        )
        relay_onward(tile_relay, 1, tile_send, tile_recv, (over, f), cases)

    for h in range(PARTS):
        receive(tile_piece(h), prev_send.at[h], prev_recv.at[h], (before, f))
    for i, j in enumerate((far, cross, sib)):
        receive(next_ref.at[:, group(j)], turn_send.at[i], turn_recv.at[i], (b, j))
    own_turned.wait()
    own_same.wait()
    for copy in sent:
        copy.wait_send()

    def relayed(here_is, buffer, slot, send_sem, recv_sem):
        @pl.when(here_is)
        def _():
            pltpu.make_async_remote_copy(
                src_ref=buffer.at[slot],
                dst_ref=buffer.at[slot],
                send_sem=send_sem.at[slot],
                recv_sem=recv_sem.at[slot],
                device_id=(over, f),
                device_id_type=MESH,
            ).wait_send()

    relayed(jnp.logical_or(is_end, is_side), raw_relay, 0, raw_send, raw_recv)
    relayed(jnp.logical_or(is_near, is_side), raw_relay, 1, raw_send, raw_recv)
    relayed(jnp.logical_or(is_near, is_side), tile_relay, 0, tile_send, tile_recv)
    relayed(jnp.logical_or(is_end, is_side), tile_relay, 1, tile_send, tile_recv)


def per_device(blocks, series, scales, width):
    block, quarter = series.shape
    dims, share, wide = 4 * quarter, block // 4, block + LANE
    inv = (1.0 / scales.astype(jnp.float32)).reshape(block // LANE, LANE)
    out = jax.ShapeDtypeStruct((share, block), jnp.float32)
    dma = lambda n: pltpu.SemaphoreType.DMA((n,))
    early = (4, 4, 1, 1)
    late = (8, 8, 8, 8, 4, 4, 5, 5, 1, 1, PARTS, PARTS, 3, 3, 2, 2, 2, 2, 2, 2)
    return pl.pallas_call(
        functools.partial(tiles_kernel, blocks),
        out_shape=(out, out, out),
        in_specs=[
            pl.BlockSpec(memory_space=pl.ANY),
            pl.BlockSpec(memory_space=pltpu.VMEM),
            pl.BlockSpec(memory_space=pltpu.SMEM),
        ],
        out_specs=(pl.BlockSpec(memory_space=pl.ANY),) * 3,
        scratch_shapes=[
            pltpu.VMEM((wide, dims), series.dtype),
            pltpu.VMEM((LEAD + share, dims), series.dtype),
            pltpu.VMEM((LEAD + share, dims), series.dtype),
            pltpu.VMEM((block // LANE, LANE), jnp.float32),
            pltpu.VMEM((8 + LEAD + share, wide), jnp.float32),
            pltpu.VMEM((LEAD + share, wide), jnp.float32),
            pltpu.VMEM((8, wide), jnp.float32),
            pltpu.VMEM((share, LANE), jnp.float32),
            pltpu.VMEM((share, LANE), jnp.float32),
            pltpu.VMEM((share, block), jnp.float32),
            pltpu.VMEM((block, share), jnp.float32),
            pltpu.VMEM((share, block), jnp.float32),
            dma(3),
        ]
        + [dma(n) for n in early]
        + [
            pltpu.VMEM((2, 4, share // 2, quarter), series.dtype),
            pltpu.VMEM((2, share, share), jnp.float32),
            pltpu.VMEM((2, share, quarter), series.dtype),
            pltpu.VMEM((2, share // PARTS, block), jnp.float32),
        ]
        + [dma(n) for n in late],
        compiler_params=pltpu.CompilerParams(
            collective_id=0, has_side_effects=True, vmem_limit_bytes=48 * 1024 * 1024
        ),
    )(series, inv, width)


def solution(mesh):
    in_specs = (P("blk", "feat"), P("blk"), P())
    out_specs = (P(("blk", "feat"), None), P(("blk", "feat"), None), P(("blk", "feat"), None))
    return jax.shard_map(
        functools.partial(per_device, mesh.shape["blk"]),
        mesh=mesh,
        in_specs=in_specs,
        out_specs=out_specs,
        check_vma=False,
    )
```

```python
import functools

import jax
import jax.numpy as jnp
from jax import lax
from jax.experimental import pallas as pl
from jax.experimental.pallas import tpu as pltpu
from jax.sharding import PartitionSpec as P

LAGS = 24
LEAD = 32
LANE = 128
Z_SIZE = 16
CHUNKS = 8
PIECES = 8
MESH = pl.DeviceIdType.MESH
CONTRACT_LAST = (((1,), (1,)), ((), ()))


def multiple(value, of):
    return pl.multiple_of(value, of)


def tiles_kernel(
    blocks,
    series_ref,
    inv_ref,
    width_ref,
    same_ref,
    next_ref,
    prev_ref,
    whole,
    rows,
    nrows,
    mrows,
    ninv,
    minv,
    gram,
    mgram,
    same_gram,
    sums,
    norms,
    row_norms,
    row_factor,
    kept,
    mkept,
    turned,
    mturned,
    same_kept,
    hop,
    turn_hop,
    mturn_hop,
    k_relay,
    mk_relay,
    local_sem,
    tail_send,
    tail_recv,
    sib_send,
    sib_recv,
    hop_send,
    hop_recv,
    far_send,
    far_recv,
    pass_send,
    pass_recv,
    lead_send,
    lead_recv,
    inv_send,
    inv_recv,
    turn_send,
    turn_recv,
    turn_hop_send,
    turn_hop_recv,
    n_send,
    n_recv,
    m_send,
    m_recv,
    k_send,
    k_recv,
    mk_send,
    mk_recv,
    ride_send,
    relay_send,
    relay_recv,
):
    block, quarter = series_ref.shape
    dims = 4 * quarter
    share = block // 4
    part_rows = share // 2
    wide = block + LANE
    past = wide - LEAD

    b, f = lax.axis_index("blk"), lax.axis_index("feat")
    core, chip = lax.rem(f, 2), f // 2
    sib, far, cross = f + 1 - 2 * core, lax.rem(f + 2, 4), 3 - f
    after, before = lax.rem(b + 1, blocks), lax.rem(b + blocks - 1, blocks)
    half = blocks // 2
    pos, first = lax.rem(b, half), (b // half) * half
    over = lax.rem(b + half, blocks)
    others = (sib, far, cross)
    everyone = (f, sib, far, cross)
    near, end = first, first + half - 1
    side_pos = (Z_SIZE - 1, half - Z_SIZE, Z_SIZE, half - Z_SIZE - 1, 2 * Z_SIZE, 2 * Z_SIZE - 1)
    is_near, is_end = pos == 0, pos == half - 1
    is_sides = [pos == p for p in side_pos]
    any_of = lambda conditions: functools.reduce(jnp.logical_or, conditions)
    is_side = any_of(is_sides)
    is_seam = jnp.logical_or(is_near, is_end)
    ordinary = jnp.logical_not(is_seam)

    barrier = pltpu.get_barrier_semaphore()
    peers = [(b, j) for j in others] + [(after, f), (before, f)] + [(over, j) for j in (f, far, sib)]
    for peer in peers:
        pl.semaphore_signal(barrier, inc=1, device_id=peer, device_id_type=MESH)

    def greet(condition, corners):
        @pl.when(condition)
        def _():
            for corner in corners:
                pl.semaphore_signal(barrier, inc=1, device_id=corner, device_id_type=MESH)
            pl.semaphore_wait(barrier, len(peers) + len(corners))

    sides = [first + p for p in side_pos]
    greet(is_near, [(side, f) for side in sides] + [(end, f), (end, sib)])
    greet(is_end, [(side, f) for side in sides] + [(near, f), (near, sib)])
    greet(is_side, [(near, f), (end, f)])

    @pl.when(jnp.logical_not(jnp.logical_or(is_seam, is_side)))
    def _():
        pl.semaphore_wait(barrier, len(peers))

    sent = []

    def copy_of(src, dst, send_sem, recv_sem, to):
        return pltpu.make_async_remote_copy(
            src_ref=src, dst_ref=dst, send_sem=send_sem, recv_sem=recv_sem, device_id=to, device_id_type=MESH
        )

    def post(src, dst, send_sem, recv_sem, to):
        copy_of(src, dst, send_sem, recv_sem, to).start()

    def leaves(src, send_sem, recv_sem, condition=None):
        sent.append((condition, copy_of(src, src, send_sem, recv_sem, (b, sib))))

    def send(src, dst, send_sem, recv_sem, to):
        post(src, dst, send_sem, recv_sem, to)
        leaves(src, send_sem, recv_sem)

    def receive(dst, send_sem, recv_sem, sender):
        copy_of(dst, dst, send_sem, recv_sem, sender).wait_recv()

    def when(condition, act):
        @pl.when(condition)
        def _():
            act()

    def cols(q):
        return pl.ds(multiple(q * quarter, quarter), quarter)

    def group(g):
        return pl.ds(multiple(g * share, share), share)

    class Route:
        def __init__(self, back, spot, relay, i, send_sem, recv_sem):
            self.back, self.spot, self.relay, self.i = back, spot, relay, i
            self.send_sem, self.recv_sem = send_sem, recv_sem
            self.to, self.sender = (before, after) if back else (after, before)
            self.is_origin, self.origin, self.goal = (is_near, near, end) if back else (is_end, end, near)

        def slot(self, s):
            return self.relay.at[s], relay_send.at[2 * self.i + s], relay_recv.at[2 * self.i + s]

        def start(self, p, src):
            def direct():
                post(src, self.spot(p), self.send_sem.at[p], self.recv_sem.at[p], (self.to, f))

            def detour():
                if p < 6:
                    by, s = sides[p], 0
                elif p == 6:
                    by, s = (over, 1) if self.back else (near, 0)
                else:
                    by, s = (end, 0) if self.back else (over, 1)
                buffer, _, recv_sem = self.slot(s)
                post(src, buffer, self.send_sem.at[p], recv_sem, (by, f))

            when(self.is_origin, detour)
            when(jnp.logical_not(self.is_origin), direct)

        def register(self, p, src):
            leaves(src, self.send_sem.at[p], self.recv_sem.at[p])

        def go(self, p, src):
            self.start(p, src)
            self.register(p, src)

        def await_piece(self, p):
            receive(self.spot(p), self.send_sem.at[p], self.recv_sem.at[p], (self.sender, f))

        def forward(self, condition, s, sender, dst, dst_sem, to):
            def act():
                buffer, send_sem, recv_sem = self.slot(s)
                receive(buffer, send_sem, recv_sem, (sender, f))
                post(buffer, dst, send_sem, dst_sem, (to, f))

            when(condition, act)

        def outward(self, condition):
            buffer, _, recv_sem = self.slot(1)
            self.forward(condition, 0, self.origin, buffer, recv_sem, over)

        def inward(self, condition):
            for p in range(6):
                self.forward(
                    jnp.logical_and(condition, is_sides[p]), 1, over, self.spot(p), self.recv_sem.at[p], self.goal
                )

        def at_seam(self):
            p, q = (7, 6) if self.back else (6, 7)
            at_p, at_q = (is_end, is_near) if self.back else (is_near, is_end)
            self.forward(at_p, 0, self.origin, self.spot(p), self.recv_sem.at[p], over)
            self.forward(at_q, 1, over, self.spot(q), self.recv_sem.at[q], self.goal)

        def drain(self):
            at_p, at_q = (is_end, is_near) if self.back else (is_near, is_end)
            for s, condition in ((0, at_p), (1, at_q)):
                buffer, send_sem, recv_sem = self.slot(s)
                copy = copy_of(buffer, buffer, send_sem, recv_sem, (over, f))
                when(jnp.logical_or(is_side, condition), copy.wait_send)

    def n_spot(p):
        return nrows.at[pl.ds(LEAD + (p % 2) * part_rows, part_rows), cols(everyone[p // 2])]

    def m_spot(p):
        size = part_rows // 2
        return mrows.at[pl.ds(LEAD + (p % 2) * size, size), cols(everyone[p // 2])]

    def k_spot(p):
        g, h = p % 4, p // 4
        return prev_ref.at[pl.ds(h * part_rows, part_rows), pl.ds(g * share + part_rows, part_rows)]

    def mk_spot(p):
        size = part_rows // PIECES
        return next_ref.at[pl.ds(p * size, size), :]

    k_route = Route(False, k_spot, k_relay, 0, k_send, k_recv)
    mk_route = Route(True, mk_spot, mk_relay, 1, mk_send, mk_recv)

    quarter_rows = share // 4

    def own_rows(ref, start, size, columns):
        return ref.at[pl.ds(multiple(f * share + start, size), size), columns]

    def send_n(ref, qi, columns, condition):
        for p in (2 * qi, 2 * qi + 1):
            piece = own_rows(ref, (p % 2) * part_rows, part_rows, columns)
            when(condition, functools.partial(post, piece, n_spot(p), n_send.at[p], n_recv.at[p], (before, f)))

    def send_n_quarter(qi, i, condition):
        p, columns = 2 * qi + i // 2, cols(everyone[qi])
        piece = own_rows(whole, i * quarter_rows, quarter_rows, columns)
        spot = nrows.at[pl.ds(LEAD + i * quarter_rows, quarter_rows), columns]
        when(condition, functools.partial(post, piece, spot, n_send.at[p], n_recv.at[p], (before, f)))

    def send_m(ref, qi, columns, condition, pieces=(0, 1)):
        for i in pieces:
            p = 2 * qi + i
            piece = own_rows(ref, i * quarter_rows, quarter_rows, columns)
            when(condition, functools.partial(post, piece, m_spot(p), m_send.at[p], m_recv.at[p], (after, f)))

    def await_n(p):
        receive(n_spot(p), n_send.at[p], n_recv.at[p], (after, f))

    def await_m(p):
        receive(m_spot(p), m_send.at[p], m_recv.at[p], (before, f))

    has_n, has_m = jnp.logical_not(is_near), jnp.logical_not(is_end)

    def order(c, j):
        return j + c * (2, 2, -1, -3)[j]

    def halved(sender, k, s):
        c = sender if s == 0 else 1 - sender
        usual = order(1 - sender, k // 2) * share + (k % 2) * 2 * quarter_rows + s * quarter_rows
        at_seam = (2 * c + k % 2) * share + (k // 2) * quarter_rows
        return pl.ds(multiple(jnp.where(is_seam, at_seam, usual), quarter_rows), quarter_rows)

    here = pltpu.make_async_copy(series_ref, whole.at[pl.ds(0, block), cols(f)], local_sem.at[0])
    here.start()
    send(
        series_ref.at[pl.ds(block - LEAD, LEAD), :],
        whole.at[pl.ds(past, LEAD), cols(f)],
        tail_send.at[0],
        tail_recv.at[0],
        (after, f),
    )

    def set_out(k):
        for s, j in enumerate((f, far)):
            i = CHUNKS * s + k
            send(series_ref.at[halved(chip, k, s), :], hop.at[s, k], hop_send.at[i], hop_recv.at[i], (over, j))

    def hand_over(k):
        for s, j in enumerate((f, far)):
            i = CHUNKS * s + k
            receive(hop.at[s, k], hop_send.at[i], hop_recv.at[i], (over, j))
            c, to = (chip, far) if s == 0 else (1 - chip, f)
            send(hop.at[s, k], whole.at[halved(c, k, s), cols(j)], far_send.at[i], far_recv.at[i], (over, to))

            to, place = 2 * chip + k % 2, k // 2
            qi = lax.rem(core + k % 2, 2) + 2 * s
            spot = pl.ds(LEAD + place * quarter_rows, quarter_rows)

            def ride_back():
                post(
                    hop.at[s, k], nrows.at[spot, cols(j)], ride_send.at[i], n_recv.at[2 * qi + place // 2], (end, to)
                )

            def ride_on():
                post(hop.at[s, k], mrows.at[spot, cols(j)], ride_send.at[i], m_recv.at[2 * qi + place], (near, to))

            when(is_near, ride_back)
            leaves(hop.at[s, k], ride_send.at[i], n_recv.at[0], is_near)
            if place < 2:
                when(is_end, ride_on)
                leaves(hop.at[s, k], ride_send.at[i], n_recv.at[0], is_end)

    set_out(0)
    set_out(1)
    send(series_ref, whole.at[pl.ds(0, block), cols(f)], sib_send.at[0], sib_recv.at[0], (b, sib))
    send_n(series_ref, 0, slice(None), has_n)
    send_m(series_ref, 0, slice(None), has_m)
    send(inv_ref, ninv, inv_send.at[0], inv_recv.at[0], (before, f))
    send(inv_ref, minv, inv_send.at[1], inv_recv.at[1], (after, f))

    whole[pl.ds(block, LANE - LEAD), :] = jnp.zeros((LANE - LEAD, dims), whole.dtype)
    for buffer in (gram, mgram, same_gram):
        buffer[pl.ds(0, 8), :] = jnp.zeros((8, wide), jnp.float32)

    def pass_on(k):
        for s in range(2):
            i = CHUNKS * s + k
            piece = whole.at[halved(1 - chip, k, s), cols(far)]
            receive(piece, far_send.at[i], far_recv.at[i], (over, far if s == 0 else f))
            send(piece, piece, pass_send.at[i], pass_recv.at[i], (b, sib))

    def passed(k):
        for s in range(2):
            i = CHUNKS * s + k
            piece = whole.at[halved(1 - chip, k, s), cols(cross)]
            receive(piece, pass_send.at[i], pass_recv.at[i], (b, sib))

    lead = multiple(lax.rem(f * share + wide - LEAD, wide), LEAD)
    near_half = pl.ds(multiple(chip * 2 * quarter, quarter), 2 * quarter)
    far_half = pl.ds(multiple((1 - chip) * 2 * quarter, quarter), 2 * quarter)
    leads = (near_half, far_half)
    lead_ways = ((nrows, before, after), (mrows, after, before))

    def post_lead(i):
        for w, (dst, to, _) in enumerate(lead_ways):
            s = 2 * w + i
            post(
                whole.at[pl.ds(lead, LEAD), leads[i]],
                dst.at[pl.ds(0, LEAD), leads[i]],
                lead_send.at[s],
                lead_recv.at[s],
                (to, f),
            )

    def receive_lead(w, i):
        dst, _, sender = lead_ways[w]
        receive(dst.at[pl.ds(0, LEAD), leads[i]], lead_send.at[2 * w + i], lead_recv.at[2 * w + i], (sender, f))

    def squares(x):
        total = jnp.zeros((x.shape[0], LANE), jnp.float32)
        for g in range(x.shape[1] // LANE):
            piece = x[:, g * LANE : (g + 1) * LANE].astype(jnp.float32)
            total = total + piece * piece
        return total

    def norm_of(start):
        part = pl.ds(multiple(start, LANE), LANE)
        norms[:, part] = jnp.broadcast_to(jnp.sum(squares(whole[part, :]).T, axis=0, keepdims=True), (8, LANE))

    def norm_of_group(j):
        for i in range(share // LANE):
            norm_of(order(chip, j) * share + i * LANE)

    def lag_sum(x, axis):
        for step in (1, 2, 4):
            x = x + pltpu.roll(x, step, axis)
        return x + pltpu.roll(x, 8, axis) + pltpu.roll(x, 16, axis)

    def products(left, right):
        return lax.dot_general(left, right, CONTRACT_LAST, preferred_element_type=jnp.float32)

    def same_products(start, size):
        part = pl.ds(multiple(start, LANE), size)
        same_gram[pl.ds(8, LEAD + share), part] = products(rows[...], whole[part, :])

    def add_products(target, source, which, fresh):
        size, height = 256, source.shape[0]
        for start in range(0, wide, size):
            part = pl.ds(start, min(size, wide - start))
            found = products(source[:, which], whole[part, which])
            if fresh:
                target[pl.ds(8, height), part] = found
            else:
                target[pl.ds(8, height), part] += found

    def near_products():
        for p in range(4):
            await_n(p)
        receive_lead(0, 0)
        add_products(gram, nrows, near_half, True)

    both = jnp.logical_and
    first_core, second_core = both(ordinary, core == 0), both(ordinary, core == 1)
    for k in range(CHUNKS):
        hand_over(k)
        if k + 2 < CHUNKS:
            set_out(k + 2)
        if k == 0:
            receive(whole.at[pl.ds(0, block), cols(sib)], sib_send.at[0], sib_recv.at[0], (b, sib))
            send_n(whole, 1, cols(sib), has_n)
            send_m(whole, 1, cols(sib), has_m)
            tail = whole.at[pl.ds(past, LEAD), cols(f)]
            receive(tail, tail_send.at[0], tail_recv.at[0], (before, f))
            for i, j in enumerate(others):
                send(tail, tail, tail_send.at[1 + i], tail_recv.at[1 + i], (b, j))
        else:
            pass_on(k - 1)
        if k == 2:
            here.wait()
            for i, j in enumerate(others):
                receive(whole.at[pl.ds(past, LEAD), cols(j)], tail_send.at[1 + i], tail_recv.at[1 + i], (b, j))
            post_lead(0)
            send_n(whole, 2, cols(far), first_core)
            send_m(whole, 2, cols(far), first_core)
            send_n_quarter(2, 0, is_end)
            send_m(whole, 2, cols(far), is_near, (0,))
        if k == 3:
            send_m(whole, 2, cols(far), second_core)
            passed(0)
            passed(1)
            send_n(whole, 3, cols(cross), first_core)
            send_m(whole, 3, cols(cross), first_core)
            send_n_quarter(3, 0, is_end)
            send_m(whole, 3, cols(cross), is_near, (0,))
            when(ordinary, lambda: norm_of_group(0))
            norm_of(block)
        if k == 4:
            send_n(whole, 2, cols(far), second_core)
            passed(2)
            send_m(whole, 3, cols(cross), second_core)
            send_n_quarter(2, 1, is_end)
            send_m(whole, 2, cols(far), is_near, (1,))
        if k == 5:
            passed(3)
            send_n(whole, 3, cols(cross), second_core)
            send_n_quarter(3, 1, is_end)
            send_m(whole, 3, cols(cross), is_near, (1,))
            when(ordinary, lambda: norm_of_group(1))
        if k == 6:
            send_n_quarter(2, 2, is_end)
            for p in range(4):
                await_m(p)
            receive_lead(1, 0)
            add_products(mgram, mrows, near_half, True)
        if k == 7:
            passed(4)
            passed(5)
            send_n_quarter(3, 2, is_end)
            when(ordinary, lambda: post_lead(1))
            when(ordinary, lambda: norm_of_group(2))
            when(jnp.logical_not(is_end), near_products)
    pass_on(7)
    send_n_quarter(2, 3, is_end)
    passed(6)
    passed(7)
    send_n_quarter(3, 3, is_end)
    when(is_seam, lambda: post_lead(1))
    for i in range(2):
        for w in range(2):
            leaves(whole.at[pl.ds(lead, LEAD), leads[i]], lead_send.at[2 * w + i], lead_recv.at[2 * w + i])
    for p in range(8):
        leaves(n_spot(p), n_send.at[p], n_recv.at[p], has_n)
        leaves(m_spot(p), m_send.at[p], m_recv.at[p], has_m)
    when(ordinary, lambda: norm_of_group(3))

    def all_norms():
        def step(j, carry):
            norm_of(j * LANE)
            return carry

        lax.fori_loop(0, block // LANE, step, 0)

    when(is_seam, all_norms)
    when(is_end, near_products)
    norms[...] = lag_sum(norms[...], 1)

    inv_row = jnp.concatenate([inv_ref[j : j + 1, :] for j in range(block // LANE)], axis=1)
    width_row = jnp.full((1, LANE), width_ref[0], jnp.float32) * (LAGS * dims)

    def factors(ref, count):
        for j in range(count // LANE):
            line = ref[pl.ds(f * (share // LANE) + j, 1), :] / width_row
            row_factor[pl.ds(j * LANE, LANE), :] = jnp.broadcast_to(-line, (LANE, LANE)).T

    def group_norms(near_squares, source):
        height = source.shape[0]
        lagged = jnp.sum(near_squares + squares(source[:, far_half]), axis=1, keepdims=True)
        row_norms[pl.ds(0, height - LEAD), :] = lag_sum(jnp.broadcast_to(lagged, (height, LANE)), 0)[LEAD:, :]

    def all_columns(x):
        return x[:, :block]

    def second_halves(x):
        return jnp.concatenate([x[:, g * share + part_rows : (g + 1) * share] for g in range(4)], axis=1)

    def tile(products_of, target, pick, parts, ready):
        per = target.shape[0] // 32 // parts
        for h in range(parts):
            for t in range(h * per + 1 if h else 0, (h + 1) * per + 1):
                x = products_of[pl.ds(t * 32, 40), :]
                for step in (1, 2, 4):
                    x = x + pltpu.roll(pltpu.roll(x, step, 0), step, 1)
                sums[pl.ds(t * 32, 32), :] = x[8:, :]
            for t in range(h * per, (h + 1) * per):
                x = sums[pl.ds(t * 32 + 32, 32), :]
                x = x + pltpu.roll(sums[pl.ds(t * 32 + 24, 32), :], 8, 1)
                x = x + pltpu.roll(sums[pl.ds(t * 32 + 16, 32), :], 16, 1)
                part = pl.ds(t * 32, 32)
                spread = row_norms[part, :][:, :1] + pick(norms[pl.ds(0, 1), :]) - 2.0 * pick(x)
                target[part, :] = jnp.exp(spread * (row_factor[part, :][:, :1] * pick(inv_row)))
            ready(h)

    receive(minv, inv_send.at[1], inv_recv.at[1], (before, f))
    receive(ninv, inv_send.at[0], inv_recv.at[0], (after, f))
    factors(minv, part_rows)
    m_squares = squares(mrows[:, near_half])
    for p in range(4, 8):
        await_m(p)
    receive_lead(1, 1)
    add_products(mgram, mrows, far_half, False)
    group_norms(m_squares, mrows)

    def send_mk(h):
        for p in range(h * PIECES // 2, (h + 1) * PIECES // 2):
            mk_route.go(p, mkept.at[pl.ds(p * (part_rows // PIECES), part_rows // PIECES), :])

    tile(mgram, mkept, all_columns, 2, send_mk)

    my_columns = pl.ds(multiple(f * share, share), share)
    my_first = pl.ds(multiple(f * share, part_rows), part_rows)
    lower = pl.ds(part_rows, part_rows)
    hops = ((0, far, f), (1, cross, far))

    def turn_m(j):
        for i in range(share // LANE):
            part = pl.ds(multiple(j * share + i * LANE, LANE), LANE)
            mturned[part, :] = mkept[:, part].T

    for s, j, by in hops:
        turn_m(j)
        send(mturned.at[group(j), :], mturn_hop.at[s], turn_hop_send.at[2 + s], turn_hop_recv.at[2 + s], (over, by))
    turn_m(sib)
    send(mturned.at[group(sib), :], prev_ref.at[:, my_first], turn_send.at[5], turn_recv.at[5], (b, sib))
    turn_m(f)
    own_mturned = pltpu.make_async_copy(mturned.at[group(f), :], prev_ref.at[:, my_first], local_sem.at[3])
    own_mturned.start()

    factors(ninv, share)
    n_squares = squares(nrows[:, near_half])
    for p in range(4, 8):
        await_n(p)
    receive_lead(0, 1)
    add_products(gram, nrows, far_half, False)
    group_norms(n_squares, nrows)

    def send_k(h):
        for g in range(4):
            k_route.go(4 * h + g, kept.at[pl.ds(h * part_rows, part_rows), pl.ds(g * part_rows, part_rows)])

    tile(gram, kept, second_halves, 2, send_k)

    def seconds(j):
        return pl.ds(multiple(j * part_rows, part_rows), part_rows)

    def turn(j):
        turned[seconds(j), :] = kept[:, seconds(j)].T

    for s, j, by in hops:
        turn(j)
        send(turned.at[seconds(j), :], turn_hop.at[s], turn_hop_send.at[s], turn_hop_recv.at[s], (over, by))
    turn(sib)
    send(turned.at[seconds(sib), :], next_ref.at[lower, my_columns], turn_send.at[2], turn_recv.at[2], (b, sib))
    turn(f)
    own_turned = pltpu.make_async_copy(turned.at[seconds(f), :], next_ref.at[lower, my_columns], local_sem.at[1])
    own_turned.start()

    def firsts_of(j):
        return pl.ds(multiple(j * share, part_rows), part_rows)

    for s, j, to in ((0, f, far), (1, far, sib)):
        receive(mturn_hop.at[s], turn_hop_send.at[2 + s], turn_hop_recv.at[2 + s], (over, j))
        send(mturn_hop.at[s], prev_ref.at[:, firsts_of(j)], turn_send.at[3 + s], turn_recv.at[3 + s], (over, to))

    rows[pl.ds(0, LEAD), :] = whole[pl.ds(lead, LEAD), :]
    rows[pl.ds(LEAD, share), :] = whole[group(f), :]
    for j in range(4):
        same_products(order(chip, j) * share, share)
    same_products(block, LANE)
    factors(inv_ref, share)
    for j in range(share // LANE):
        line = norms[pl.ds(0, 1), pl.ds(multiple(f * share + j * LANE, LANE), LANE)]
        row_norms[pl.ds(j * LANE, LANE), :] = jnp.broadcast_to(line, (LANE, LANE)).T

    def between(h):
        if h == 0:
            for s, j, to in ((0, f, far), (1, far, sib)):
                receive(turn_hop.at[s], turn_hop_send.at[s], turn_hop_recv.at[s], (over, j))
                send(turn_hop.at[s], next_ref.at[lower, group(j)], turn_send.at[s], turn_recv.at[s], (over, to))
            mk_route.outward(is_side)

    tile(same_gram, same_kept, all_columns, 2, between)
    own_same = pltpu.make_async_copy(same_kept, same_ref, local_sem.at[2])
    own_same.start()

    k_route.outward(is_side)
    mk_route.inward(is_side)
    mk_route.at_seam()
    k_route.inward(is_side)
    k_route.at_seam()

    for p in range(PIECES):
        mk_route.await_piece(p)
        k_route.await_piece(p)
    for i, j in enumerate((far, cross, sib)):
        receive(next_ref.at[lower, group(j)], turn_send.at[i], turn_recv.at[i], (b, j))
        receive(prev_ref.at[:, firsts_of(j)], turn_send.at[3 + i], turn_recv.at[3 + i], (b, j))
    own_turned.wait()
    own_mturned.wait()
    own_same.wait()
    for condition, copy in sent:
        if condition is None:
            copy.wait_send()
        else:
            when(condition, copy.wait_send)
    for route in (k_route, mk_route):
        route.drain()


def per_device(blocks, series, scales, width):
    block, quarter = series.shape
    dims, share, wide = 4 * quarter, block // 4, block + LANE
    part_rows = share // 2
    inv = (1.0 / scales.astype(jnp.float32)).reshape(block // LANE, LANE)
    out = jax.ShapeDtypeStruct((share, block), jnp.float32)
    raw = lambda *shape: pltpu.VMEM(shape, series.dtype)
    wider = lambda *shape: pltpu.VMEM(shape, jnp.float32)
    hops = 2 * CHUNKS
    pairs = (4, 1, hops, hops, hops, 4, 2, 6, 4, PIECES, PIECES, PIECES, PIECES)
    counts = [n for n in pairs for _ in range(2)] + [hops, 4, 4]
    return pl.pallas_call(
        functools.partial(tiles_kernel, blocks),
        out_shape=(out, out, out),
        in_specs=[
            pl.BlockSpec(memory_space=pl.ANY),
            pl.BlockSpec(memory_space=pltpu.VMEM),
            pl.BlockSpec(memory_space=pltpu.SMEM),
        ],
        out_specs=(pl.BlockSpec(memory_space=pl.ANY),) * 3,
        scratch_shapes=[
            raw(wide, dims),
            raw(LEAD + share, dims),
            raw(LEAD + share, dims),
            raw(LEAD + part_rows, dims),
            wider(block // LANE, LANE),
            wider(block // LANE, LANE),
            wider(8 + LEAD + share, wide),
            wider(8 + LEAD + part_rows, wide),
            wider(8 + LEAD + share, wide),
            wider(LEAD + share, wide),
            wider(8, wide),
            wider(share, LANE),
            wider(share, LANE),
            wider(share, block // 2),
            wider(part_rows, block),
            wider(block // 2, share),
            wider(block, part_rows),
            wider(share, block),
            raw(2, CHUNKS, 2 * share // CHUNKS, quarter),
            wider(2, part_rows, share),
            wider(2, share, part_rows),
            wider(2, part_rows, part_rows),
            wider(2, part_rows // PIECES, block),
            pltpu.SemaphoreType.DMA((4,)),
        ]
        + [pltpu.SemaphoreType.DMA((n,)) for n in counts],
        compiler_params=pltpu.CompilerParams(
            collective_id=0, has_side_effects=True, vmem_limit_bytes=48 * 1024 * 1024
        ),
    )(series, inv, width)


def solution(mesh):
    in_specs = (P("blk", "feat"), P("blk"), P())
    out_specs = (P(("blk", "feat"), None), P(("blk", "feat"), None), P(("blk", "feat"), None))
    return jax.shard_map(
        functools.partial(per_device, mesh.shape["blk"]),
        mesh=mesh,
        in_specs=in_specs,
        out_specs=out_specs,
        check_vma=False,
    )
```

```python
import functools

import jax
import jax.numpy as jnp
from jax import lax
from jax.experimental import pallas as pl
from jax.experimental.pallas import tpu as pltpu
from jax.sharding import PartitionSpec as P

LAGS = 24
LEAD = 32
LANE = 128
CHUNKS = 8
PIECES = 8
PARTS = 2
MESH = pl.DeviceIdType.MESH
CONTRACT_LAST = (((1,), (1,)), ((), ()))


def multiple(value, of):
    return pl.multiple_of(value, of)


def tiles_kernel(
    blocks,
    series_ref,
    inv_ref,
    width_ref,
    same_ref,
    next_ref,
    prev_ref,
    whole,
    rows,
    nrows,
    mrows,
    mrows_rest,
    ninv,
    minv,
    gram,
    mgram,
    same_gram,
    sums,
    partial,
    squared,
    past_squared,
    lagged,
    nlagged,
    mlagged,
    norms,
    row_norms,
    row_factor,
    kept,
    mkept,
    turned,
    mturned,
    kept_rest,
    mkept_rest,
    turned_rest,
    mturned_rest,
    hop,
    turn_hop,
    mturn_hop,
    rest_hop,
    mrest_hop,
    tail_send,
    tail_recv,
    sib_send,
    sib_recv,
    hop_send,
    hop_recv,
    far_send,
    far_recv,
    pass_send,
    pass_recv,
    lead_send,
    lead_recv,
    inv_send,
    inv_recv,
    square_send,
    square_recv,
    turn_send,
    turn_recv,
    turn_hop_send,
    turn_hop_recv,
    rest_send,
    rest_recv,
    rest_hop_send,
    rest_hop_recv,
    n_send,
    n_recv,
    m_send,
    m_recv,
    k_send,
    k_recv,
    mk_send,
    mk_recv,
    ride_send,
):
    block, quarter = series_ref.shape
    dims = 4 * quarter
    share = block // 4
    part_rows = share // 2
    wide = block + LANE
    past = wide - LEAD

    b, f = lax.axis_index("blk"), lax.axis_index("feat")
    core, chip = lax.rem(f, 2), f // 2
    sib, far, cross = f + 1 - 2 * core, lax.rem(f + 2, 4), 3 - f
    after, before = lax.rem(b + 1, blocks), lax.rem(b + blocks - 1, blocks)
    half = blocks // 2
    pos, first = lax.rem(b, half), (b // half) * half
    over = lax.rem(b + half, blocks)
    others = (sib, far, cross)
    everyone = (f, sib, far, cross)
    near, end = first, first + half - 1
    is_near, is_end = pos == 0, pos == half - 1
    is_seam = jnp.logical_or(is_near, is_end)
    ordinary = jnp.logical_not(is_seam)

    barrier = pltpu.get_barrier_semaphore()
    peers = [(b, j) for j in others] + [(after, f), (before, f)] + [(over, j) for j in (f, far, sib)]
    for peer in peers:
        pl.semaphore_signal(barrier, inc=1, device_id=peer, device_id_type=MESH)

    def greet(condition, corners):
        @pl.when(condition)
        def _():
            for corner in corners:
                pl.semaphore_signal(barrier, inc=1, device_id=corner, device_id_type=MESH)
            pl.semaphore_wait(barrier, len(peers) + len(corners))

    greet(is_near, [(end, f), (end, sib)])
    greet(is_end, [(near, f), (near, sib)])

    @pl.when(ordinary)
    def _():
        pl.semaphore_wait(barrier, len(peers))

    sent = []

    def copy_of(src, dst, send_sem, recv_sem, to):
        return pltpu.make_async_remote_copy(
            src_ref=src, dst_ref=dst, send_sem=send_sem, recv_sem=recv_sem, device_id=to, device_id_type=MESH
        )

    def post(src, dst, send_sem, recv_sem, to):
        copy_of(src, dst, send_sem, recv_sem, to).start()

    def leaves(src, send_sem, recv_sem, condition=None):
        sent.append((condition, copy_of(src, src, send_sem, recv_sem, (b, sib))))

    def send(src, dst, send_sem, recv_sem, to):
        post(src, dst, send_sem, recv_sem, to)
        leaves(src, send_sem, recv_sem)

    def receive(dst, send_sem, recv_sem, sender):
        copy_of(dst, dst, send_sem, recv_sem, sender).wait_recv()

    def when(condition, act):
        @pl.when(condition)
        def _():
            act()

    def cols(q):
        return pl.ds(multiple(q * quarter, quarter), quarter)

    def group(g):
        return pl.ds(multiple(g * share, share), share)

    def n_spot(p):
        return nrows.at[pl.ds(LEAD + (p % 2) * part_rows, part_rows), cols(everyone[p // 2])]

    def m_spot(p):
        size = part_rows // 2
        return mrows.at[pl.ds(LEAD + (p % 2) * size, size), cols(everyone[p // 2])]

    def k_spot(p):
        g, h = p % 4, p // 4
        return prev_ref.at[pl.ds(h * part_rows, part_rows), pl.ds(g * share + part_rows, part_rows)]

    def mk_spot(p):
        size = part_rows // PARTS
        return next_ref.at[pl.ds(p * size, size), :]

    quarter_rows = share // 4

    def own_rows(ref, start, size, columns):
        return ref.at[pl.ds(multiple(f * share + start, size), size), columns]

    def send_n(ref, qi, columns, condition):
        for p in (2 * qi, 2 * qi + 1):
            piece = own_rows(ref, (p % 2) * part_rows, part_rows, columns)
            when(condition, functools.partial(post, piece, n_spot(p), n_send.at[p], n_recv.at[p], (before, f)))

    def send_n_quarter(qi, i, condition):
        p, columns = 2 * qi + i // 2, cols(everyone[qi])
        piece = own_rows(whole, i * quarter_rows, quarter_rows, columns)
        spot = nrows.at[pl.ds(LEAD + i * quarter_rows, quarter_rows), columns]
        when(condition, functools.partial(post, piece, spot, n_send.at[p], n_recv.at[p], (before, f)))

    def send_m(ref, qi, columns, condition, pieces=(0, 1)):
        for i in pieces:
            p = 2 * qi + i
            piece = own_rows(ref, i * quarter_rows, quarter_rows, columns)
            when(condition, functools.partial(post, piece, m_spot(p), m_send.at[p], m_recv.at[p], (after, f)))

    def await_n(p):
        receive(n_spot(p), n_send.at[p], n_recv.at[p], (after, f))

    def await_m(p):
        receive(m_spot(p), m_send.at[p], m_recv.at[p], (before, f))

    has_n, has_m = jnp.logical_not(is_near), jnp.logical_not(is_end)

    def order(c, j):
        return j + c * (2, 2, -1, -3)[j]

    def place_of(k):
        return (k // 2 + 3) % 4

    def halved(sender, k, s):
        c = sender if s == 0 else 1 - sender
        usual = order(1 - sender, k // 2) * share + (k % 2) * 2 * quarter_rows + s * quarter_rows
        at_seam = (2 * c + k % 2) * share + place_of(k) * quarter_rows
        return pl.ds(multiple(jnp.where(is_seam, at_seam, usual), quarter_rows), quarter_rows)

    send(
        series_ref.at[pl.ds(block - LEAD, LEAD), :],
        whole.at[pl.ds(past, LEAD), cols(f)],
        tail_send.at[0],
        tail_recv.at[0],
        (after, f),
    )

    def set_out(k):
        for s, j in enumerate((f, far)):
            i = CHUNKS * s + k
            send(series_ref.at[halved(chip, k, s), :], hop.at[s, k], hop_send.at[i], hop_recv.at[i], (over, j))

    def hand_over(k):
        for s, j in enumerate((f, far)):
            i = CHUNKS * s + k
            receive(hop.at[s, k], hop_send.at[i], hop_recv.at[i], (over, j))
            c, to = (chip, far) if s == 0 else (1 - chip, f)
            send(hop.at[s, k], whole.at[halved(c, k, s), cols(j)], far_send.at[i], far_recv.at[i], (over, to))

            to, place = 2 * chip + k % 2, place_of(k)
            qi = lax.rem(core + k % 2, 2) + 2 * s
            spot = pl.ds(LEAD + place * quarter_rows, quarter_rows)

            def ride_back():
                post(
                    hop.at[s, k], nrows.at[spot, cols(j)], ride_send.at[i], n_recv.at[2 * qi + place // 2], (end, to)
                )

            def ride_on():
                at = pl.ds(LEAD + (place % 2) * quarter_rows, quarter_rows)
                rows_there = mrows if place < 2 else mrows_rest
                sem = m_recv.at[2 * qi + place] if place < 2 else rest_recv.at[6 + 2 * qi + place - 2]
                post(hop.at[s, k], rows_there.at[at, cols(j)], ride_send.at[i], sem, (near, to))

            when(is_near, ride_back)
            leaves(hop.at[s, k], ride_send.at[i], n_recv.at[0], is_near)
            when(is_end, ride_on)
            leaves(hop.at[s, k], ride_send.at[i], n_recv.at[0], is_end)

    set_out(0)
    set_out(1)
    send(series_ref, whole.at[pl.ds(0, block), cols(f)], sib_send.at[0], sib_recv.at[0], (b, sib))
    send_n(series_ref, 0, slice(None), has_n)
    send_m(series_ref, 0, slice(None), has_m)
    send(inv_ref, ninv, inv_send.at[0], inv_recv.at[0], (before, f))
    send(inv_ref, minv, inv_send.at[1], inv_recv.at[1], (after, f))

    whole[pl.ds(0, block), cols(f)] = series_ref[...]
    whole[pl.ds(block, LANE - LEAD), :] = jnp.zeros((LANE - LEAD, dims), whole.dtype)
    for buffer in (gram, mgram, same_gram):
        buffer[pl.ds(0, 8), :] = jnp.zeros((8, wide), jnp.float32)

    def pass_on(k):
        for s in range(2):
            i = CHUNKS * s + k
            piece = whole.at[halved(1 - chip, k, s), cols(far)]
            receive(piece, far_send.at[i], far_recv.at[i], (over, far if s == 0 else f))
            send(piece, piece, pass_send.at[i], pass_recv.at[i], (b, sib))

    def passed(k):
        for s in range(2):
            i = CHUNKS * s + k
            piece = whole.at[halved(1 - chip, k, s), cols(cross)]
            receive(piece, pass_send.at[i], pass_recv.at[i], (b, sib))

    lead = multiple(lax.rem(f * share + wide - LEAD, wide), LEAD)
    near_half = pl.ds(multiple(chip * 2 * quarter, quarter), 2 * quarter)
    far_half = pl.ds(multiple((1 - chip) * 2 * quarter, quarter), 2 * quarter)
    leads = (near_half, far_half)
    lead_ways = ((nrows, before, after), (mrows, after, before))

    def post_lead(i):
        for w, (dst, to, _) in enumerate(lead_ways):
            s = 2 * w + i
            post(
                whole.at[pl.ds(lead, LEAD), leads[i]],
                dst.at[pl.ds(0, LEAD), leads[i]],
                lead_send.at[s],
                lead_recv.at[s],
                (to, f),
            )

    def receive_lead(w, i):
        dst, _, sender = lead_ways[w]
        receive(dst.at[pl.ds(0, LEAD), leads[i]], lead_send.at[2 * w + i], lead_recv.at[2 * w + i], (sender, f))

    lines = block // LANE

    def square_lines(lines_now):
        for j in lines_now:
            x = whole[pl.ds(j * LANE, LANE), cols(f)]
            total = jnp.zeros((LANE, LANE), jnp.float32)
            for g in range(quarter // LANE):
                piece = x[:, g * LANE : (g + 1) * LANE].astype(jnp.float32)
                total = total + piece * piece
            partial[pl.ds(f, 1), pl.ds(j, 1), :] = jnp.sum(total.T, axis=0, keepdims=True)[None]

    def share_squares():
        for i, j in enumerate(others):
            send(partial.at[f], partial.at[f], square_send.at[i], square_recv.at[i], (b, j))

    def sum_squares():
        for i, j in enumerate(others):
            receive(partial.at[j], square_send.at[i], square_recv.at[i], (b, j))
        squared[...] = partial[0] + partial[1] + partial[2] + partial[3]
        send(squared, past_squared, square_send.at[3], square_recv.at[3], (after, f))

    def lag_squares():
        receive(past_squared, square_send.at[3], square_recv.at[3], (before, f))
        line = [squared[j : j + 1, :] for j in range(lines)] + [past_squared[lines - 1 : lines, :]]
        norms[...] = lag_sum(jnp.broadcast_to(jnp.concatenate(line, axis=1), (8, wide)), 1)
        for j in range(lines):
            lagged[j : j + 1, :] = norms[0:1, j * LANE : (j + 1) * LANE]
        send(lagged, nlagged, square_send.at[4], square_recv.at[4], (before, f))
        send(lagged, mlagged, square_send.at[5], square_recv.at[5], (after, f))

    def lag_sum(x, axis):
        for step in (1, 2, 4):
            x = x + pltpu.roll(x, step, axis)
        return x + pltpu.roll(x, 8, axis) + pltpu.roll(x, 16, axis)

    def products(left, right):
        return lax.dot_general(left, right, CONTRACT_LAST, preferred_element_type=jnp.float32)

    def same_products(start, size):
        part = pl.ds(multiple(start, LANE), size)
        same_gram[pl.ds(8, LEAD + share), part] = products(rows[...], whole[part, :])

    def add_products(target, source, which, fresh):
        size, height = 256, source.shape[0]
        for start in range(0, wide, size):
            part = pl.ds(start, min(size, wide - start))
            found = products(source[:, which], whole[part, which])
            if fresh:
                target[pl.ds(8, height), part] = found
            else:
                target[pl.ds(8, height), part] += found

    def near_products():
        for p in range(4):
            await_n(p)
        receive_lead(0, 0)
        add_products(gram, nrows, near_half, True)

    both = jnp.logical_and
    first_core, second_core = both(ordinary, core == 0), both(ordinary, core == 1)
    for k in range(CHUNKS):
        hand_over(k)
        if k + 2 < CHUNKS:
            set_out(k + 2)
        if k == 0:
            receive(whole.at[pl.ds(0, block), cols(sib)], sib_send.at[0], sib_recv.at[0], (b, sib))
            send_n(whole, 1, cols(sib), has_n)
            send_m(whole, 1, cols(sib), has_m)
            tail = whole.at[pl.ds(past, LEAD), cols(f)]
            receive(tail, tail_send.at[0], tail_recv.at[0], (before, f))
            for i, j in enumerate(others):
                send(tail, tail, tail_send.at[1 + i], tail_recv.at[1 + i], (b, j))
            square_lines(range(lines // 2))
        else:
            pass_on(k - 1)
        if k == 1:
            square_lines(range(lines // 2, lines))
            share_squares()
        if k == 2:
            for i, j in enumerate(others):
                receive(whole.at[pl.ds(past, LEAD), cols(j)], tail_send.at[1 + i], tail_recv.at[1 + i], (b, j))
            post_lead(0)
            send_n(whole, 2, cols(far), first_core)
            send_m(whole, 2, cols(far), first_core)
            send_n_quarter(2, place_of(0), is_end)
            sum_squares()
        if k == 3:
            send_m(whole, 2, cols(far), second_core)
            passed(0)
            passed(1)
            send_n(whole, 3, cols(cross), first_core)
            send_m(whole, 3, cols(cross), first_core)
            send_n_quarter(3, place_of(0), is_end)
            when(is_seam, lambda: post_lead(1))
            lag_squares()
        if k == 4:
            send_n(whole, 2, cols(far), second_core)
            passed(2)
            send_m(whole, 3, cols(cross), second_core)
            send_n_quarter(2, place_of(2), is_end)
            send_m(whole, 2, cols(far), is_near, (0,))
        if k == 5:
            passed(3)
            send_n(whole, 3, cols(cross), second_core)
            send_n_quarter(3, place_of(2), is_end)
            send_m(whole, 3, cols(cross), is_near, (0,))
        if k == 6:
            send_n_quarter(2, place_of(4), is_end)
            send_m(whole, 2, cols(far), is_near, (1,))
            for p in range(4):
                await_m(p)
            receive_lead(1, 0)
            add_products(mgram, mrows, near_half, True)
        if k == 7:
            passed(4)
            passed(5)
            send_n_quarter(3, place_of(4), is_end)
            send_m(whole, 3, cols(cross), is_near, (1,))
            when(ordinary, lambda: post_lead(1))
            when(jnp.logical_not(is_end), near_products)
    pass_on(7)
    send_n_quarter(2, place_of(6), is_end)
    passed(6)
    passed(7)
    send_n_quarter(3, place_of(6), is_end)
    for i in range(2):
        for w in range(2):
            leaves(whole.at[pl.ds(lead, LEAD), leads[i]], lead_send.at[2 * w + i], lead_recv.at[2 * w + i])
    for p in range(8):
        leaves(n_spot(p), n_send.at[p], n_recv.at[p], has_n)
        leaves(m_spot(p), m_send.at[p], m_recv.at[p], has_m)
    when(is_end, near_products)

    inv_row = jnp.concatenate([inv_ref[j : j + 1, :] for j in range(block // LANE)], axis=1)
    width_row = jnp.full((1, LANE), width_ref[0], jnp.float32) * (LAGS * dims)

    def down(line):
        return jnp.broadcast_to(line, (LANE, LANE)).T

    def row_values(inv, squares, count, skip=0):
        for j in range(count // LANE):
            line, part = pl.ds(f * (share // LANE) + skip + j, 1), pl.ds(j * LANE, LANE)
            row_factor[part, :] = down(-inv[line, :] / width_row)
            row_norms[part, :] = down(squares[line, :])

    def all_columns(x):
        return x[:, :block]

    def first_halves(x):
        return jnp.concatenate([x[:, g * share : g * share + part_rows] for g in range(4)], axis=1)

    def second_halves(x):
        return jnp.concatenate([x[:, g * share + part_rows : (g + 1) * share] for g in range(4)], axis=1)

    def tile(products_of, target, pick, parts, ready):
        per = target.shape[0] // 32 // parts
        for h in range(parts):
            for t in range(h * per + 1 if h else 0, (h + 1) * per + 1):
                x = products_of[pl.ds(t * 32, 40), :]
                for step in (1, 2, 4):
                    x = x + pltpu.roll(pltpu.roll(x, step, 0), step, 1)
                sums[pl.ds(t * 32, 32), :] = x[8:, :]
            for t in range(h * per, (h + 1) * per):
                x = sums[pl.ds(t * 32 + 32, 32), :]
                x = x + pltpu.roll(sums[pl.ds(t * 32 + 24, 32), :], 8, 1)
                x = x + pltpu.roll(sums[pl.ds(t * 32 + 16, 32), :], 16, 1)
                part = pl.ds(t * 32, 32)
                spread = row_norms[part, :][:, :1] + pick(norms[pl.ds(0, 1), :]) - 2.0 * pick(x)
                target[part, :] = jnp.exp(spread * (row_factor[part, :][:, :1] * pick(inv_row)))
            ready(h)

    receive(minv, inv_send.at[1], inv_recv.at[1], (before, f))
    receive(ninv, inv_send.at[0], inv_recv.at[0], (after, f))
    receive(nlagged, square_send.at[4], square_recv.at[4], (after, f))
    receive(mlagged, square_send.at[5], square_recv.at[5], (before, f))
    row_values(minv, mlagged, part_rows)
    for p in range(4, 8):
        await_m(p)
    receive_lead(1, 1)
    add_products(mgram, mrows, far_half, False)

    def send_mk(h):
        piece = mkept.at[pl.ds(h * (part_rows // PARTS), part_rows // PARTS), :]
        when(has_n, functools.partial(post, piece, mk_spot(h), mk_send.at[h], mk_recv.at[h], (before, f)))
        leaves(piece, mk_send.at[h], mk_recv.at[h], has_n)

    tile(mgram, mkept, all_columns, PARTS, send_mk)

    my_columns = pl.ds(multiple(f * share, share), share)
    my_first = pl.ds(multiple(f * share, part_rows), part_rows)
    lower = pl.ds(part_rows, part_rows)
    hops = ((0, far, f), (1, cross, far))

    def own_transposed(source):
        lines = [source[:, pl.ds(multiple(f * share + i * LANE, LANE), LANE)].T for i in range(share // LANE)]
        return jnp.concatenate(lines, axis=0)

    def turn_m(j):
        for i in range(share // LANE):
            part = pl.ds(multiple(j * share + i * LANE, LANE), LANE)
            mturned[part, :] = mkept[:, part].T

    for s, j, by in hops:
        turn_m(j)
        send(mturned.at[group(j), :], mturn_hop.at[s], turn_hop_send.at[2 + s], turn_hop_recv.at[2 + s], (over, by))
    turn_m(sib)
    send(mturned.at[group(sib), :], prev_ref.at[:, my_first], turn_send.at[5], turn_recv.at[5], (b, sib))
    prev_ref[:, my_first] = own_transposed(mkept)

    row_values(ninv, nlagged, share)
    for p in range(4, 8):
        await_n(p)
    receive_lead(0, 1)
    add_products(gram, nrows, far_half, False)

    def send_k(h):
        for g in range(4):
            piece, p = kept.at[pl.ds(h * part_rows, part_rows), pl.ds(g * part_rows, part_rows)], 4 * h + g
            when(has_m, functools.partial(post, piece, k_spot(p), k_send.at[p], k_recv.at[p], (after, f)))
            leaves(piece, k_send.at[p], k_recv.at[p], has_m)

    tile(gram, kept, second_halves, PARTS, send_k)

    def seconds(j):
        return pl.ds(multiple(j * part_rows, part_rows), part_rows)

    def turn(j):
        turned[seconds(j), :] = kept[:, seconds(j)].T

    for s, j, by in hops:
        turn(j)
        send(turned.at[seconds(j), :], turn_hop.at[s], turn_hop_send.at[s], turn_hop_recv.at[s], (over, by))
    turn(sib)
    send(turned.at[seconds(sib), :], next_ref.at[lower, my_columns], turn_send.at[2], turn_recv.at[2], (b, sib))
    next_ref[lower, my_columns] = kept[:, seconds(f)].T

    def firsts_of(j):
        return pl.ds(multiple(j * share, part_rows), part_rows)

    for s, j, to in ((0, f, far), (1, far, sib)):
        receive(mturn_hop.at[s], turn_hop_send.at[2 + s], turn_hop_recv.at[2 + s], (over, j))
        send(mturn_hop.at[s], prev_ref.at[:, firsts_of(j)], turn_send.at[3 + s], turn_recv.at[3 + s], (over, to))

    upper = pl.ds(0, part_rows)

    def rest_of_next():
        tile(gram, kept_rest, first_halves, 1, lambda h: None)
        for s, j, by in hops:
            turned_rest[seconds(j), :] = kept_rest[:, seconds(j)].T
            post(turned_rest.at[seconds(j), :], rest_hop.at[s], rest_hop_send.at[s], rest_hop_recv.at[s], (over, by))
        turned_rest[seconds(sib), :] = kept_rest[:, seconds(sib)].T
        post(
            turned_rest.at[seconds(sib), :],
            next_ref.at[upper, my_columns],
            rest_send.at[2],
            rest_recv.at[2],
            (b, sib),
        )
        next_ref[upper, my_columns] = kept_rest[:, seconds(f)].T
        for s, j, to in ((0, f, far), (1, far, sib)):
            receive(rest_hop.at[s], rest_hop_send.at[s], rest_hop_recv.at[s], (over, j))
            post(rest_hop.at[s], next_ref.at[upper, group(j)], rest_send.at[s], rest_recv.at[s], (over, to))

    def rest_of_prev():
        for qi in range(4):
            for i in range(2):
                sem = 6 + 2 * qi + i
                spot = mrows_rest.at[pl.ds(LEAD + i * quarter_rows, quarter_rows), cols(everyone[qi])]
                receive(spot, rest_send.at[sem], rest_recv.at[sem], (before, f))
        mrows_rest[pl.ds(0, LEAD), :] = mrows[pl.ds(part_rows, LEAD), :]
        add_products(mgram, mrows_rest, slice(None), True)
        row_values(minv, mlagged, part_rows, 1)
        tile(mgram, mkept_rest, all_columns, 1, lambda h: None)
        for s, j, by in hops:
            turn_rest(j)
            post(mturned_rest.at[group(j), :], mrest_hop.at[s], rest_hop_send.at[s], rest_hop_recv.at[s], (over, by))
        turn_rest(sib)
        post(mturned_rest.at[group(sib), :], prev_ref.at[:, my_second], rest_send.at[5], rest_recv.at[5], (b, sib))
        prev_ref[:, my_second] = own_transposed(mkept_rest)
        for s, j, to in ((0, f, far), (1, far, sib)):
            receive(mrest_hop.at[s], rest_hop_send.at[s], rest_hop_recv.at[s], (over, j))
            post(mrest_hop.at[s], prev_ref.at[:, seconds_of(j)], rest_send.at[3 + s], rest_recv.at[3 + s], (over, to))

    def turn_rest(j):
        for i in range(share // LANE):
            part = pl.ds(multiple(j * share + i * LANE, LANE), LANE)
            mturned_rest[part, :] = mkept_rest[:, part].T

    def seconds_of(j):
        return pl.ds(multiple(j * share + part_rows, part_rows), part_rows)

    my_second = seconds_of(f)
    when(is_end, rest_of_next)
    when(is_near, rest_of_prev)

    rows[pl.ds(0, LEAD), :] = whole[pl.ds(lead, LEAD), :]
    rows[pl.ds(LEAD, share), :] = whole[group(f), :]
    for j in range(4):
        same_products(order(chip, j) * share, share)
    same_products(block, LANE)
    row_values(inv_ref, lagged, share)

    def between(h):
        if h == 0:
            for s, j, to in ((0, f, far), (1, far, sib)):
                receive(turn_hop.at[s], turn_hop_send.at[s], turn_hop_recv.at[s], (over, j))
                send(turn_hop.at[s], next_ref.at[lower, group(j)], turn_send.at[s], turn_recv.at[s], (over, to))

    tile(same_gram, same_ref, all_columns, PARTS, between)

    def await_mk():
        for p in range(PARTS):
            receive(mk_spot(p), mk_send.at[p], mk_recv.at[p], (after, f))

    def await_k():
        for p in range(4 * PARTS):
            receive(k_spot(p), k_send.at[p], k_recv.at[p], (before, f))

    when(has_m, await_mk)
    when(has_n, await_k)

    def await_rest(i, dst, source):
        receive(dst, rest_send.at[i], rest_recv.at[i], (b, source))

    for i, j in enumerate((far, cross, sib)):
        when(is_end, functools.partial(await_rest, i, next_ref.at[upper, group(j)], j))
        when(is_near, functools.partial(await_rest, 3 + i, prev_ref.at[:, seconds_of(j)], j))
    for s in range(2):
        leaves(rest_hop.at[s], rest_hop_send.at[s], rest_hop_recv.at[s], is_seam)
        leaves(rest_hop.at[s], rest_send.at[s], rest_recv.at[s], is_end)
        leaves(mrest_hop.at[s], rest_send.at[3 + s], rest_recv.at[3 + s], is_near)
    leaves(turned_rest.at[seconds(sib), :], rest_send.at[2], rest_recv.at[2], is_end)
    leaves(mturned_rest.at[group(sib), :], rest_send.at[5], rest_recv.at[5], is_near)
    for i, j in enumerate((far, cross, sib)):
        receive(next_ref.at[lower, group(j)], turn_send.at[i], turn_recv.at[i], (b, j))
        receive(prev_ref.at[:, firsts_of(j)], turn_send.at[3 + i], turn_recv.at[3 + i], (b, j))
    for condition, copy in sent:
        if condition is None:
            copy.wait_send()
        else:
            when(condition, copy.wait_send)


def per_device(blocks, series, scales, width):
    block, quarter = series.shape
    dims, share, wide = 4 * quarter, block // 4, block + LANE
    part_rows = share // 2
    inv = (1.0 / scales.astype(jnp.float32)).reshape(block // LANE, LANE)
    out = jax.ShapeDtypeStruct((share, block), jnp.float32)
    raw = lambda *shape: pltpu.VMEM(shape, series.dtype)
    wider = lambda *shape: pltpu.VMEM(shape, jnp.float32)
    hops = 2 * CHUNKS
    pairs = (4, 1, hops, hops, hops, 4, 2, 6, 6, 4, 14, 2, PIECES, PIECES, 4 * PARTS, PARTS)
    counts = [n for n in pairs for _ in range(2)] + [hops]
    return pl.pallas_call(
        functools.partial(tiles_kernel, blocks),
        out_shape=(out, out, out),
        in_specs=[
            pl.BlockSpec(memory_space=pltpu.VMEM),
            pl.BlockSpec(memory_space=pltpu.VMEM),
            pl.BlockSpec(memory_space=pltpu.SMEM),
        ],
        out_specs=(pl.BlockSpec(memory_space=pltpu.VMEM),) * 3,
        scratch_shapes=[
            raw(wide, dims),
            raw(LEAD + share, dims),
            raw(LEAD + share, dims),
            raw(LEAD + part_rows, dims),
            raw(LEAD + part_rows, dims),
            wider(block // LANE, LANE),
            wider(block // LANE, LANE),
            wider(8 + LEAD + share, wide),
            wider(8 + LEAD + part_rows, wide),
            wider(8 + LEAD + share, wide),
            wider(LEAD + share, wide),
            wider(4, block // LANE, LANE),
        ]
        + [wider(block // LANE, LANE)] * 5
        + [
            wider(8, wide),
            wider(share, LANE),
            wider(share, LANE),
            wider(share, block // 2),
            wider(part_rows, block),
            wider(block // 2, share),
            wider(block, part_rows),
            wider(share, block // 2),
            wider(part_rows, block),
            wider(block // 2, share),
            wider(block, part_rows),
            raw(2, CHUNKS, 2 * share // CHUNKS, quarter),
            wider(2, part_rows, share),
            wider(2, share, part_rows),
            wider(2, part_rows, share),
            wider(2, share, part_rows),
        ]
        + [pltpu.SemaphoreType.DMA((n,)) for n in counts],
        compiler_params=pltpu.CompilerParams(
            collective_id=0, has_side_effects=True, vmem_limit_bytes=48 * 1024 * 1024
        ),
    )(series, inv, width)


def solution(mesh):
    in_specs = (P("blk", "feat"), P("blk"), P())
    out_specs = (P(("blk", "feat"), None), P(("blk", "feat"), None), P(("blk", "feat"), None))
    return jax.shard_map(
        functools.partial(per_device, mesh.shape["blk"]),
        mesh=mesh,
        in_specs=in_specs,
        out_specs=out_specs,
        check_vma=False,
    )
```

```python
import functools

import jax
import jax.numpy as jnp
from jax import lax
from jax.experimental import pallas as pl
from jax.experimental.pallas import tpu as pltpu
from jax.sharding import PartitionSpec as P

LAGS = 24
LEAD = 32
LANE = 128
CHUNKS = 8
PIECES = 8
PARTS = 2
MESH = pl.DeviceIdType.MESH
CONTRACT_LAST = (((1,), (1,)), ((), ()))


def multiple(value, of):
    return pl.multiple_of(value, of)


def tiles_kernel(
    blocks,
    series_ref,
    inv_ref,
    width_ref,
    same_ref,
    next_ref,
    prev_ref,
    whole,
    rows,
    nrows,
    mrows,
    mrows_rest,
    ninv,
    minv,
    gram,
    mgram,
    same_gram,
    sums,
    partial,
    squared,
    past_squared,
    lagged,
    nlagged,
    mlagged,
    norms,
    row_norms,
    row_factor,
    kept,
    mkept,
    turned,
    mturned,
    kept_rest,
    mkept_rest,
    turned_rest,
    mturned_rest,
    hop,
    turn_hop,
    mturn_hop,
    rest_hop,
    mrest_hop,
    tail_send,
    tail_recv,
    sib_send,
    sib_recv,
    hop_send,
    hop_recv,
    far_send,
    far_recv,
    pass_send,
    pass_recv,
    lead_send,
    lead_recv,
    inv_send,
    inv_recv,
    square_send,
    square_recv,
    turn_send,
    turn_recv,
    turn_hop_send,
    turn_hop_recv,
    rest_send,
    rest_recv,
    rest_hop_send,
    rest_hop_recv,
    n_send,
    n_recv,
    m_send,
    m_recv,
    k_send,
    k_recv,
    mk_send,
    mk_recv,
    ride_send,
):
    block, quarter = series_ref.shape
    dims = 4 * quarter
    share = block // 4
    part_rows = share // 2
    wide = block + LANE
    past = wide - LEAD

    b, f = lax.axis_index("blk"), lax.axis_index("feat")
    core, chip = lax.rem(f, 2), f // 2
    sib, far, cross = f + 1 - 2 * core, lax.rem(f + 2, 4), 3 - f
    after, before = lax.rem(b + 1, blocks), lax.rem(b + blocks - 1, blocks)
    half = blocks // 2
    pos, first = lax.rem(b, half), (b // half) * half
    over = lax.rem(b + half, blocks)
    others = (sib, far, cross)
    everyone = (f, sib, far, cross)
    near, end = first, first + half - 1
    is_near, is_end = pos == 0, pos == half - 1
    is_seam = jnp.logical_or(is_near, is_end)
    ordinary = jnp.logical_not(is_seam)

    barrier = pltpu.get_barrier_semaphore()
    peers = [(b, j) for j in others] + [(after, f), (before, f)] + [(over, j) for j in (f, far, sib)]
    for peer in peers:
        pl.semaphore_signal(barrier, inc=1, device_id=peer, device_id_type=MESH)

    def greet(condition, corners):
        @pl.when(condition)
        def _():
            for corner in corners:
                pl.semaphore_signal(barrier, inc=1, device_id=corner, device_id_type=MESH)
            pl.semaphore_wait(barrier, len(peers) + len(corners))

    greet(is_near, [(end, f), (end, sib)])
    greet(is_end, [(near, f), (near, sib)])

    @pl.when(ordinary)
    def _():
        pl.semaphore_wait(barrier, len(peers))

    sent = []

    def copy_of(src, dst, send_sem, recv_sem, to):
        return pltpu.make_async_remote_copy(
            src_ref=src, dst_ref=dst, send_sem=send_sem, recv_sem=recv_sem, device_id=to, device_id_type=MESH
        )

    def post(src, dst, send_sem, recv_sem, to):
        copy_of(src, dst, send_sem, recv_sem, to).start()

    def leaves(src, send_sem, recv_sem, condition=None):
        sent.append((condition, copy_of(src, src, send_sem, recv_sem, (b, sib))))

    def send(src, dst, send_sem, recv_sem, to):
        post(src, dst, send_sem, recv_sem, to)
        leaves(src, send_sem, recv_sem)

    def receive(dst, send_sem, recv_sem, sender):
        copy_of(dst, dst, send_sem, recv_sem, sender).wait_recv()

    def when(condition, act):
        @pl.when(condition)
        def _():
            act()

    def cols(q):
        return pl.ds(multiple(q * quarter, quarter), quarter)

    def group(g):
        return pl.ds(multiple(g * share, share), share)

    def n_spot(p):
        return nrows.at[pl.ds(LEAD + (p % 2) * part_rows, part_rows), cols(everyone[p // 2])]

    def m_spot(p):
        size = part_rows // 2
        return mrows.at[pl.ds(LEAD + (p % 2) * size, size), cols(everyone[p // 2])]

    def k_spot(p):
        g, h = p % 4, p // 4
        return prev_ref.at[pl.ds(h * part_rows, part_rows), pl.ds(g * share + part_rows, part_rows)]

    def mk_spot(p):
        size = part_rows // PARTS
        return next_ref.at[pl.ds(p * size, size), :]

    quarter_rows = share // 4

    def own_rows(ref, start, size, columns):
        return ref.at[pl.ds(multiple(f * share + start, size), size), columns]

    def send_n(ref, qi, columns, condition):
        for p in (2 * qi, 2 * qi + 1):
            piece = own_rows(ref, (p % 2) * part_rows, part_rows, columns)
            when(condition, functools.partial(post, piece, n_spot(p), n_send.at[p], n_recv.at[p], (before, f)))

    def send_n_quarter(qi, i, condition):
        p, columns = 2 * qi + i // 2, cols(everyone[qi])
        piece = own_rows(whole, i * quarter_rows, quarter_rows, columns)
        spot = nrows.at[pl.ds(LEAD + i * quarter_rows, quarter_rows), columns]
        when(condition, functools.partial(post, piece, spot, n_send.at[p], n_recv.at[p], (before, f)))

    def send_m(ref, qi, columns, condition, pieces=(0, 1)):
        for i in pieces:
            p = 2 * qi + i
            piece = own_rows(ref, i * quarter_rows, quarter_rows, columns)
            when(condition, functools.partial(post, piece, m_spot(p), m_send.at[p], m_recv.at[p], (after, f)))

    def await_n(p):
        receive(n_spot(p), n_send.at[p], n_recv.at[p], (after, f))

    def await_m(p):
        receive(m_spot(p), m_send.at[p], m_recv.at[p], (before, f))

    has_n, has_m = jnp.logical_not(is_near), jnp.logical_not(is_end)

    def order(c, j):
        return j + c * (2, 2, -1, -3)[j]

    def place_of(k):
        return (k // 2 + 3) % 4

    def halved(sender, k, s):
        c = sender if s == 0 else 1 - sender
        usual = order(1 - sender, k // 2) * share + (k % 2) * 2 * quarter_rows + s * quarter_rows
        at_seam = (2 * c + k % 2) * share + place_of(k) * quarter_rows
        return pl.ds(multiple(jnp.where(is_seam, at_seam, usual), quarter_rows), quarter_rows)

    send(
        series_ref.at[pl.ds(block - LEAD, LEAD), :],
        whole.at[pl.ds(past, LEAD), cols(f)],
        tail_send.at[0],
        tail_recv.at[0],
        (after, f),
    )

    def set_out(k):
        for s, j in enumerate((f, far)):
            i = CHUNKS * s + k
            send(series_ref.at[halved(chip, k, s), :], hop.at[s, k], hop_send.at[i], hop_recv.at[i], (over, j))

    def hand_over(k):
        for s, j in enumerate((f, far)):
            i = CHUNKS * s + k
            receive(hop.at[s, k], hop_send.at[i], hop_recv.at[i], (over, j))
            c, to = (chip, far) if s == 0 else (1 - chip, f)
            send(hop.at[s, k], whole.at[halved(c, k, s), cols(j)], far_send.at[i], far_recv.at[i], (over, to))

            to, place = 2 * chip + k % 2, place_of(k)
            qi = lax.rem(core + k % 2, 2) + 2 * s
            spot = pl.ds(LEAD + place * quarter_rows, quarter_rows)

            def ride_back():
                post(
                    hop.at[s, k], nrows.at[spot, cols(j)], ride_send.at[i], n_recv.at[2 * qi + place // 2], (end, to)
                )

            def ride_on():
                at = pl.ds(LEAD + (place % 2) * quarter_rows, quarter_rows)
                rows_there = mrows if place < 2 else mrows_rest
                sem = m_recv.at[2 * qi + place] if place < 2 else rest_recv.at[6 + 2 * qi + place - 2]
                post(hop.at[s, k], rows_there.at[at, cols(j)], ride_send.at[i], sem, (near, to))

            when(is_near, ride_back)
            leaves(hop.at[s, k], ride_send.at[i], n_recv.at[0], is_near)
            when(is_end, ride_on)
            leaves(hop.at[s, k], ride_send.at[i], n_recv.at[0], is_end)

    set_out(0)
    set_out(1)
    send(series_ref, whole.at[pl.ds(0, block), cols(f)], sib_send.at[0], sib_recv.at[0], (b, sib))
    send_n(series_ref, 0, slice(None), has_n)
    send_m(series_ref, 0, slice(None), has_m)
    send(inv_ref, ninv, inv_send.at[0], inv_recv.at[0], (before, f))
    send(inv_ref, minv, inv_send.at[1], inv_recv.at[1], (after, f))

    whole[pl.ds(0, block), cols(f)] = series_ref[...]
    whole[pl.ds(block, LANE - LEAD), :] = jnp.zeros((LANE - LEAD, dims), whole.dtype)
    for buffer in (gram, mgram, same_gram):
        buffer[pl.ds(0, 8), :] = jnp.zeros((8, wide), jnp.float32)

    def pass_on(k):
        for s in range(2):
            i = CHUNKS * s + k
            piece = whole.at[halved(1 - chip, k, s), cols(far)]
            receive(piece, far_send.at[i], far_recv.at[i], (over, far if s == 0 else f))
            send(piece, piece, pass_send.at[i], pass_recv.at[i], (b, sib))

    def passed(k):
        for s in range(2):
            i = CHUNKS * s + k
            piece = whole.at[halved(1 - chip, k, s), cols(cross)]
            receive(piece, pass_send.at[i], pass_recv.at[i], (b, sib))

    lead = multiple(lax.rem(f * share + wide - LEAD, wide), LEAD)
    near_half = pl.ds(multiple(chip * 2 * quarter, quarter), 2 * quarter)
    far_half = pl.ds(multiple((1 - chip) * 2 * quarter, quarter), 2 * quarter)
    leads = (near_half, far_half)
    lead_ways = ((nrows, before, after), (mrows, after, before))

    def post_lead(i):
        for w, (dst, to, _) in enumerate(lead_ways):
            s = 2 * w + i
            post(
                whole.at[pl.ds(lead, LEAD), leads[i]],
                dst.at[pl.ds(0, LEAD), leads[i]],
                lead_send.at[s],
                lead_recv.at[s],
                (to, f),
            )

    def receive_lead(w, i):
        dst, _, sender = lead_ways[w]
        receive(dst.at[pl.ds(0, LEAD), leads[i]], lead_send.at[2 * w + i], lead_recv.at[2 * w + i], (sender, f))

    lines = block // LANE

    def square_lines(lines_now):
        for j in lines_now:
            x = whole[pl.ds(j * LANE, LANE), cols(f)]
            total = jnp.zeros((LANE, LANE), jnp.float32)
            for g in range(quarter // LANE):
                piece = x[:, g * LANE : (g + 1) * LANE].astype(jnp.float32)
                total = total + piece * piece
            partial[pl.ds(f, 1), pl.ds(j, 1), :] = jnp.sum(total.T, axis=0, keepdims=True)[None]

    def share_squares():
        for i, j in enumerate(others):
            send(partial.at[f], partial.at[f], square_send.at[i], square_recv.at[i], (b, j))

    def sum_squares():
        for i, j in enumerate(others):
            receive(partial.at[j], square_send.at[i], square_recv.at[i], (b, j))
        squared[...] = partial[0] + partial[1] + partial[2] + partial[3]
        send(squared, past_squared, square_send.at[3], square_recv.at[3], (after, f))

    def lag_squares():
        receive(past_squared, square_send.at[3], square_recv.at[3], (before, f))
        line = [squared[j : j + 1, :] for j in range(lines)] + [past_squared[lines - 1 : lines, :]]
        norms[...] = lag_sum(jnp.broadcast_to(jnp.concatenate(line, axis=1), (8, wide)), 1)
        for j in range(lines):
            lagged[j : j + 1, :] = norms[0:1, j * LANE : (j + 1) * LANE]
        send(lagged, nlagged, square_send.at[4], square_recv.at[4], (before, f))
        send(lagged, mlagged, square_send.at[5], square_recv.at[5], (after, f))

    def lag_sum(x, axis):
        for step in (1, 2, 4):
            x = x + pltpu.roll(x, step, axis)
        return x + pltpu.roll(x, 8, axis) + pltpu.roll(x, 16, axis)

    def products(left, right):
        return lax.dot_general(left, right, CONTRACT_LAST, preferred_element_type=jnp.float32)

    def own_group(which):
        rows[pl.ds(0, LEAD), which] = whole[pl.ds(lead, LEAD), which]
        rows[pl.ds(LEAD, share), which] = whole[group(f), which]

    def add_products(target, source, which, fresh):
        size, height = 256, source.shape[0]
        for start in range(0, wide, size):
            part = pl.ds(start, min(size, wide - start))
            found = products(source[:, which], whole[part, which])
            if fresh:
                target[pl.ds(8, height), part] = found
            else:
                target[pl.ds(8, height), part] += found

    def near_products():
        for p in range(4):
            await_n(p)
        receive_lead(0, 0)
        add_products(gram, nrows, near_half, True)

    both = jnp.logical_and
    first_core, second_core = both(ordinary, core == 0), both(ordinary, core == 1)
    for k in range(CHUNKS):
        hand_over(k)
        if k + 2 < CHUNKS:
            set_out(k + 2)
        if k == 0:
            receive(whole.at[pl.ds(0, block), cols(sib)], sib_send.at[0], sib_recv.at[0], (b, sib))
            send_n(whole, 1, cols(sib), has_n)
            send_m(whole, 1, cols(sib), has_m)
            tail = whole.at[pl.ds(past, LEAD), cols(f)]
            receive(tail, tail_send.at[0], tail_recv.at[0], (before, f))
            for i, j in enumerate(others):
                send(tail, tail, tail_send.at[1 + i], tail_recv.at[1 + i], (b, j))
            square_lines(range(lines // 2))
        else:
            pass_on(k - 1)
        if k == 1:
            square_lines(range(lines // 2, lines))
            share_squares()
        if k == 2:
            for i, j in enumerate(others):
                receive(whole.at[pl.ds(past, LEAD), cols(j)], tail_send.at[1 + i], tail_recv.at[1 + i], (b, j))
            post_lead(0)
            send_n(whole, 2, cols(far), first_core)
            send_m(whole, 2, cols(far), first_core)
            send_n_quarter(2, place_of(0), is_end)
            sum_squares()
        if k == 3:
            send_m(whole, 2, cols(far), second_core)
            passed(0)
            passed(1)
            send_n(whole, 3, cols(cross), first_core)
            send_m(whole, 3, cols(cross), first_core)
            send_n_quarter(3, place_of(0), is_end)
            when(is_seam, lambda: post_lead(1))
            lag_squares()
        if k == 4:
            send_n(whole, 2, cols(far), second_core)
            passed(2)
            send_m(whole, 3, cols(cross), second_core)
            send_n_quarter(2, place_of(2), is_end)
            send_m(whole, 2, cols(far), is_near, (0,))
            own_group(near_half)
            add_products(same_gram, rows, near_half, True)
        if k == 5:
            passed(3)
            send_n(whole, 3, cols(cross), second_core)
            send_n_quarter(3, place_of(2), is_end)
            send_m(whole, 3, cols(cross), is_near, (0,))
        if k == 6:
            send_n_quarter(2, place_of(4), is_end)
            send_m(whole, 2, cols(far), is_near, (1,))
            for p in range(4):
                await_m(p)
            receive_lead(1, 0)
            add_products(mgram, mrows, near_half, True)
        if k == 7:
            passed(4)
            passed(5)
            send_n_quarter(3, place_of(4), is_end)
            send_m(whole, 3, cols(cross), is_near, (1,))
            when(ordinary, lambda: post_lead(1))
            when(jnp.logical_not(is_end), near_products)
    pass_on(7)
    send_n_quarter(2, place_of(6), is_end)
    passed(6)
    passed(7)
    send_n_quarter(3, place_of(6), is_end)
    for i in range(2):
        for w in range(2):
            leaves(whole.at[pl.ds(lead, LEAD), leads[i]], lead_send.at[2 * w + i], lead_recv.at[2 * w + i])
    for p in range(8):
        leaves(n_spot(p), n_send.at[p], n_recv.at[p], has_n)
        leaves(m_spot(p), m_send.at[p], m_recv.at[p], has_m)
    when(is_end, near_products)

    inv_row = jnp.concatenate([inv_ref[j : j + 1, :] for j in range(block // LANE)], axis=1)
    width_row = jnp.full((1, LANE), width_ref[0], jnp.float32) * (LAGS * dims)

    def down(line):
        return jnp.broadcast_to(line, (LANE, LANE)).T

    def row_values(inv, squares, count, skip=0):
        for j in range(count // LANE):
            line, part = pl.ds(f * (share // LANE) + skip + j, 1), pl.ds(j * LANE, LANE)
            row_factor[part, :] = down(-inv[line, :] / width_row)
            row_norms[part, :] = down(squares[line, :])

    middle = block // 2

    def with_lead(ref, part, c):
        if c:
            return ref[part, middle - LANE : block]
        return jnp.concatenate([ref[part, block:wide], ref[part, :middle]], axis=1)

    def all_columns(c):
        return [(c * middle, middle)]

    def first_halves(c):
        return [(g * share, part_rows) for g in (2 * c, 2 * c + 1)]

    def second_halves(c):
        return [(g * share + part_rows, part_rows) for g in (2 * c, 2 * c + 1)]

    def tile(products_of, target, pick, parts, ready):
        per = target.shape[0] // 32 // parts
        span = target.shape[1] // 2
        for h in range(parts):
            for c in range(2):
                for t in range(h * per + 1 if h else 0, (h + 1) * per + 1):
                    x = with_lead(products_of, pl.ds(t * 32, 40), c)
                    for step in (1, 2, 4):
                        x = x + pltpu.roll(pltpu.roll(x, step, 0), step, 1)
                    part = pl.ds(t * 32, 32)
                    sums[part, c * middle : (c + 1) * middle] = x[8:, LANE:]
                    if c == 0:
                        sums[part, block:wide] = x[8:, :LANE]
                picked = lambda x, base: jnp.concatenate([x[:, s - base : s - base + n] for s, n in pick(c)], axis=1)
                for t in range(h * per, (h + 1) * per):
                    x = with_lead(sums, pl.ds(t * 32 + 32, 32), c)
                    x = x + pltpu.roll(with_lead(sums, pl.ds(t * 32 + 24, 32), c), 8, 1)
                    x = x + pltpu.roll(with_lead(sums, pl.ds(t * 32 + 16, 32), c), 16, 1)
                    part = pl.ds(t * 32, 32)
                    found = picked(x, c * middle - LANE)
                    spread = row_norms[part, :][:, :1] + picked(norms[pl.ds(0, 1), :], 0) - 2.0 * found
                    values = jnp.exp(spread * (row_factor[part, :][:, :1] * picked(inv_row, 0)))
                    target[part, c * span : (c + 1) * span] = values
            ready(h)

    receive(minv, inv_send.at[1], inv_recv.at[1], (before, f))
    receive(ninv, inv_send.at[0], inv_recv.at[0], (after, f))
    receive(nlagged, square_send.at[4], square_recv.at[4], (after, f))
    receive(mlagged, square_send.at[5], square_recv.at[5], (before, f))
    row_values(minv, mlagged, part_rows)
    for p in range(4, 8):
        await_m(p)
    receive_lead(1, 1)
    add_products(mgram, mrows, far_half, False)

    def send_mk(h):
        piece = mkept.at[pl.ds(h * (part_rows // PARTS), part_rows // PARTS), :]
        when(has_n, functools.partial(post, piece, mk_spot(h), mk_send.at[h], mk_recv.at[h], (before, f)))
        leaves(piece, mk_send.at[h], mk_recv.at[h], has_n)

    tile(mgram, mkept, all_columns, PARTS, send_mk)

    my_columns = pl.ds(multiple(f * share, share), share)
    my_first = pl.ds(multiple(f * share, part_rows), part_rows)
    lower = pl.ds(part_rows, part_rows)
    hops = ((0, far, f), (1, cross, far))

    def own_transposed(source):
        lines = [source[:, pl.ds(multiple(f * share + i * LANE, LANE), LANE)].T for i in range(share // LANE)]
        return jnp.concatenate(lines, axis=0)

    def turn_m(j):
        for i in range(share // LANE):
            part = pl.ds(multiple(j * share + i * LANE, LANE), LANE)
            mturned[part, :] = mkept[:, part].T

    for s, j, by in hops:
        turn_m(j)
        send(mturned.at[group(j), :], mturn_hop.at[s], turn_hop_send.at[2 + s], turn_hop_recv.at[2 + s], (over, by))
    turn_m(sib)
    send(mturned.at[group(sib), :], prev_ref.at[:, my_first], turn_send.at[5], turn_recv.at[5], (b, sib))
    prev_ref[:, my_first] = own_transposed(mkept)

    row_values(ninv, nlagged, share)
    for p in range(4, 8):
        await_n(p)
    receive_lead(0, 1)
    add_products(gram, nrows, far_half, False)

    def send_k(h):
        for g in range(4):
            piece, p = kept.at[pl.ds(h * part_rows, part_rows), pl.ds(g * part_rows, part_rows)], 4 * h + g
            when(has_m, functools.partial(post, piece, k_spot(p), k_send.at[p], k_recv.at[p], (after, f)))
            leaves(piece, k_send.at[p], k_recv.at[p], has_m)

    tile(gram, kept, second_halves, PARTS, send_k)

    def seconds(j):
        return pl.ds(multiple(j * part_rows, part_rows), part_rows)

    def turn(j):
        turned[seconds(j), :] = kept[:, seconds(j)].T

    for s, j, by in hops:
        turn(j)
        send(turned.at[seconds(j), :], turn_hop.at[s], turn_hop_send.at[s], turn_hop_recv.at[s], (over, by))
    turn(sib)
    send(turned.at[seconds(sib), :], next_ref.at[lower, my_columns], turn_send.at[2], turn_recv.at[2], (b, sib))
    next_ref[lower, my_columns] = kept[:, seconds(f)].T

    def firsts_of(j):
        return pl.ds(multiple(j * share, part_rows), part_rows)

    upper = pl.ds(0, part_rows)

    def rest_of_next():
        tile(gram, kept_rest, first_halves, 1, lambda h: None)
        for s, j, by in hops:
            turned_rest[seconds(j), :] = kept_rest[:, seconds(j)].T
            post(turned_rest.at[seconds(j), :], rest_hop.at[s], rest_hop_send.at[s], rest_hop_recv.at[s], (over, by))
        turned_rest[seconds(sib), :] = kept_rest[:, seconds(sib)].T
        post(
            turned_rest.at[seconds(sib), :],
            next_ref.at[upper, my_columns],
            rest_send.at[2],
            rest_recv.at[2],
            (b, sib),
        )
        next_ref[upper, my_columns] = kept_rest[:, seconds(f)].T

    def relay_rest_of_next():
        for s, j, to in ((0, f, far), (1, far, sib)):
            receive(rest_hop.at[s], rest_hop_send.at[s], rest_hop_recv.at[s], (over, j))
            post(rest_hop.at[s], next_ref.at[upper, group(j)], rest_send.at[s], rest_recv.at[s], (over, to))

    def rest_of_prev():
        for qi in range(4):
            for i in range(2):
                sem = 6 + 2 * qi + i
                spot = mrows_rest.at[pl.ds(LEAD + i * quarter_rows, quarter_rows), cols(everyone[qi])]
                receive(spot, rest_send.at[sem], rest_recv.at[sem], (before, f))
        mrows_rest[pl.ds(0, LEAD), :] = mrows[pl.ds(part_rows, LEAD), :]
        add_products(mgram, mrows_rest, slice(None), True)
        row_values(minv, mlagged, part_rows, 1)
        tile(mgram, mkept_rest, all_columns, 1, lambda h: None)
        for s, j, by in hops:
            turn_rest(j)
            post(mturned_rest.at[group(j), :], mrest_hop.at[s], rest_hop_send.at[s], rest_hop_recv.at[s], (over, by))
        turn_rest(sib)
        post(mturned_rest.at[group(sib), :], prev_ref.at[:, my_second], rest_send.at[5], rest_recv.at[5], (b, sib))
        prev_ref[:, my_second] = own_transposed(mkept_rest)

    def relay_rest_of_prev():
        for s, j, to in ((0, f, far), (1, far, sib)):
            receive(mrest_hop.at[s], rest_hop_send.at[s], rest_hop_recv.at[s], (over, j))
            post(mrest_hop.at[s], prev_ref.at[:, seconds_of(j)], rest_send.at[3 + s], rest_recv.at[3 + s], (over, to))

    def turn_rest(j):
        for i in range(share // LANE):
            part = pl.ds(multiple(j * share + i * LANE, LANE), LANE)
            mturned_rest[part, :] = mkept_rest[:, part].T

    def seconds_of(j):
        return pl.ds(multiple(j * share + part_rows, part_rows), part_rows)

    my_second = seconds_of(f)
    for s, j, to in ((0, f, far), (1, far, sib)):
        receive(mturn_hop.at[s], turn_hop_send.at[2 + s], turn_hop_recv.at[2 + s], (over, j))
        send(mturn_hop.at[s], prev_ref.at[:, firsts_of(j)], turn_send.at[3 + s], turn_recv.at[3 + s], (over, to))

    when(is_end, rest_of_next)
    when(is_near, rest_of_prev)

    own_group(far_half)
    add_products(same_gram, rows, far_half, False)
    row_values(inv_ref, lagged, share)

    def between(h):
        if h == 0:
            for s, j, to in ((0, f, far), (1, far, sib)):
                receive(turn_hop.at[s], turn_hop_send.at[s], turn_hop_recv.at[s], (over, j))
                send(turn_hop.at[s], next_ref.at[lower, group(j)], turn_send.at[s], turn_recv.at[s], (over, to))
            when(is_end, relay_rest_of_next)
            when(is_near, relay_rest_of_prev)

    tile(same_gram, same_ref, all_columns, PARTS, between)

    def await_mk():
        for p in range(PARTS):
            receive(mk_spot(p), mk_send.at[p], mk_recv.at[p], (after, f))

    def await_k():
        for p in range(4 * PARTS):
            receive(k_spot(p), k_send.at[p], k_recv.at[p], (before, f))

    when(has_m, await_mk)
    when(has_n, await_k)

    def await_rest(i, dst, source):
        receive(dst, rest_send.at[i], rest_recv.at[i], (b, source))

    for i, j in enumerate((far, cross, sib)):
        when(is_end, functools.partial(await_rest, i, next_ref.at[upper, group(j)], j))
        when(is_near, functools.partial(await_rest, 3 + i, prev_ref.at[:, seconds_of(j)], j))
    for s in range(2):
        leaves(rest_hop.at[s], rest_hop_send.at[s], rest_hop_recv.at[s], is_seam)
        leaves(rest_hop.at[s], rest_send.at[s], rest_recv.at[s], is_end)
        leaves(mrest_hop.at[s], rest_send.at[3 + s], rest_recv.at[3 + s], is_near)
    leaves(turned_rest.at[seconds(sib), :], rest_send.at[2], rest_recv.at[2], is_end)
    leaves(mturned_rest.at[group(sib), :], rest_send.at[5], rest_recv.at[5], is_near)
    for i, j in enumerate((far, cross, sib)):
        receive(next_ref.at[lower, group(j)], turn_send.at[i], turn_recv.at[i], (b, j))
        receive(prev_ref.at[:, firsts_of(j)], turn_send.at[3 + i], turn_recv.at[3 + i], (b, j))
    for condition, copy in sent:
        if condition is None:
            copy.wait_send()
        else:
            when(condition, copy.wait_send)


def per_device(blocks, series, scales, width):
    block, quarter = series.shape
    dims, share, wide = 4 * quarter, block // 4, block + LANE
    part_rows = share // 2
    inv = (1.0 / scales.astype(jnp.float32)).reshape(block // LANE, LANE)
    out = jax.ShapeDtypeStruct((share, block), jnp.float32)
    raw = lambda *shape: pltpu.VMEM(shape, series.dtype)
    wider = lambda *shape: pltpu.VMEM(shape, jnp.float32)
    hops = 2 * CHUNKS
    pairs = (4, 1, hops, hops, hops, 4, 2, 6, 6, 4, 14, 2, PIECES, PIECES, 4 * PARTS, PARTS)
    counts = [n for n in pairs for _ in range(2)] + [hops]
    return pl.pallas_call(
        functools.partial(tiles_kernel, blocks),
        out_shape=(out, out, out),
        in_specs=[
            pl.BlockSpec(memory_space=pltpu.VMEM),
            pl.BlockSpec(memory_space=pltpu.VMEM),
            pl.BlockSpec(memory_space=pltpu.SMEM),
        ],
        out_specs=(pl.BlockSpec(memory_space=pltpu.VMEM),) * 3,
        scratch_shapes=[
            raw(wide, dims),
            raw(LEAD + share, dims),
            raw(LEAD + share, dims),
            raw(LEAD + part_rows, dims),
            raw(LEAD + part_rows, dims),
            wider(block // LANE, LANE),
            wider(block // LANE, LANE),
            wider(8 + LEAD + share, wide),
            wider(8 + LEAD + part_rows, wide),
            wider(8 + LEAD + share, wide),
            wider(LEAD + share, wide),
            wider(4, block // LANE, LANE),
        ]
        + [wider(block // LANE, LANE)] * 5
        + [
            wider(8, wide),
            wider(share, LANE),
            wider(share, LANE),
            wider(share, block // 2),
            wider(part_rows, block),
            wider(block // 2, share),
            wider(block, part_rows),
            wider(share, block // 2),
            wider(part_rows, block),
            wider(block // 2, share),
            wider(block, part_rows),
            raw(2, CHUNKS, 2 * share // CHUNKS, quarter),
            wider(2, part_rows, share),
            wider(2, share, part_rows),
            wider(2, part_rows, share),
            wider(2, share, part_rows),
        ]
        + [pltpu.SemaphoreType.DMA((n,)) for n in counts],
        compiler_params=pltpu.CompilerParams(
            collective_id=0, has_side_effects=True, vmem_limit_bytes=48 * 1024 * 1024
        ),
    )(series, inv, width)


def solution(mesh):
    in_specs = (P("blk", "feat"), P("blk"), P())
    out_specs = (P(("blk", "feat"), None), P(("blk", "feat"), None), P(("blk", "feat"), None))
    return jax.shard_map(
        functools.partial(per_device, mesh.shape["blk"]),
        mesh=mesh,
        in_specs=in_specs,
        out_specs=out_specs,
        check_vma=False,
    )
```

```python
import functools

import jax
import jax.numpy as jnp
from jax import lax
from jax.experimental import pallas as pl
from jax.experimental.pallas import tpu as pltpu
from jax.sharding import PartitionSpec as P

LAGS = 24
LEAD = 32
LANE = 128
CHUNKS = 8
PIECES = 8
PARTS = 2
AHEAD = 4
MESH = pl.DeviceIdType.MESH
CONTRACT_LAST = (((1,), (1,)), ((), ()))


def multiple(value, of):
    return pl.multiple_of(value, of)


def tiles_kernel(
    blocks,
    series_ref,
    inv_ref,
    width_ref,
    same_ref,
    next_ref,
    prev_ref,
    whole,
    rows,
    nrows,
    mrows,
    mrows_rest,
    ninv,
    minv,
    gram,
    mgram,
    same_gram,
    sums,
    partial,
    squared,
    past_squared,
    lagged,
    nlagged,
    mlagged,
    norms,
    row_norms,
    row_factor,
    kept,
    mkept,
    turned,
    mturned,
    kept_rest,
    mkept_rest,
    turned_rest,
    mturned_rest,
    hop,
    turn_hop,
    mturn_hop,
    rest_hop,
    mrest_hop,
    tail_send,
    tail_recv,
    sib_send,
    sib_recv,
    hop_send,
    hop_recv,
    far_send,
    far_recv,
    pass_send,
    pass_recv,
    lead_send,
    lead_recv,
    inv_send,
    inv_recv,
    square_send,
    square_recv,
    turn_send,
    turn_recv,
    turn_hop_send,
    turn_hop_recv,
    rest_send,
    rest_recv,
    rest_hop_send,
    rest_hop_recv,
    n_send,
    n_recv,
    m_send,
    m_recv,
    k_send,
    k_recv,
    mk_send,
    mk_recv,
    ride_send,
):
    block, quarter = series_ref.shape
    dims = 4 * quarter
    share = block // 4
    part_rows = share // 2
    wide = block + LANE
    past = wide - LEAD

    b, f = lax.axis_index("blk"), lax.axis_index("feat")
    core, chip = lax.rem(f, 2), f // 2
    sib, far, cross = f + 1 - 2 * core, lax.rem(f + 2, 4), 3 - f
    after, before = lax.rem(b + 1, blocks), lax.rem(b + blocks - 1, blocks)
    half = blocks // 2
    pos, first = lax.rem(b, half), (b // half) * half
    over = lax.rem(b + half, blocks)
    others = (sib, far, cross)
    everyone = (f, sib, far, cross)
    near, end = first, first + half - 1
    is_near, is_end = pos == 0, pos == half - 1
    is_seam = jnp.logical_or(is_near, is_end)
    ordinary = jnp.logical_not(is_seam)

    barrier = pltpu.get_barrier_semaphore()
    peers = [(b, j) for j in others] + [(after, f), (before, f)] + [(over, j) for j in (f, far, sib)]
    for peer in peers:
        pl.semaphore_signal(barrier, inc=1, device_id=peer, device_id_type=MESH)

    def greet(condition, corners):
        @pl.when(condition)
        def _():
            for corner in corners:
                pl.semaphore_signal(barrier, inc=1, device_id=corner, device_id_type=MESH)
            pl.semaphore_wait(barrier, len(peers) + len(corners))

    greet(is_near, [(end, f), (end, sib)])
    greet(is_end, [(near, f), (near, sib)])

    @pl.when(ordinary)
    def _():
        pl.semaphore_wait(barrier, len(peers))

    sent = []

    def copy_of(src, dst, send_sem, recv_sem, to):
        return pltpu.make_async_remote_copy(
            src_ref=src, dst_ref=dst, send_sem=send_sem, recv_sem=recv_sem, device_id=to, device_id_type=MESH
        )

    def post(src, dst, send_sem, recv_sem, to):
        copy_of(src, dst, send_sem, recv_sem, to).start()

    def leaves(src, send_sem, recv_sem, condition=None):
        sent.append((condition, copy_of(src, src, send_sem, recv_sem, (b, sib))))

    def send(src, dst, send_sem, recv_sem, to):
        post(src, dst, send_sem, recv_sem, to)
        leaves(src, send_sem, recv_sem)

    def receive(dst, send_sem, recv_sem, sender):
        copy_of(dst, dst, send_sem, recv_sem, sender).wait_recv()

    def when(condition, act):
        @pl.when(condition)
        def _():
            act()

    def cols(q):
        return pl.ds(multiple(q * quarter, quarter), quarter)

    def group(g):
        return pl.ds(multiple(g * share, share), share)

    def n_spot(p):
        return nrows.at[pl.ds(LEAD + (p % 2) * part_rows, part_rows), cols(everyone[p // 2])]

    def m_spot(p):
        size = part_rows // 2
        return mrows.at[pl.ds(LEAD + (p % 2) * size, size), cols(everyone[p // 2])]

    def k_spot(p):
        g, h = p % 4, p // 4
        return prev_ref.at[pl.ds(h * part_rows, part_rows), pl.ds(g * share + part_rows, part_rows)]

    def mk_spot(p):
        size = part_rows // PARTS
        return next_ref.at[pl.ds(p * size, size), :]

    quarter_rows = share // 4

    def own_rows(ref, start, size, columns):
        return ref.at[pl.ds(multiple(f * share + start, size), size), columns]

    def send_n(ref, qi, columns, condition):
        for p in (2 * qi, 2 * qi + 1):
            piece = own_rows(ref, (p % 2) * part_rows, part_rows, columns)
            when(condition, functools.partial(post, piece, n_spot(p), n_send.at[p], n_recv.at[p], (before, f)))

    def send_n_quarter(qi, i, condition):
        p, columns = 2 * qi + i // 2, cols(everyone[qi])
        piece = own_rows(whole, i * quarter_rows, quarter_rows, columns)
        spot = nrows.at[pl.ds(LEAD + i * quarter_rows, quarter_rows), columns]
        when(condition, functools.partial(post, piece, spot, n_send.at[p], n_recv.at[p], (before, f)))

    def send_m(ref, qi, columns, condition, pieces=(0, 1)):
        for i in pieces:
            p = 2 * qi + i
            piece = own_rows(ref, i * quarter_rows, quarter_rows, columns)
            when(condition, functools.partial(post, piece, m_spot(p), m_send.at[p], m_recv.at[p], (after, f)))

    def await_n(p):
        receive(n_spot(p), n_send.at[p], n_recv.at[p], (after, f))

    def await_m(p):
        receive(m_spot(p), m_send.at[p], m_recv.at[p], (before, f))

    has_n, has_m = jnp.logical_not(is_near), jnp.logical_not(is_end)

    def order(c, j):
        return j + c * (2, 2, -1, -3)[j]

    def place_of(k):
        return (k // 2 + 3) % 4

    def halved(sender, k, s):
        c = sender if s == 0 else 1 - sender
        usual = order(1 - sender, k // 2) * share + (k % 2) * 2 * quarter_rows + s * quarter_rows
        at_seam = (2 * c + k % 2) * share + place_of(k) * quarter_rows
        return pl.ds(multiple(jnp.where(is_seam, at_seam, usual), quarter_rows), quarter_rows)

    send(
        series_ref.at[pl.ds(block - LEAD, LEAD), :],
        whole.at[pl.ds(past, LEAD), cols(f)],
        tail_send.at[0],
        tail_recv.at[0],
        (after, f),
    )

    def set_out(k):
        for s, j in enumerate((f, far)):
            i = CHUNKS * s + k
            send(series_ref.at[halved(chip, k, s), :], hop.at[s, k], hop_send.at[i], hop_recv.at[i], (over, j))

    def hand_over(k):
        for s, j in enumerate((f, far)):
            i = CHUNKS * s + k
            receive(hop.at[s, k], hop_send.at[i], hop_recv.at[i], (over, j))
            c, to = (chip, far) if s == 0 else (1 - chip, f)
            send(hop.at[s, k], whole.at[halved(c, k, s), cols(j)], far_send.at[i], far_recv.at[i], (over, to))

            to, place = 2 * chip + k % 2, place_of(k)
            qi = lax.rem(core + k % 2, 2) + 2 * s
            spot = pl.ds(LEAD + place * quarter_rows, quarter_rows)

            def ride_back():
                post(
                    hop.at[s, k], nrows.at[spot, cols(j)], ride_send.at[i], n_recv.at[2 * qi + place // 2], (end, to)
                )

            def ride_on():
                at = pl.ds(LEAD + (place % 2) * quarter_rows, quarter_rows)
                rows_there = mrows if place < 2 else mrows_rest
                sem = m_recv.at[2 * qi + place] if place < 2 else rest_recv.at[6 + 2 * qi + place - 2]
                post(hop.at[s, k], rows_there.at[at, cols(j)], ride_send.at[i], sem, (near, to))

            when(is_near, ride_back)
            leaves(hop.at[s, k], ride_send.at[i], n_recv.at[0], is_near)
            when(is_end, ride_on)
            leaves(hop.at[s, k], ride_send.at[i], n_recv.at[0], is_end)

    for k in range(AHEAD):
        set_out(k)
    send(series_ref, whole.at[pl.ds(0, block), cols(f)], sib_send.at[0], sib_recv.at[0], (b, sib))
    send_n(series_ref, 0, slice(None), has_n)
    send_m(series_ref, 0, slice(None), has_m)
    send(inv_ref, ninv, inv_send.at[0], inv_recv.at[0], (before, f))
    send(inv_ref, minv, inv_send.at[1], inv_recv.at[1], (after, f))

    whole[pl.ds(0, block), cols(f)] = series_ref[...]
    whole[pl.ds(block, LANE - LEAD), :] = jnp.zeros((LANE - LEAD, dims), whole.dtype)
    for buffer in (gram, mgram, same_gram):
        buffer[pl.ds(0, 8), :] = jnp.zeros((8, wide), jnp.float32)

    def pass_on(k):
        for s in range(2):
            i = CHUNKS * s + k
            piece = whole.at[halved(1 - chip, k, s), cols(far)]
            receive(piece, far_send.at[i], far_recv.at[i], (over, far if s == 0 else f))
            send(piece, piece, pass_send.at[i], pass_recv.at[i], (b, sib))

    def passed(k):
        for s in range(2):
            i = CHUNKS * s + k
            piece = whole.at[halved(1 - chip, k, s), cols(cross)]
            receive(piece, pass_send.at[i], pass_recv.at[i], (b, sib))

    lead = multiple(lax.rem(f * share + wide - LEAD, wide), LEAD)
    near_half = pl.ds(multiple(chip * 2 * quarter, quarter), 2 * quarter)
    far_half = pl.ds(multiple((1 - chip) * 2 * quarter, quarter), 2 * quarter)
    leads = (near_half, far_half)
    lead_ways = ((nrows, before, after), (mrows, after, before))

    def post_lead(i):
        for w, (dst, to, _) in enumerate(lead_ways):
            s = 2 * w + i
            post(
                whole.at[pl.ds(lead, LEAD), leads[i]],
                dst.at[pl.ds(0, LEAD), leads[i]],
                lead_send.at[s],
                lead_recv.at[s],
                (to, f),
            )

    def receive_lead(w, i):
        dst, _, sender = lead_ways[w]
        receive(dst.at[pl.ds(0, LEAD), leads[i]], lead_send.at[2 * w + i], lead_recv.at[2 * w + i], (sender, f))

    lines = block // LANE

    def square_lines(lines_now):
        for j in lines_now:
            x = whole[pl.ds(j * LANE, LANE), cols(f)]
            total = jnp.zeros((LANE, LANE), jnp.float32)
            for g in range(quarter // LANE):
                piece = x[:, g * LANE : (g + 1) * LANE].astype(jnp.float32)
                total = total + piece * piece
            partial[pl.ds(f, 1), pl.ds(j, 1), :] = jnp.sum(total.T, axis=0, keepdims=True)[None]

    def share_squares():
        for i, j in enumerate(others):
            send(partial.at[f], partial.at[f], square_send.at[i], square_recv.at[i], (b, j))

    def sum_squares():
        for i, j in enumerate(others):
            receive(partial.at[j], square_send.at[i], square_recv.at[i], (b, j))
        squared[...] = partial[0] + partial[1] + partial[2] + partial[3]
        send(squared, past_squared, square_send.at[3], square_recv.at[3], (after, f))

    def lag_squares():
        receive(past_squared, square_send.at[3], square_recv.at[3], (before, f))
        line = [squared[j : j + 1, :] for j in range(lines)] + [past_squared[lines - 1 : lines, :]]
        norms[...] = lag_sum(jnp.broadcast_to(jnp.concatenate(line, axis=1), (8, wide)), 1)
        for j in range(lines):
            lagged[j : j + 1, :] = norms[0:1, j * LANE : (j + 1) * LANE]
        send(lagged, nlagged, square_send.at[4], square_recv.at[4], (before, f))
        send(lagged, mlagged, square_send.at[5], square_recv.at[5], (after, f))

    def lag_sum(x, axis):
        for step in (1, 2, 4):
            x = x + pltpu.roll(x, step, axis)
        return x + pltpu.roll(x, 8, axis) + pltpu.roll(x, 16, axis)

    def products(left, right):
        return lax.dot_general(left, right, CONTRACT_LAST, preferred_element_type=jnp.float32)

    def own_group(which):
        rows[pl.ds(0, LEAD), which] = whole[pl.ds(lead, LEAD), which]
        rows[pl.ds(LEAD, share), which] = whole[group(f), which]

    def add_products(target, source, which, fresh):
        size, height = 256, source.shape[0]
        for start in range(0, wide, size):
            part = pl.ds(start, min(size, wide - start))
            found = products(source[:, which], whole[part, which])
            if fresh:
                target[pl.ds(8, height), part] = found
            else:
                target[pl.ds(8, height), part] += found

    def near_products():
        for p in range(4):
            await_n(p)
        receive_lead(0, 0)
        add_products(gram, nrows, near_half, True)

    both = jnp.logical_and
    first_core, second_core = both(ordinary, core == 0), both(ordinary, core == 1)
    for k in range(CHUNKS):
        hand_over(k)
        if k + AHEAD < CHUNKS:
            set_out(k + AHEAD)
        if k == 0:
            receive(whole.at[pl.ds(0, block), cols(sib)], sib_send.at[0], sib_recv.at[0], (b, sib))
            send_n(whole, 1, cols(sib), has_n)
            send_m(whole, 1, cols(sib), has_m)
            tail = whole.at[pl.ds(past, LEAD), cols(f)]
            receive(tail, tail_send.at[0], tail_recv.at[0], (before, f))
            for i, j in enumerate(others):
                send(tail, tail, tail_send.at[1 + i], tail_recv.at[1 + i], (b, j))
            square_lines(range(lines // 2))
        else:
            pass_on(k - 1)
        if k == 1:
            square_lines(range(lines // 2, lines))
            share_squares()
        if k == 2:
            for i, j in enumerate(others):
                receive(whole.at[pl.ds(past, LEAD), cols(j)], tail_send.at[1 + i], tail_recv.at[1 + i], (b, j))
            post_lead(0)
            send_n(whole, 2, cols(far), first_core)
            send_m(whole, 2, cols(far), first_core)
            send_n_quarter(2, place_of(0), is_end)
            sum_squares()
        if k == 3:
            send_m(whole, 2, cols(far), second_core)
            passed(0)
            passed(1)
            send_n(whole, 3, cols(cross), first_core)
            send_m(whole, 3, cols(cross), first_core)
            send_n_quarter(3, place_of(0), is_end)
            when(is_seam, lambda: post_lead(1))
            lag_squares()
        if k == 4:
            send_n(whole, 2, cols(far), second_core)
            passed(2)
            send_m(whole, 3, cols(cross), second_core)
            send_n_quarter(2, place_of(2), is_end)
            send_m(whole, 2, cols(far), is_near, (0,))
            own_group(near_half)
            add_products(same_gram, rows, near_half, True)
        if k == 5:
            passed(3)
            send_n(whole, 3, cols(cross), second_core)
            send_n_quarter(3, place_of(2), is_end)
            send_m(whole, 3, cols(cross), is_near, (0,))
        if k == 6:
            send_n_quarter(2, place_of(4), is_end)
            send_m(whole, 2, cols(far), is_near, (1,))
            for p in range(4):
                await_m(p)
            receive_lead(1, 0)
            add_products(mgram, mrows, near_half, True)
        if k == 7:
            passed(4)
            passed(5)
            send_n_quarter(3, place_of(4), is_end)
            send_m(whole, 3, cols(cross), is_near, (1,))
            when(ordinary, lambda: post_lead(1))
            when(jnp.logical_not(is_end), near_products)
    pass_on(7)
    send_n_quarter(2, place_of(6), is_end)
    passed(6)
    passed(7)
    send_n_quarter(3, place_of(6), is_end)
    for i in range(2):
        for w in range(2):
            leaves(whole.at[pl.ds(lead, LEAD), leads[i]], lead_send.at[2 * w + i], lead_recv.at[2 * w + i])
    for p in range(8):
        leaves(n_spot(p), n_send.at[p], n_recv.at[p], has_n)
        leaves(m_spot(p), m_send.at[p], m_recv.at[p], has_m)
    when(is_end, near_products)

    inv_row = jnp.concatenate([inv_ref[j : j + 1, :] for j in range(block // LANE)], axis=1)
    width_row = jnp.full((1, LANE), width_ref[0], jnp.float32) * (LAGS * dims)

    def down(line):
        return jnp.broadcast_to(line, (LANE, LANE)).T

    def row_values(inv, squares, count, skip=0):
        for j in range(count // LANE):
            line, part = pl.ds(f * (share // LANE) + skip + j, 1), pl.ds(j * LANE, LANE)
            row_factor[part, :] = down(-inv[line, :] / width_row)
            row_norms[part, :] = down(squares[line, :])

    middle = block // 2

    def with_lead(ref, part, c):
        if c:
            return ref[part, middle - LANE : block]
        return jnp.concatenate([ref[part, block:wide], ref[part, :middle]], axis=1)

    def all_columns(c):
        return [(c * middle, middle)]

    def first_halves(c):
        return [(g * share, part_rows) for g in (2 * c, 2 * c + 1)]

    def second_halves(c):
        return [(g * share + part_rows, part_rows) for g in (2 * c, 2 * c + 1)]

    def tile(products_of, target, pick, parts, ready):
        per = target.shape[0] // 32 // parts
        span = target.shape[1] // 2
        for h in range(parts):
            for c in range(2):
                for t in range(h * per + 1 if h else 0, (h + 1) * per + 1):
                    x = with_lead(products_of, pl.ds(t * 32, 40), c)
                    for step in (1, 2, 4):
                        x = x + pltpu.roll(pltpu.roll(x, step, 0), step, 1)
                    part = pl.ds(t * 32, 32)
                    sums[part, c * middle : (c + 1) * middle] = x[8:, LANE:]
                    if c == 0:
                        sums[part, block:wide] = x[8:, :LANE]
                picked = lambda x, base: jnp.concatenate([x[:, s - base : s - base + n] for s, n in pick(c)], axis=1)
                for t in range(h * per, (h + 1) * per):
                    x = with_lead(sums, pl.ds(t * 32 + 32, 32), c)
                    x = x + pltpu.roll(with_lead(sums, pl.ds(t * 32 + 24, 32), c), 8, 1)
                    x = x + pltpu.roll(with_lead(sums, pl.ds(t * 32 + 16, 32), c), 16, 1)
                    part = pl.ds(t * 32, 32)
                    found = picked(x, c * middle - LANE)
                    spread = row_norms[part, :][:, :1] + picked(norms[pl.ds(0, 1), :], 0) - 2.0 * found
                    values = jnp.exp(spread * (row_factor[part, :][:, :1] * picked(inv_row, 0)))
                    target[part, c * span : (c + 1) * span] = values
            ready(h)

    receive(minv, inv_send.at[1], inv_recv.at[1], (before, f))
    receive(ninv, inv_send.at[0], inv_recv.at[0], (after, f))
    receive(nlagged, square_send.at[4], square_recv.at[4], (after, f))
    receive(mlagged, square_send.at[5], square_recv.at[5], (before, f))
    row_values(minv, mlagged, part_rows)
    for p in range(4, 8):
        await_m(p)
    receive_lead(1, 1)
    add_products(mgram, mrows, far_half, False)

    def send_mk(h):
        piece = mkept.at[pl.ds(h * (part_rows // PARTS), part_rows // PARTS), :]
        when(has_n, functools.partial(post, piece, mk_spot(h), mk_send.at[h], mk_recv.at[h], (before, f)))
        leaves(piece, mk_send.at[h], mk_recv.at[h], has_n)

    tile(mgram, mkept, all_columns, PARTS, send_mk)

    my_columns = pl.ds(multiple(f * share, share), share)
    my_first = pl.ds(multiple(f * share, part_rows), part_rows)
    lower = pl.ds(part_rows, part_rows)
    hops = ((0, far, f), (1, cross, far))

    def own_transposed(source):
        lines = [source[:, pl.ds(multiple(f * share + i * LANE, LANE), LANE)].T for i in range(share // LANE)]
        return jnp.concatenate(lines, axis=0)

    def turn_m(j):
        for i in range(share // LANE):
            part = pl.ds(multiple(j * share + i * LANE, LANE), LANE)
            mturned[part, :] = mkept[:, part].T

    for s, j, by in hops:
        turn_m(j)
        send(mturned.at[group(j), :], mturn_hop.at[s], turn_hop_send.at[2 + s], turn_hop_recv.at[2 + s], (over, by))
    turn_m(sib)
    send(mturned.at[group(sib), :], prev_ref.at[:, my_first], turn_send.at[5], turn_recv.at[5], (b, sib))
    prev_ref[:, my_first] = own_transposed(mkept)

    row_values(ninv, nlagged, share)
    for p in range(4, 8):
        await_n(p)
    receive_lead(0, 1)
    add_products(gram, nrows, far_half, False)

    def send_k(h):
        for g in range(4):
            piece, p = kept.at[pl.ds(h * part_rows, part_rows), pl.ds(g * part_rows, part_rows)], 4 * h + g
            when(has_m, functools.partial(post, piece, k_spot(p), k_send.at[p], k_recv.at[p], (after, f)))
            leaves(piece, k_send.at[p], k_recv.at[p], has_m)

    tile(gram, kept, second_halves, PARTS, send_k)

    def seconds(j):
        return pl.ds(multiple(j * part_rows, part_rows), part_rows)

    def turn(j):
        turned[seconds(j), :] = kept[:, seconds(j)].T

    for s, j, by in hops:
        turn(j)
        send(turned.at[seconds(j), :], turn_hop.at[s], turn_hop_send.at[s], turn_hop_recv.at[s], (over, by))
    turn(sib)
    send(turned.at[seconds(sib), :], next_ref.at[lower, my_columns], turn_send.at[2], turn_recv.at[2], (b, sib))
    next_ref[lower, my_columns] = kept[:, seconds(f)].T

    def firsts_of(j):
        return pl.ds(multiple(j * share, part_rows), part_rows)

    upper = pl.ds(0, part_rows)

    def rest_of_next():
        tile(gram, kept_rest, first_halves, 1, lambda h: None)
        for s, j, by in hops:
            turned_rest[seconds(j), :] = kept_rest[:, seconds(j)].T
            post(turned_rest.at[seconds(j), :], rest_hop.at[s], rest_hop_send.at[s], rest_hop_recv.at[s], (over, by))
        turned_rest[seconds(sib), :] = kept_rest[:, seconds(sib)].T
        post(
            turned_rest.at[seconds(sib), :],
            next_ref.at[upper, my_columns],
            rest_send.at[2],
            rest_recv.at[2],
            (b, sib),
        )
        next_ref[upper, my_columns] = kept_rest[:, seconds(f)].T

    def relay_rest_of_next():
        for s, j, to in ((0, f, far), (1, far, sib)):
            receive(rest_hop.at[s], rest_hop_send.at[s], rest_hop_recv.at[s], (over, j))
            post(rest_hop.at[s], next_ref.at[upper, group(j)], rest_send.at[s], rest_recv.at[s], (over, to))

    def rest_of_prev():
        for qi in range(4):
            for i in range(2):
                sem = 6 + 2 * qi + i
                spot = mrows_rest.at[pl.ds(LEAD + i * quarter_rows, quarter_rows), cols(everyone[qi])]
                receive(spot, rest_send.at[sem], rest_recv.at[sem], (before, f))
        mrows_rest[pl.ds(0, LEAD), :] = mrows[pl.ds(part_rows, LEAD), :]
        add_products(mgram, mrows_rest, slice(None), True)
        row_values(minv, mlagged, part_rows, 1)
        tile(mgram, mkept_rest, all_columns, 1, lambda h: None)
        for s, j, by in hops:
            turn_rest(j)
            post(mturned_rest.at[group(j), :], mrest_hop.at[s], rest_hop_send.at[s], rest_hop_recv.at[s], (over, by))
        turn_rest(sib)
        post(mturned_rest.at[group(sib), :], prev_ref.at[:, my_second], rest_send.at[5], rest_recv.at[5], (b, sib))
        prev_ref[:, my_second] = own_transposed(mkept_rest)

    def relay_rest_of_prev():
        for s, j, to in ((0, f, far), (1, far, sib)):
            receive(mrest_hop.at[s], rest_hop_send.at[s], rest_hop_recv.at[s], (over, j))
            post(mrest_hop.at[s], prev_ref.at[:, seconds_of(j)], rest_send.at[3 + s], rest_recv.at[3 + s], (over, to))

    def turn_rest(j):
        for i in range(share // LANE):
            part = pl.ds(multiple(j * share + i * LANE, LANE), LANE)
            mturned_rest[part, :] = mkept_rest[:, part].T

    def seconds_of(j):
        return pl.ds(multiple(j * share + part_rows, part_rows), part_rows)

    my_second = seconds_of(f)
    for s, j, to in ((0, f, far), (1, far, sib)):
        receive(mturn_hop.at[s], turn_hop_send.at[2 + s], turn_hop_recv.at[2 + s], (over, j))
        send(mturn_hop.at[s], prev_ref.at[:, firsts_of(j)], turn_send.at[3 + s], turn_recv.at[3 + s], (over, to))

    when(is_end, rest_of_next)
    when(is_near, rest_of_prev)

    own_group(far_half)
    add_products(same_gram, rows, far_half, False)
    row_values(inv_ref, lagged, share)

    def between(h):
        if h == 0:
            for s, j, to in ((0, f, far), (1, far, sib)):
                receive(turn_hop.at[s], turn_hop_send.at[s], turn_hop_recv.at[s], (over, j))
                send(turn_hop.at[s], next_ref.at[lower, group(j)], turn_send.at[s], turn_recv.at[s], (over, to))
            when(is_end, relay_rest_of_next)
            when(is_near, relay_rest_of_prev)

    tile(same_gram, same_ref, all_columns, PARTS, between)

    def await_mk():
        for p in range(PARTS):
            receive(mk_spot(p), mk_send.at[p], mk_recv.at[p], (after, f))

    def await_k():
        for p in range(4 * PARTS):
            receive(k_spot(p), k_send.at[p], k_recv.at[p], (before, f))

    when(has_m, await_mk)
    when(has_n, await_k)

    def await_rest(i, dst, source):
        receive(dst, rest_send.at[i], rest_recv.at[i], (b, source))

    for i, j in enumerate((far, cross, sib)):
        when(is_end, functools.partial(await_rest, i, next_ref.at[upper, group(j)], j))
        when(is_near, functools.partial(await_rest, 3 + i, prev_ref.at[:, seconds_of(j)], j))
    for s in range(2):
        leaves(rest_hop.at[s], rest_hop_send.at[s], rest_hop_recv.at[s], is_seam)
        leaves(rest_hop.at[s], rest_send.at[s], rest_recv.at[s], is_end)
        leaves(mrest_hop.at[s], rest_send.at[3 + s], rest_recv.at[3 + s], is_near)
    leaves(turned_rest.at[seconds(sib), :], rest_send.at[2], rest_recv.at[2], is_end)
    leaves(mturned_rest.at[group(sib), :], rest_send.at[5], rest_recv.at[5], is_near)
    for i, j in enumerate((far, cross, sib)):
        receive(next_ref.at[lower, group(j)], turn_send.at[i], turn_recv.at[i], (b, j))
        receive(prev_ref.at[:, firsts_of(j)], turn_send.at[3 + i], turn_recv.at[3 + i], (b, j))
    for condition, copy in sent:
        if condition is None:
            copy.wait_send()
        else:
            when(condition, copy.wait_send)


def settle(*refs):
    sems = refs[-1]
    copies = [pltpu.make_async_copy(refs[i], refs[3 + i], sems.at[i]) for i in range(3)]
    for copy in copies:
        copy.start()
    for copy in copies:
        copy.wait()


def per_device(blocks, series, scales, width):
    block, quarter = series.shape
    dims, share, wide = 4 * quarter, block // 4, block + LANE
    part_rows = share // 2
    inv = (1.0 / scales.astype(jnp.float32)).reshape(block // LANE, LANE)
    out = jax.ShapeDtypeStruct((share, block), jnp.float32)
    raw = lambda *shape: pltpu.VMEM(shape, series.dtype)
    wider = lambda *shape: pltpu.VMEM(shape, jnp.float32)
    hops = 2 * CHUNKS
    pairs = (4, 1, hops, hops, hops, 4, 2, 6, 6, 4, 14, 2, PIECES, PIECES, 4 * PARTS, PARTS)
    counts = [n for n in pairs for _ in range(2)] + [hops]
    tiles = pl.pallas_call(
        functools.partial(tiles_kernel, blocks),
        out_shape=(out, out, out),
        in_specs=[
            pl.BlockSpec(memory_space=pltpu.VMEM),
            pl.BlockSpec(memory_space=pltpu.VMEM),
            pl.BlockSpec(memory_space=pltpu.SMEM),
        ],
        out_specs=(pl.BlockSpec(memory_space=pltpu.VMEM),) * 3,
        scratch_shapes=[
            raw(wide, dims),
            raw(LEAD + share, dims),
            raw(LEAD + share, dims),
            raw(LEAD + part_rows, dims),
            raw(LEAD + part_rows, dims),
            wider(block // LANE, LANE),
            wider(block // LANE, LANE),
            wider(8 + LEAD + share, wide),
            wider(8 + LEAD + part_rows, wide),
            wider(8 + LEAD + share, wide),
            wider(LEAD + share, wide),
            wider(4, block // LANE, LANE),
        ]
        + [wider(block // LANE, LANE)] * 5
        + [
            wider(8, wide),
            wider(share, LANE),
            wider(share, LANE),
            wider(share, block // 2),
            wider(part_rows, block),
            wider(block // 2, share),
            wider(block, part_rows),
            wider(share, block // 2),
            wider(part_rows, block),
            wider(block // 2, share),
            wider(block, part_rows),
            raw(2, CHUNKS, 2 * share // CHUNKS, quarter),
            wider(2, part_rows, share),
            wider(2, share, part_rows),
            wider(2, part_rows, share),
            wider(2, share, part_rows),
        ]
        + [pltpu.SemaphoreType.DMA((n,)) for n in counts],
        compiler_params=pltpu.CompilerParams(
            collective_id=0, has_side_effects=True, vmem_limit_bytes=48 * 1024 * 1024
        ),
    )(series, inv, width)
    return pl.pallas_call(
        settle,
        out_shape=(out, out, out),
        in_specs=[pl.BlockSpec(memory_space=pltpu.VMEM)] * 3,
        out_specs=(pl.BlockSpec(memory_space=pltpu.HBM),) * 3,
        scratch_shapes=[pltpu.SemaphoreType.DMA((3,))],
    )(*tiles)


def solution(mesh):
    in_specs = (P("blk", "feat"), P("blk"), P())
    out_specs = (P(("blk", "feat"), None), P(("blk", "feat"), None), P(("blk", "feat"), None))
    return jax.shard_map(
        functools.partial(per_device, mesh.shape["blk"]),
        mesh=mesh,
        in_specs=in_specs,
        out_specs=out_specs,
        check_vma=False,
    )
```

```python
import functools

import jax
import jax.numpy as jnp
from jax import lax
from jax.experimental import pallas as pl
from jax.experimental.pallas import tpu as pltpu
from jax.sharding import PartitionSpec as P

LAGS = 24
LEAD = 32
LANE = 128
CHUNKS = 8
PIECES = 8
PARTS = 2
MESH = pl.DeviceIdType.MESH
CONTRACT_LAST = (((1,), (1,)), ((), ()))


def multiple(value, of):
    return pl.multiple_of(value, of)


def tiles_kernel(
    blocks,
    series_ref,
    inv_ref,
    width_ref,
    same_ref,
    next_ref,
    prev_ref,
    whole,
    rows,
    nrows,
    mrows,
    mrows_rest,
    ninv,
    minv,
    gram,
    mgram,
    same_gram,
    sums,
    partial,
    squared,
    past_squared,
    lagged,
    nlagged,
    mlagged,
    norms,
    row_norms,
    row_factor,
    kept,
    mkept,
    turned,
    mturned,
    kept_rest,
    mkept_rest,
    turned_rest,
    mturned_rest,
    hop,
    turn_hop,
    mturn_hop,
    rest_hop,
    mrest_hop,
    tail_send,
    tail_recv,
    sib_send,
    sib_recv,
    hop_send,
    hop_recv,
    far_send,
    far_recv,
    pass_send,
    pass_recv,
    lead_send,
    lead_recv,
    inv_send,
    inv_recv,
    square_send,
    square_recv,
    turn_send,
    turn_recv,
    turn_hop_send,
    turn_hop_recv,
    rest_send,
    rest_recv,
    rest_hop_send,
    rest_hop_recv,
    n_send,
    n_recv,
    m_send,
    m_recv,
    k_send,
    k_recv,
    mk_send,
    mk_recv,
    ride_send,
):
    block, quarter = series_ref.shape
    dims = 4 * quarter
    share = block // 4
    part_rows = share // 2
    wide = block + LANE
    past = wide - LEAD

    b, f = lax.axis_index("blk"), lax.axis_index("feat")
    core, chip = lax.rem(f, 2), f // 2
    sib, far, cross = f + 1 - 2 * core, lax.rem(f + 2, 4), 3 - f
    after, before = lax.rem(b + 1, blocks), lax.rem(b + blocks - 1, blocks)
    half = blocks // 2
    pos, first = lax.rem(b, half), (b // half) * half
    over = lax.rem(b + half, blocks)
    others = (sib, far, cross)
    everyone = (f, sib, far, cross)
    near, end = first, first + half - 1
    is_near, is_end = pos == 0, pos == half - 1
    is_seam = jnp.logical_or(is_near, is_end)
    ordinary = jnp.logical_not(is_seam)

    barrier = pltpu.get_barrier_semaphore()
    peers = [(b, j) for j in others] + [(after, f), (before, f)] + [(over, j) for j in (f, far, sib)]
    for peer in peers:
        pl.semaphore_signal(barrier, inc=1, device_id=peer, device_id_type=MESH)

    def greet(condition, corners):
        @pl.when(condition)
        def _():
            for corner in corners:
                pl.semaphore_signal(barrier, inc=1, device_id=corner, device_id_type=MESH)
            pl.semaphore_wait(barrier, len(peers) + len(corners))

    greet(is_near, [(end, f), (end, sib)])
    greet(is_end, [(near, f), (near, sib)])

    @pl.when(ordinary)
    def _():
        pl.semaphore_wait(barrier, len(peers))

    sent = []

    def copy_of(src, dst, send_sem, recv_sem, to):
        return pltpu.make_async_remote_copy(
            src_ref=src, dst_ref=dst, send_sem=send_sem, recv_sem=recv_sem, device_id=to, device_id_type=MESH
        )

    def post(src, dst, send_sem, recv_sem, to):
        copy_of(src, dst, send_sem, recv_sem, to).start()

    def leaves(src, send_sem, recv_sem, condition=None):
        sent.append((condition, copy_of(src, src, send_sem, recv_sem, (b, sib))))

    def send(src, dst, send_sem, recv_sem, to):
        post(src, dst, send_sem, recv_sem, to)
        leaves(src, send_sem, recv_sem)

    def receive(dst, send_sem, recv_sem, sender):
        copy_of(dst, dst, send_sem, recv_sem, sender).wait_recv()

    def when(condition, act):
        @pl.when(condition)
        def _():
            act()

    def cols(q):
        return pl.ds(multiple(q * quarter, quarter), quarter)

    def group(g):
        return pl.ds(multiple(g * share, share), share)

    def n_spot(p):
        return nrows.at[pl.ds(LEAD + (p % 2) * part_rows, part_rows), cols(everyone[p // 2])]

    def m_spot(p):
        size = part_rows // 2
        return mrows.at[pl.ds(LEAD + (p % 2) * size, size), cols(everyone[p // 2])]

    def k_spot(p):
        g, h = p % 4, p // 4
        return prev_ref.at[pl.ds(h * part_rows, part_rows), pl.ds(g * share + part_rows, part_rows)]

    def mk_spot(p):
        size = part_rows // PARTS
        return next_ref.at[pl.ds(p * size, size), :]

    quarter_rows = share // 4

    def own_rows(ref, start, size, columns):
        return ref.at[pl.ds(multiple(f * share + start, size), size), columns]

    def send_n(ref, qi, columns, condition):
        for p in (2 * qi, 2 * qi + 1):
            piece = own_rows(ref, (p % 2) * part_rows, part_rows, columns)
            when(condition, functools.partial(post, piece, n_spot(p), n_send.at[p], n_recv.at[p], (before, f)))

    def send_n_quarter(qi, i, condition):
        p, columns = 2 * qi + i // 2, cols(everyone[qi])
        piece = own_rows(whole, i * quarter_rows, quarter_rows, columns)
        spot = nrows.at[pl.ds(LEAD + i * quarter_rows, quarter_rows), columns]
        when(condition, functools.partial(post, piece, spot, n_send.at[p], n_recv.at[p], (before, f)))

    def send_m(ref, qi, columns, condition, pieces=(0, 1)):
        for i in pieces:
            p = 2 * qi + i
            piece = own_rows(ref, i * quarter_rows, quarter_rows, columns)
            when(condition, functools.partial(post, piece, m_spot(p), m_send.at[p], m_recv.at[p], (after, f)))

    def await_n(p):
        receive(n_spot(p), n_send.at[p], n_recv.at[p], (after, f))

    def await_m(p):
        receive(m_spot(p), m_send.at[p], m_recv.at[p], (before, f))

    has_n, has_m = jnp.logical_not(is_near), jnp.logical_not(is_end)

    def order(c, j):
        return j + c * (2, 2, -1, -3)[j]

    def place_of(k):
        return (k // 2 + 3) % 4

    def halved(sender, k, s):
        c = sender if s == 0 else 1 - sender
        usual = order(1 - sender, k // 2) * share + (k % 2) * 2 * quarter_rows + s * quarter_rows
        at_seam = (2 * c + k % 2) * share + place_of(k) * quarter_rows
        return pl.ds(multiple(jnp.where(is_seam, at_seam, usual), quarter_rows), quarter_rows)

    send(
        series_ref.at[pl.ds(block - LEAD, LEAD), :],
        whole.at[pl.ds(past, LEAD), cols(f)],
        tail_send.at[0],
        tail_recv.at[0],
        (after, f),
    )

    def set_out(k):
        for s, j in enumerate((f, far)):
            i = CHUNKS * s + k
            send(series_ref.at[halved(chip, k, s), :], hop.at[s, k], hop_send.at[i], hop_recv.at[i], (over, j))

    def hand_over(k):
        for s, j in enumerate((f, far)):
            i = CHUNKS * s + k
            receive(hop.at[s, k], hop_send.at[i], hop_recv.at[i], (over, j))
            c, to = (chip, far) if s == 0 else (1 - chip, f)
            send(hop.at[s, k], whole.at[halved(c, k, s), cols(j)], far_send.at[i], far_recv.at[i], (over, to))

            to, place = 2 * chip + k % 2, place_of(k)
            qi = lax.rem(core + k % 2, 2) + 2 * s
            spot = pl.ds(LEAD + place * quarter_rows, quarter_rows)

            def ride_back():
                post(
                    hop.at[s, k], nrows.at[spot, cols(j)], ride_send.at[i], n_recv.at[2 * qi + place // 2], (end, to)
                )

            def ride_on():
                at = pl.ds(LEAD + (place % 2) * quarter_rows, quarter_rows)
                rows_there = mrows if place < 2 else mrows_rest
                sem = m_recv.at[2 * qi + place] if place < 2 else rest_recv.at[6 + 2 * qi + place - 2]
                post(hop.at[s, k], rows_there.at[at, cols(j)], ride_send.at[i], sem, (near, to))

            when(is_near, ride_back)
            leaves(hop.at[s, k], ride_send.at[i], n_recv.at[0], is_near)
            when(is_end, ride_on)
            leaves(hop.at[s, k], ride_send.at[i], n_recv.at[0], is_end)

    set_out(0)
    set_out(1)
    send(series_ref, whole.at[pl.ds(0, block), cols(f)], sib_send.at[0], sib_recv.at[0], (b, sib))
    send_n(series_ref, 0, slice(None), has_n)
    send_m(series_ref, 0, slice(None), has_m)
    send(inv_ref, ninv, inv_send.at[0], inv_recv.at[0], (before, f))
    send(inv_ref, minv, inv_send.at[1], inv_recv.at[1], (after, f))

    whole[pl.ds(0, block), cols(f)] = series_ref[...]
    whole[pl.ds(block, LANE - LEAD), :] = jnp.zeros((LANE - LEAD, dims), whole.dtype)
    for buffer in (gram, mgram, same_gram):
        buffer[pl.ds(0, 8), :] = jnp.zeros((8, wide), jnp.float32)

    def pass_on(k):
        for s in range(2):
            i = CHUNKS * s + k
            piece = whole.at[halved(1 - chip, k, s), cols(far)]
            receive(piece, far_send.at[i], far_recv.at[i], (over, far if s == 0 else f))
            send(piece, piece, pass_send.at[i], pass_recv.at[i], (b, sib))

    def passed(k):
        for s in range(2):
            i = CHUNKS * s + k
            piece = whole.at[halved(1 - chip, k, s), cols(cross)]
            receive(piece, pass_send.at[i], pass_recv.at[i], (b, sib))

    lead = multiple(lax.rem(f * share + wide - LEAD, wide), LEAD)
    near_half = pl.ds(multiple(chip * 2 * quarter, quarter), 2 * quarter)
    far_half = pl.ds(multiple((1 - chip) * 2 * quarter, quarter), 2 * quarter)
    leads = (near_half, far_half)
    lead_ways = ((nrows, before, after), (mrows, after, before))

    def post_lead(i):
        for w, (dst, to, _) in enumerate(lead_ways):
            s = 2 * w + i
            post(
                whole.at[pl.ds(lead, LEAD), leads[i]],
                dst.at[pl.ds(0, LEAD), leads[i]],
                lead_send.at[s],
                lead_recv.at[s],
                (to, f),
            )

    def receive_lead(w, i):
        dst, _, sender = lead_ways[w]
        receive(dst.at[pl.ds(0, LEAD), leads[i]], lead_send.at[2 * w + i], lead_recv.at[2 * w + i], (sender, f))

    lines = block // LANE

    def square_lines(lines_now):
        for j in lines_now:
            x = whole[pl.ds(j * LANE, LANE), cols(f)]
            total = jnp.zeros((LANE, LANE), jnp.float32)
            for g in range(quarter // LANE):
                piece = x[:, g * LANE : (g + 1) * LANE].astype(jnp.float32)
                total = total + piece * piece
            partial[pl.ds(f, 1), pl.ds(j, 1), :] = jnp.sum(total.T, axis=0, keepdims=True)[None]

    def share_squares():
        for i, j in enumerate(others):
            send(partial.at[f], partial.at[f], square_send.at[i], square_recv.at[i], (b, j))

    def sum_squares():
        for i, j in enumerate(others):
            receive(partial.at[j], square_send.at[i], square_recv.at[i], (b, j))
        squared[...] = partial[0] + partial[1] + partial[2] + partial[3]
        send(squared, past_squared, square_send.at[3], square_recv.at[3], (after, f))

    def lag_squares():
        receive(past_squared, square_send.at[3], square_recv.at[3], (before, f))
        line = [squared[j : j + 1, :] for j in range(lines)] + [past_squared[lines - 1 : lines, :]]
        norms[...] = lag_sum(jnp.broadcast_to(jnp.concatenate(line, axis=1), (8, wide)), 1)
        for j in range(lines):
            lagged[j : j + 1, :] = norms[0:1, j * LANE : (j + 1) * LANE]
        send(lagged, nlagged, square_send.at[4], square_recv.at[4], (before, f))
        send(lagged, mlagged, square_send.at[5], square_recv.at[5], (after, f))

    def lag_sum(x, axis):
        for step in (1, 2, 4):
            x = x + pltpu.roll(x, step, axis)
        return x + pltpu.roll(x, 8, axis) + pltpu.roll(x, 16, axis)

    def products(left, right):
        return lax.dot_general(left, right, CONTRACT_LAST, preferred_element_type=jnp.float32)

    def own_group(which):
        rows[pl.ds(0, LEAD), which] = whole[pl.ds(lead, LEAD), which]
        rows[pl.ds(LEAD, share), which] = whole[group(f), which]

    def add_products(target, source, which, fresh):
        size, height = 256, source.shape[0]
        for start in range(0, wide, size):
            part = pl.ds(start, min(size, wide - start))
            found = products(source[:, which], whole[part, which])
            if fresh:
                target[pl.ds(8, height), part] = found
            else:
                target[pl.ds(8, height), part] += found

    def near_products():
        for p in range(4):
            await_n(p)
        receive_lead(0, 0)
        add_products(gram, nrows, near_half, True)

    both = jnp.logical_and
    first_core, second_core = both(ordinary, core == 0), both(ordinary, core == 1)
    for k in range(CHUNKS):
        hand_over(k)
        if k + 2 < CHUNKS:
            set_out(k + 2)
        if k == 0:
            receive(whole.at[pl.ds(0, block), cols(sib)], sib_send.at[0], sib_recv.at[0], (b, sib))
            send_n(whole, 1, cols(sib), has_n)
            send_m(whole, 1, cols(sib), has_m)
            tail = whole.at[pl.ds(past, LEAD), cols(f)]
            receive(tail, tail_send.at[0], tail_recv.at[0], (before, f))
            for i, j in enumerate(others):
                send(tail, tail, tail_send.at[1 + i], tail_recv.at[1 + i], (b, j))
            square_lines(range(lines // 2))
        else:
            pass_on(k - 1)
        if k == 1:
            square_lines(range(lines // 2, lines))
            share_squares()
        if k == 2:
            for i, j in enumerate(others):
                receive(whole.at[pl.ds(past, LEAD), cols(j)], tail_send.at[1 + i], tail_recv.at[1 + i], (b, j))
            post_lead(0)
            send_n(whole, 2, cols(far), first_core)
            send_m(whole, 2, cols(far), first_core)
            send_n_quarter(2, place_of(0), is_end)
            sum_squares()
        if k == 3:
            send_m(whole, 2, cols(far), second_core)
            passed(0)
            passed(1)
            send_n(whole, 3, cols(cross), first_core)
            send_m(whole, 3, cols(cross), first_core)
            send_n_quarter(3, place_of(0), is_end)
            when(is_seam, lambda: post_lead(1))
            lag_squares()
        if k == 4:
            send_n(whole, 2, cols(far), second_core)
            passed(2)
            send_m(whole, 3, cols(cross), second_core)
            send_n_quarter(2, place_of(2), is_end)
            send_m(whole, 2, cols(far), is_near, (0,))
        if k == 5:
            passed(3)
            send_n(whole, 3, cols(cross), second_core)
            send_n_quarter(3, place_of(2), is_end)
            send_m(whole, 3, cols(cross), is_near, (0,))
            own_group(near_half)
            add_products(same_gram, rows, near_half, True)
        if k == 6:
            send_n_quarter(2, place_of(4), is_end)
            send_m(whole, 2, cols(far), is_near, (1,))
            for p in range(4):
                await_m(p)
            receive_lead(1, 0)
            add_products(mgram, mrows, near_half, True)
        if k == 7:
            passed(4)
            passed(5)
            send_n_quarter(3, place_of(4), is_end)
            send_m(whole, 3, cols(cross), is_near, (1,))
            when(ordinary, lambda: post_lead(1))
            when(jnp.logical_not(is_end), near_products)
    pass_on(7)
    send_n_quarter(2, place_of(6), is_end)
    passed(6)
    passed(7)
    send_n_quarter(3, place_of(6), is_end)
    for i in range(2):
        for w in range(2):
            leaves(whole.at[pl.ds(lead, LEAD), leads[i]], lead_send.at[2 * w + i], lead_recv.at[2 * w + i])
    for p in range(8):
        leaves(n_spot(p), n_send.at[p], n_recv.at[p], has_n)
        leaves(m_spot(p), m_send.at[p], m_recv.at[p], has_m)
    when(is_end, near_products)

    inv_row = jnp.concatenate([inv_ref[j : j + 1, :] for j in range(block // LANE)], axis=1)
    width_row = jnp.full((1, LANE), width_ref[0], jnp.float32) * (LAGS * dims)

    def down(line):
        return jnp.broadcast_to(line, (LANE, LANE)).T

    def row_values(inv, squares, count, skip=0):
        for j in range(count // LANE):
            line, part = pl.ds(f * (share // LANE) + skip + j, 1), pl.ds(j * LANE, LANE)
            row_factor[part, :] = down(-inv[line, :] / width_row)
            row_norms[part, :] = down(squares[line, :])

    middle = block // 2

    def with_lead(ref, part, c):
        if c:
            return ref[part, middle - LANE : block]
        return jnp.concatenate([ref[part, block:wide], ref[part, :middle]], axis=1)

    def all_columns(c):
        return [(c * middle, middle)]

    def first_halves(c):
        return [(g * share, part_rows) for g in (2 * c, 2 * c + 1)]

    def second_halves(c):
        return [(g * share + part_rows, part_rows) for g in (2 * c, 2 * c + 1)]

    def tile(products_of, target, pick, parts, ready, summed=False):
        per = target.shape[0] // 32 // parts
        span = target.shape[1] // 2
        for h in range(parts):
            for c in range(2):
                for t in () if summed else range(h * per + 1 if h else 0, (h + 1) * per + 1):
                    x = with_lead(products_of, pl.ds(t * 32, 40), c)
                    for step in (1, 2, 4):
                        x = x + pltpu.roll(pltpu.roll(x, step, 0), step, 1)
                    part = pl.ds(t * 32, 32)
                    sums[part, c * middle : (c + 1) * middle] = x[8:, LANE:]
                    if c == 0:
                        sums[part, block:wide] = x[8:, :LANE]
                picked = lambda x, base: jnp.concatenate([x[:, s - base : s - base + n] for s, n in pick(c)], axis=1)
                for t in range(h * per, (h + 1) * per):
                    x = with_lead(sums, pl.ds(t * 32 + 32, 32), c)
                    x = x + pltpu.roll(with_lead(sums, pl.ds(t * 32 + 24, 32), c), 8, 1)
                    x = x + pltpu.roll(with_lead(sums, pl.ds(t * 32 + 16, 32), c), 16, 1)
                    part = pl.ds(t * 32, 32)
                    found = picked(x, c * middle - LANE)
                    spread = row_norms[part, :][:, :1] + picked(norms[pl.ds(0, 1), :], 0) - 2.0 * found
                    values = jnp.exp(spread * (row_factor[part, :][:, :1] * picked(inv_row, 0)))
                    target[part, c * span : (c + 1) * span] = values
            ready(h)

    receive(minv, inv_send.at[1], inv_recv.at[1], (before, f))
    receive(ninv, inv_send.at[0], inv_recv.at[0], (after, f))
    receive(nlagged, square_send.at[4], square_recv.at[4], (after, f))
    receive(mlagged, square_send.at[5], square_recv.at[5], (before, f))
    row_values(minv, mlagged, part_rows)
    for p in range(4, 8):
        await_m(p)
    receive_lead(1, 1)
    add_products(mgram, mrows, far_half, False)

    def send_mk(h):
        piece = mkept.at[pl.ds(h * (part_rows // PARTS), part_rows // PARTS), :]
        when(has_n, functools.partial(post, piece, mk_spot(h), mk_send.at[h], mk_recv.at[h], (before, f)))
        leaves(piece, mk_send.at[h], mk_recv.at[h], has_n)

    tile(mgram, mkept, all_columns, PARTS, send_mk)

    my_columns = pl.ds(multiple(f * share, share), share)
    my_first = pl.ds(multiple(f * share, part_rows), part_rows)
    lower = pl.ds(part_rows, part_rows)
    hops = ((0, far, f), (1, cross, far))

    def own_transposed(source):
        lines = [source[:, pl.ds(multiple(f * share + i * LANE, LANE), LANE)].T for i in range(share // LANE)]
        return jnp.concatenate(lines, axis=0)

    def turn_m(j):
        for i in range(share // LANE):
            part = pl.ds(multiple(j * share + i * LANE, LANE), LANE)
            mturned[part, :] = mkept[:, part].T

    for s, j, by in hops:
        turn_m(j)
        send(mturned.at[group(j), :], mturn_hop.at[s], turn_hop_send.at[2 + s], turn_hop_recv.at[2 + s], (over, by))
    turn_m(sib)
    send(mturned.at[group(sib), :], prev_ref.at[:, my_first], turn_send.at[5], turn_recv.at[5], (b, sib))
    prev_ref[:, my_first] = own_transposed(mkept)

    row_values(ninv, nlagged, share)
    for p in range(4, 8):
        await_n(p)
    receive_lead(0, 1)
    add_products(gram, nrows, far_half, False)

    def send_k(h):
        for g in range(4):
            piece, p = kept.at[pl.ds(h * part_rows, part_rows), pl.ds(g * part_rows, part_rows)], 4 * h + g
            when(has_m, functools.partial(post, piece, k_spot(p), k_send.at[p], k_recv.at[p], (after, f)))
            leaves(piece, k_send.at[p], k_recv.at[p], has_m)

    tile(gram, kept, second_halves, PARTS, send_k)

    def seconds(j):
        return pl.ds(multiple(j * part_rows, part_rows), part_rows)

    def turn(j):
        turned[seconds(j), :] = kept[:, seconds(j)].T

    for s, j, by in hops:
        turn(j)
        send(turned.at[seconds(j), :], turn_hop.at[s], turn_hop_send.at[s], turn_hop_recv.at[s], (over, by))
    turn(sib)
    send(turned.at[seconds(sib), :], next_ref.at[lower, my_columns], turn_send.at[2], turn_recv.at[2], (b, sib))
    next_ref[lower, my_columns] = kept[:, seconds(f)].T

    def firsts_of(j):
        return pl.ds(multiple(j * share, part_rows), part_rows)

    upper = pl.ds(0, part_rows)

    def rest_of_next():
        tile(gram, kept_rest, first_halves, 1, lambda h: None, summed=True)
        for s, j, by in hops:
            turned_rest[seconds(j), :] = kept_rest[:, seconds(j)].T
            post(turned_rest.at[seconds(j), :], rest_hop.at[s], rest_hop_send.at[s], rest_hop_recv.at[s], (over, by))
        turned_rest[seconds(sib), :] = kept_rest[:, seconds(sib)].T
        post(
            turned_rest.at[seconds(sib), :],
            next_ref.at[upper, my_columns],
            rest_send.at[2],
            rest_recv.at[2],
            (b, sib),
        )
        next_ref[upper, my_columns] = kept_rest[:, seconds(f)].T

    def relay_rest_of_next():
        for s, j, to in ((0, f, far), (1, far, sib)):
            receive(rest_hop.at[s], rest_hop_send.at[s], rest_hop_recv.at[s], (over, j))
            post(rest_hop.at[s], next_ref.at[upper, group(j)], rest_send.at[s], rest_recv.at[s], (over, to))

    def rest_of_prev():
        for qi in range(4):
            for i in range(2):
                sem = 6 + 2 * qi + i
                spot = mrows_rest.at[pl.ds(LEAD + i * quarter_rows, quarter_rows), cols(everyone[qi])]
                receive(spot, rest_send.at[sem], rest_recv.at[sem], (before, f))
        mrows_rest[pl.ds(0, LEAD), :] = mrows[pl.ds(part_rows, LEAD), :]
        add_products(mgram, mrows_rest, slice(None), True)
        row_values(minv, mlagged, part_rows, 1)
        tile(mgram, mkept_rest, all_columns, 1, lambda h: None)
        for s, j, by in hops:
            turn_rest(j)
            post(mturned_rest.at[group(j), :], mrest_hop.at[s], rest_hop_send.at[s], rest_hop_recv.at[s], (over, by))
        turn_rest(sib)
        post(mturned_rest.at[group(sib), :], prev_ref.at[:, my_second], rest_send.at[5], rest_recv.at[5], (b, sib))
        prev_ref[:, my_second] = own_transposed(mkept_rest)

    def relay_rest_of_prev():
        for s, j, to in ((0, f, far), (1, far, sib)):
            receive(mrest_hop.at[s], rest_hop_send.at[s], rest_hop_recv.at[s], (over, j))
            post(mrest_hop.at[s], prev_ref.at[:, seconds_of(j)], rest_send.at[3 + s], rest_recv.at[3 + s], (over, to))

    def turn_rest(j):
        for i in range(share // LANE):
            part = pl.ds(multiple(j * share + i * LANE, LANE), LANE)
            mturned_rest[part, :] = mkept_rest[:, part].T

    def seconds_of(j):
        return pl.ds(multiple(j * share + part_rows, part_rows), part_rows)

    my_second = seconds_of(f)
    for s, j, to in ((0, f, far), (1, far, sib)):
        receive(mturn_hop.at[s], turn_hop_send.at[2 + s], turn_hop_recv.at[2 + s], (over, j))
        send(mturn_hop.at[s], prev_ref.at[:, firsts_of(j)], turn_send.at[3 + s], turn_recv.at[3 + s], (over, to))

    when(is_end, rest_of_next)
    when(is_near, rest_of_prev)

    own_group(far_half)
    add_products(same_gram, rows, far_half, False)
    row_values(inv_ref, lagged, share)

    def between(h):
        if h == 0:
            for s, j, to in ((0, f, far), (1, far, sib)):
                receive(turn_hop.at[s], turn_hop_send.at[s], turn_hop_recv.at[s], (over, j))
                send(turn_hop.at[s], next_ref.at[lower, group(j)], turn_send.at[s], turn_recv.at[s], (over, to))
            when(is_end, relay_rest_of_next)
            when(is_near, relay_rest_of_prev)

    tile(same_gram, same_ref, all_columns, PARTS, between)

    def await_mk():
        for p in range(PARTS):
            receive(mk_spot(p), mk_send.at[p], mk_recv.at[p], (after, f))

    def await_k():
        for p in range(4 * PARTS):
            receive(k_spot(p), k_send.at[p], k_recv.at[p], (before, f))

    when(has_m, await_mk)
    when(has_n, await_k)

    def await_rest(i, dst, source):
        receive(dst, rest_send.at[i], rest_recv.at[i], (b, source))

    for i, j in enumerate((far, cross, sib)):
        when(is_end, functools.partial(await_rest, i, next_ref.at[upper, group(j)], j))
        when(is_near, functools.partial(await_rest, 3 + i, prev_ref.at[:, seconds_of(j)], j))
    for s in range(2):
        leaves(rest_hop.at[s], rest_hop_send.at[s], rest_hop_recv.at[s], is_seam)
        leaves(rest_hop.at[s], rest_send.at[s], rest_recv.at[s], is_end)
        leaves(mrest_hop.at[s], rest_send.at[3 + s], rest_recv.at[3 + s], is_near)
    leaves(turned_rest.at[seconds(sib), :], rest_send.at[2], rest_recv.at[2], is_end)
    leaves(mturned_rest.at[group(sib), :], rest_send.at[5], rest_recv.at[5], is_near)
    for i, j in enumerate((far, cross, sib)):
        receive(next_ref.at[lower, group(j)], turn_send.at[i], turn_recv.at[i], (b, j))
        receive(prev_ref.at[:, firsts_of(j)], turn_send.at[3 + i], turn_recv.at[3 + i], (b, j))
    for condition, copy in sent:
        if condition is None:
            copy.wait_send()
        else:
            when(condition, copy.wait_send)


def per_device(blocks, series, scales, width):
    block, quarter = series.shape
    dims, share, wide = 4 * quarter, block // 4, block + LANE
    part_rows = share // 2
    inv = (1.0 / scales.astype(jnp.float32)).reshape(block // LANE, LANE)
    out = jax.ShapeDtypeStruct((share, block), jnp.float32)
    raw = lambda *shape: pltpu.VMEM(shape, series.dtype)
    wider = lambda *shape: pltpu.VMEM(shape, jnp.float32)
    hops = 2 * CHUNKS
    pairs = (4, 1, hops, hops, hops, 4, 2, 6, 6, 4, 14, 2, PIECES, PIECES, 4 * PARTS, PARTS)
    counts = [n for n in pairs for _ in range(2)] + [hops]
    return pl.pallas_call(
        functools.partial(tiles_kernel, blocks),
        out_shape=(out, out, out),
        in_specs=[
            pl.BlockSpec(memory_space=pltpu.VMEM),
            pl.BlockSpec(memory_space=pltpu.VMEM),
            pl.BlockSpec(memory_space=pltpu.SMEM),
        ],
        out_specs=(pl.BlockSpec(memory_space=pltpu.VMEM),) * 3,
        scratch_shapes=[
            raw(wide, dims),
            raw(LEAD + share, dims),
            raw(LEAD + share, dims),
            raw(LEAD + part_rows, dims),
            raw(LEAD + part_rows, dims),
            wider(block // LANE, LANE),
            wider(block // LANE, LANE),
            wider(8 + LEAD + share, wide),
            wider(8 + LEAD + part_rows, wide),
            wider(8 + LEAD + share, wide),
            wider(LEAD + share, wide),
            wider(4, block // LANE, LANE),
        ]
        + [wider(block // LANE, LANE)] * 5
        + [
            wider(8, wide),
            wider(share, LANE),
            wider(share, LANE),
            wider(share, block // 2),
            wider(part_rows, block),
            wider(block // 2, share),
            wider(block, part_rows),
            wider(share, block // 2),
            wider(part_rows, block),
            wider(block // 2, share),
            wider(block, part_rows),
            raw(2, CHUNKS, 2 * share // CHUNKS, quarter),
            wider(2, part_rows, share),
            wider(2, share, part_rows),
            wider(2, part_rows, share),
            wider(2, share, part_rows),
        ]
        + [pltpu.SemaphoreType.DMA((n,)) for n in counts],
        compiler_params=pltpu.CompilerParams(
            collective_id=0, has_side_effects=True, vmem_limit_bytes=48 * 1024 * 1024
        ),
    )(series, inv, width)


def solution(mesh):
    in_specs = (P("blk", "feat"), P("blk"), P())
    out_specs = (P(("blk", "feat"), None), P(("blk", "feat"), None), P(("blk", "feat"), None))
    return jax.shard_map(
        functools.partial(per_device, mesh.shape["blk"]),
        mesh=mesh,
        in_specs=in_specs,
        out_specs=out_specs,
        check_vma=False,
    )
```

```python
import functools

import jax
import jax.numpy as jnp
from jax import lax
from jax.experimental import pallas as pl
from jax.experimental.pallas import tpu as pltpu
from jax.sharding import PartitionSpec as P

LAGS = 24
LEAD = 32
LANE = 128
CHUNKS = 8
PIECES = 8
PARTS = 2
MESH = pl.DeviceIdType.MESH
CONTRACT_LAST = (((1,), (1,)), ((), ()))


def multiple(value, of):
    return pl.multiple_of(value, of)


def tiles_kernel(
    blocks,
    series_ref,
    inv_ref,
    width_ref,
    same_ref,
    next_ref,
    prev_ref,
    whole,
    rows,
    nrows,
    mrows,
    mrows_rest,
    ninv,
    minv,
    gram,
    mgram,
    same_gram,
    sums,
    partial,
    squared,
    past_squared,
    lagged,
    nlagged,
    mlagged,
    norms,
    row_norms,
    row_factor,
    kept,
    mkept,
    turned,
    mturned,
    kept_rest,
    mkept_rest,
    turned_rest,
    mturned_rest,
    hop,
    turn_hop,
    mturn_hop,
    rest_hop,
    mrest_hop,
    tail_send,
    tail_recv,
    sib_send,
    sib_recv,
    hop_send,
    hop_recv,
    far_send,
    far_recv,
    pass_send,
    pass_recv,
    lead_send,
    lead_recv,
    inv_send,
    inv_recv,
    square_send,
    square_recv,
    turn_send,
    turn_recv,
    turn_hop_send,
    turn_hop_recv,
    rest_send,
    rest_recv,
    rest_hop_send,
    rest_hop_recv,
    n_send,
    n_recv,
    m_send,
    m_recv,
    k_send,
    k_recv,
    mk_send,
    mk_recv,
    ride_send,
):
    block, quarter = series_ref.shape
    dims = 4 * quarter
    share = block // 4
    part_rows = share // 2
    wide = block + LANE
    past = wide - LEAD

    b, f = lax.axis_index("blk"), lax.axis_index("feat")
    core, chip = lax.rem(f, 2), f // 2
    sib, far, cross = f + 1 - 2 * core, lax.rem(f + 2, 4), 3 - f
    after, before = lax.rem(b + 1, blocks), lax.rem(b + blocks - 1, blocks)
    half = blocks // 2
    pos, first = lax.rem(b, half), (b // half) * half
    over = lax.rem(b + half, blocks)
    others = (sib, far, cross)
    everyone = (f, sib, far, cross)
    near, end = first, first + half - 1
    is_near, is_end = pos == 0, pos == half - 1
    is_seam = jnp.logical_or(is_near, is_end)
    ordinary = jnp.logical_not(is_seam)

    barrier = pltpu.get_barrier_semaphore()
    peers = [(b, j) for j in others] + [(after, f), (before, f)] + [(over, j) for j in (f, far, sib)]
    for peer in peers:
        pl.semaphore_signal(barrier, inc=1, device_id=peer, device_id_type=MESH)

    def greet(condition, corners):
        @pl.when(condition)
        def _():
            for corner in corners:
                pl.semaphore_signal(barrier, inc=1, device_id=corner, device_id_type=MESH)
            pl.semaphore_wait(barrier, len(peers) + len(corners))

    greet(is_near, [(end, f), (end, sib)])
    greet(is_end, [(near, f), (near, sib)])

    @pl.when(ordinary)
    def _():
        pl.semaphore_wait(barrier, len(peers))

    sent = []

    def copy_of(src, dst, send_sem, recv_sem, to):
        return pltpu.make_async_remote_copy(
            src_ref=src, dst_ref=dst, send_sem=send_sem, recv_sem=recv_sem, device_id=to, device_id_type=MESH
        )

    def post(src, dst, send_sem, recv_sem, to):
        copy_of(src, dst, send_sem, recv_sem, to).start()

    def leaves(src, send_sem, recv_sem, condition=None):
        sent.append((condition, copy_of(src, src, send_sem, recv_sem, (b, sib))))

    def send(src, dst, send_sem, recv_sem, to):
        post(src, dst, send_sem, recv_sem, to)
        leaves(src, send_sem, recv_sem)

    def receive(dst, send_sem, recv_sem, sender):
        copy_of(dst, dst, send_sem, recv_sem, sender).wait_recv()

    def when(condition, act):
        @pl.when(condition)
        def _():
            act()

    def cols(q):
        return pl.ds(multiple(q * quarter, quarter), quarter)

    def group(g):
        return pl.ds(multiple(g * share, share), share)

    def n_spot(p):
        return nrows.at[pl.ds(LEAD + (p % 2) * part_rows, part_rows), cols(everyone[p // 2])]

    def m_spot(p):
        size = part_rows // 2
        return mrows.at[pl.ds(LEAD + (p % 2) * size, size), cols(everyone[p // 2])]

    def k_spot(p):
        g, h = p % 4, p // 4
        return prev_ref.at[pl.ds(h * part_rows, part_rows), pl.ds(g * share + part_rows, part_rows)]

    def mk_spot(p):
        size = part_rows // PARTS
        return next_ref.at[pl.ds(p * size, size), :]

    quarter_rows = share // 4

    def own_rows(ref, start, size, columns):
        return ref.at[pl.ds(multiple(f * share + start, size), size), columns]

    def send_n(ref, qi, columns, condition):
        for p in (2 * qi, 2 * qi + 1):
            piece = own_rows(ref, (p % 2) * part_rows, part_rows, columns)
            when(condition, functools.partial(post, piece, n_spot(p), n_send.at[p], n_recv.at[p], (before, f)))

    def send_n_quarter(qi, i, condition):
        p, columns = 2 * qi + i // 2, cols(everyone[qi])
        piece = own_rows(whole, i * quarter_rows, quarter_rows, columns)
        spot = nrows.at[pl.ds(LEAD + i * quarter_rows, quarter_rows), columns]
        when(condition, functools.partial(post, piece, spot, n_send.at[p], n_recv.at[p], (before, f)))

    def send_m(ref, qi, columns, condition, pieces=(0, 1)):
        for i in pieces:
            p = 2 * qi + i
            piece = own_rows(ref, i * quarter_rows, quarter_rows, columns)
            when(condition, functools.partial(post, piece, m_spot(p), m_send.at[p], m_recv.at[p], (after, f)))

    def await_n(p):
        receive(n_spot(p), n_send.at[p], n_recv.at[p], (after, f))

    def await_m(p):
        receive(m_spot(p), m_send.at[p], m_recv.at[p], (before, f))

    has_n, has_m = jnp.logical_not(is_near), jnp.logical_not(is_end)

    def order(c, j):
        return j + c * (2, 2, -1, -3)[j]

    def place_of(k):
        return (k // 2 + 3) % 4

    def halved(sender, k, s):
        c = sender if s == 0 else 1 - sender
        usual = order(1 - sender, k // 2) * share + (k % 2) * 2 * quarter_rows + s * quarter_rows
        at_seam = (2 * c + k % 2) * share + place_of(k) * quarter_rows
        return pl.ds(multiple(jnp.where(is_seam, at_seam, usual), quarter_rows), quarter_rows)

    send(
        series_ref.at[pl.ds(block - LEAD, LEAD), :],
        whole.at[pl.ds(past, LEAD), cols(f)],
        tail_send.at[0],
        tail_recv.at[0],
        (after, f),
    )

    def set_out(k):
        for s, j in enumerate((f, far)):
            i = CHUNKS * s + k
            send(series_ref.at[halved(chip, k, s), :], hop.at[s, k], hop_send.at[i], hop_recv.at[i], (over, j))

    def hand_over(k):
        for s, j in enumerate((f, far)):
            i = CHUNKS * s + k
            receive(hop.at[s, k], hop_send.at[i], hop_recv.at[i], (over, j))
            c, to = (chip, far) if s == 0 else (1 - chip, f)
            send(hop.at[s, k], whole.at[halved(c, k, s), cols(j)], far_send.at[i], far_recv.at[i], (over, to))

            to, place = 2 * chip + k % 2, place_of(k)
            qi = lax.rem(core + k % 2, 2) + 2 * s
            spot = pl.ds(LEAD + place * quarter_rows, quarter_rows)

            def ride_back():
                post(
                    hop.at[s, k], nrows.at[spot, cols(j)], ride_send.at[i], n_recv.at[2 * qi + place // 2], (end, to)
                )

            def ride_on():
                at = pl.ds(LEAD + (place % 2) * quarter_rows, quarter_rows)
                rows_there = mrows if place < 2 else mrows_rest
                sem = m_recv.at[2 * qi + place] if place < 2 else rest_recv.at[6 + 2 * qi + place - 2]
                post(hop.at[s, k], rows_there.at[at, cols(j)], ride_send.at[i], sem, (near, to))

            when(is_near, ride_back)
            leaves(hop.at[s, k], ride_send.at[i], n_recv.at[0], is_near)
            when(is_end, ride_on)
            leaves(hop.at[s, k], ride_send.at[i], n_recv.at[0], is_end)

    set_out(0)
    send(series_ref, whole.at[pl.ds(0, block), cols(f)], sib_send.at[0], sib_recv.at[0], (b, sib))
    send_n(series_ref, 0, slice(None), has_n)
    send_m(series_ref, 0, slice(None), has_m)
    send(inv_ref, ninv, inv_send.at[0], inv_recv.at[0], (before, f))
    send(inv_ref, minv, inv_send.at[1], inv_recv.at[1], (after, f))

    whole[pl.ds(0, block), cols(f)] = series_ref[...]
    whole[pl.ds(block, LANE - LEAD), :] = jnp.zeros((LANE - LEAD, dims), whole.dtype)
    for buffer in (gram, mgram, same_gram):
        buffer[pl.ds(0, 8), :] = jnp.zeros((8, wide), jnp.float32)

    def pass_on(k):
        for s in range(2):
            i = CHUNKS * s + k
            piece = whole.at[halved(1 - chip, k, s), cols(far)]
            receive(piece, far_send.at[i], far_recv.at[i], (over, far if s == 0 else f))
            send(piece, piece, pass_send.at[i], pass_recv.at[i], (b, sib))

    def passed(k):
        for s in range(2):
            i = CHUNKS * s + k
            piece = whole.at[halved(1 - chip, k, s), cols(cross)]
            receive(piece, pass_send.at[i], pass_recv.at[i], (b, sib))

    lead = multiple(lax.rem(f * share + wide - LEAD, wide), LEAD)
    near_half = pl.ds(multiple(chip * 2 * quarter, quarter), 2 * quarter)
    far_half = pl.ds(multiple((1 - chip) * 2 * quarter, quarter), 2 * quarter)
    leads = (near_half, far_half)
    lead_ways = ((nrows, before, after), (mrows, after, before))

    def post_lead(i):
        for w, (dst, to, _) in enumerate(lead_ways):
            s = 2 * w + i
            post(
                whole.at[pl.ds(lead, LEAD), leads[i]],
                dst.at[pl.ds(0, LEAD), leads[i]],
                lead_send.at[s],
                lead_recv.at[s],
                (to, f),
            )

    def receive_lead(w, i):
        dst, _, sender = lead_ways[w]
        receive(dst.at[pl.ds(0, LEAD), leads[i]], lead_send.at[2 * w + i], lead_recv.at[2 * w + i], (sender, f))

    lines = block // LANE

    def square_lines(lines_now):
        for j in lines_now:
            x = whole[pl.ds(j * LANE, LANE), cols(f)]
            total = jnp.zeros((LANE, LANE), jnp.float32)
            for g in range(quarter // LANE):
                piece = x[:, g * LANE : (g + 1) * LANE].astype(jnp.float32)
                total = total + piece * piece
            partial[pl.ds(f, 1), pl.ds(j, 1), :] = jnp.sum(total.T, axis=0, keepdims=True)[None]

    def share_squares():
        for i, j in enumerate(others):
            send(partial.at[f], partial.at[f], square_send.at[i], square_recv.at[i], (b, j))

    def sum_squares():
        for i, j in enumerate(others):
            receive(partial.at[j], square_send.at[i], square_recv.at[i], (b, j))
        squared[...] = partial[0] + partial[1] + partial[2] + partial[3]
        send(squared, past_squared, square_send.at[3], square_recv.at[3], (after, f))

    def lag_squares():
        receive(past_squared, square_send.at[3], square_recv.at[3], (before, f))
        line = [squared[j : j + 1, :] for j in range(lines)] + [past_squared[lines - 1 : lines, :]]
        norms[...] = lag_sum(jnp.broadcast_to(jnp.concatenate(line, axis=1), (8, wide)), 1)
        for j in range(lines):
            lagged[j : j + 1, :] = norms[0:1, j * LANE : (j + 1) * LANE]
        send(lagged, nlagged, square_send.at[4], square_recv.at[4], (before, f))
        send(lagged, mlagged, square_send.at[5], square_recv.at[5], (after, f))

    def lag_sum(x, axis):
        for step in (1, 2, 4):
            x = x + pltpu.roll(x, step, axis)
        return x + pltpu.roll(x, 8, axis) + pltpu.roll(x, 16, axis)

    def products(left, right):
        return lax.dot_general(left, right, CONTRACT_LAST, preferred_element_type=jnp.float32)

    def own_group(which):
        rows[pl.ds(0, LEAD), which] = whole[pl.ds(lead, LEAD), which]
        rows[pl.ds(LEAD, share), which] = whole[group(f), which]

    def add_products(target, source, which, fresh):
        size, height = 256, source.shape[0]
        for start in range(0, wide, size):
            part = pl.ds(start, min(size, wide - start))
            found = products(source[:, which], whole[part, which])
            if fresh:
                target[pl.ds(8, height), part] = found
            else:
                target[pl.ds(8, height), part] += found

    def near_products():
        for p in range(4):
            await_n(p)
        receive_lead(0, 0)
        add_products(gram, nrows, near_half, True)

    both = jnp.logical_and
    first_core, second_core = both(ordinary, core == 0), both(ordinary, core == 1)
    for k in range(CHUNKS):
        hand_over(k)
        if k + 1 < CHUNKS:
            set_out(k + 1)
        if k == 0:
            receive(whole.at[pl.ds(0, block), cols(sib)], sib_send.at[0], sib_recv.at[0], (b, sib))
            send_n(whole, 1, cols(sib), has_n)
            send_m(whole, 1, cols(sib), has_m)
            tail = whole.at[pl.ds(past, LEAD), cols(f)]
            receive(tail, tail_send.at[0], tail_recv.at[0], (before, f))
            for i, j in enumerate(others):
                send(tail, tail, tail_send.at[1 + i], tail_recv.at[1 + i], (b, j))
            square_lines(range(lines // 2))
        else:
            pass_on(k - 1)
        if k == 1:
            square_lines(range(lines // 2, lines))
            share_squares()
        if k == 2:
            for i, j in enumerate(others):
                receive(whole.at[pl.ds(past, LEAD), cols(j)], tail_send.at[1 + i], tail_recv.at[1 + i], (b, j))
            post_lead(0)
            send_n(whole, 2, cols(far), first_core)
            send_m(whole, 2, cols(far), first_core)
            send_n_quarter(2, place_of(0), is_end)
            sum_squares()
        if k == 3:
            send_m(whole, 2, cols(far), second_core)
            passed(0)
            passed(1)
            send_n(whole, 3, cols(cross), first_core)
            send_m(whole, 3, cols(cross), first_core)
            send_n_quarter(3, place_of(0), is_end)
            when(is_seam, lambda: post_lead(1))
            lag_squares()
        if k == 4:
            send_n(whole, 2, cols(far), second_core)
            passed(2)
            send_m(whole, 3, cols(cross), second_core)
            send_n_quarter(2, place_of(2), is_end)
            send_m(whole, 2, cols(far), is_near, (0,))
        if k == 5:
            passed(3)
            send_n(whole, 3, cols(cross), second_core)
            send_n_quarter(3, place_of(2), is_end)
            send_m(whole, 3, cols(cross), is_near, (0,))
            own_group(near_half)
            add_products(same_gram, rows, near_half, True)
        if k == 6:
            send_n_quarter(2, place_of(4), is_end)
            send_m(whole, 2, cols(far), is_near, (1,))
            for p in range(4):
                await_m(p)
            receive_lead(1, 0)
            add_products(mgram, mrows, near_half, True)
        if k == 7:
            passed(4)
            passed(5)
            send_n_quarter(3, place_of(4), is_end)
            send_m(whole, 3, cols(cross), is_near, (1,))
            when(ordinary, lambda: post_lead(1))
            when(jnp.logical_not(is_end), near_products)
    pass_on(7)
    send_n_quarter(2, place_of(6), is_end)
    passed(6)
    passed(7)
    send_n_quarter(3, place_of(6), is_end)
    for i in range(2):
        for w in range(2):
            leaves(whole.at[pl.ds(lead, LEAD), leads[i]], lead_send.at[2 * w + i], lead_recv.at[2 * w + i])
    for p in range(8):
        leaves(n_spot(p), n_send.at[p], n_recv.at[p], has_n)
        leaves(m_spot(p), m_send.at[p], m_recv.at[p], has_m)
    when(is_end, near_products)

    inv_row = jnp.concatenate([inv_ref[j : j + 1, :] for j in range(block // LANE)], axis=1)
    width_row = jnp.full((1, LANE), width_ref[0], jnp.float32) * (LAGS * dims)

    def down(line):
        return jnp.broadcast_to(line, (LANE, LANE)).T

    def row_values(inv, squares, count, skip=0):
        for j in range(count // LANE):
            line, part = pl.ds(f * (share // LANE) + skip + j, 1), pl.ds(j * LANE, LANE)
            row_factor[part, :] = down(-inv[line, :] / width_row)
            row_norms[part, :] = down(squares[line, :])

    middle = block // 2

    def with_lead(ref, part, c):
        if c:
            return ref[part, middle - LANE : block]
        return jnp.concatenate([ref[part, block:wide], ref[part, :middle]], axis=1)

    def all_columns(c):
        return [(c * middle, middle)]

    def first_halves(c):
        return [(g * share, part_rows) for g in (2 * c, 2 * c + 1)]

    def second_halves(c):
        return [(g * share + part_rows, part_rows) for g in (2 * c, 2 * c + 1)]

    def tile(products_of, target, pick, parts, ready, summed=False):
        per = target.shape[0] // 32 // parts
        span = target.shape[1] // 2
        for h in range(parts):
            for c in range(2):
                for t in () if summed else range(h * per + 1 if h else 0, (h + 1) * per + 1):
                    x = with_lead(products_of, pl.ds(t * 32, 40), c)
                    for step in (1, 2, 4):
                        x = x + pltpu.roll(pltpu.roll(x, step, 0), step, 1)
                    part = pl.ds(t * 32, 32)
                    sums[part, c * middle : (c + 1) * middle] = x[8:, LANE:]
                    if c == 0:
                        sums[part, block:wide] = x[8:, :LANE]
                picked = lambda x, base: jnp.concatenate([x[:, s - base : s - base + n] for s, n in pick(c)], axis=1)
                for t in range(h * per, (h + 1) * per):
                    x = with_lead(sums, pl.ds(t * 32 + 32, 32), c)
                    x = x + pltpu.roll(with_lead(sums, pl.ds(t * 32 + 24, 32), c), 8, 1)
                    x = x + pltpu.roll(with_lead(sums, pl.ds(t * 32 + 16, 32), c), 16, 1)
                    part = pl.ds(t * 32, 32)
                    found = picked(x, c * middle - LANE)
                    spread = row_norms[part, :][:, :1] + picked(norms[pl.ds(0, 1), :], 0) - 2.0 * found
                    values = jnp.exp(spread * (row_factor[part, :][:, :1] * picked(inv_row, 0)))
                    target[part, c * span : (c + 1) * span] = values
            ready(h)

    receive(minv, inv_send.at[1], inv_recv.at[1], (before, f))
    receive(ninv, inv_send.at[0], inv_recv.at[0], (after, f))
    receive(nlagged, square_send.at[4], square_recv.at[4], (after, f))
    receive(mlagged, square_send.at[5], square_recv.at[5], (before, f))
    row_values(minv, mlagged, part_rows)
    for p in range(4, 8):
        await_m(p)
    receive_lead(1, 1)
    add_products(mgram, mrows, far_half, False)

    def send_mk(h):
        piece = mkept.at[pl.ds(h * (part_rows // PARTS), part_rows // PARTS), :]
        when(has_n, functools.partial(post, piece, mk_spot(h), mk_send.at[h], mk_recv.at[h], (before, f)))
        leaves(piece, mk_send.at[h], mk_recv.at[h], has_n)

    tile(mgram, mkept, all_columns, PARTS, send_mk)

    my_columns = pl.ds(multiple(f * share, share), share)
    my_first = pl.ds(multiple(f * share, part_rows), part_rows)
    lower = pl.ds(part_rows, part_rows)
    hops = ((0, far, f), (1, cross, far))

    def own_transposed(source):
        lines = [source[:, pl.ds(multiple(f * share + i * LANE, LANE), LANE)].T for i in range(share // LANE)]
        return jnp.concatenate(lines, axis=0)

    def turn_m(j):
        for i in range(share // LANE):
            part = pl.ds(multiple(j * share + i * LANE, LANE), LANE)
            mturned[part, :] = mkept[:, part].T

    for s, j, by in hops:
        turn_m(j)
        send(mturned.at[group(j), :], mturn_hop.at[s], turn_hop_send.at[2 + s], turn_hop_recv.at[2 + s], (over, by))
    turn_m(sib)
    send(mturned.at[group(sib), :], prev_ref.at[:, my_first], turn_send.at[5], turn_recv.at[5], (b, sib))
    prev_ref[:, my_first] = own_transposed(mkept)

    row_values(ninv, nlagged, share)
    for p in range(4, 8):
        await_n(p)
    receive_lead(0, 1)
    add_products(gram, nrows, far_half, False)

    def send_k(h):
        for g in range(4):
            piece, p = kept.at[pl.ds(h * part_rows, part_rows), pl.ds(g * part_rows, part_rows)], 4 * h + g
            when(has_m, functools.partial(post, piece, k_spot(p), k_send.at[p], k_recv.at[p], (after, f)))
            leaves(piece, k_send.at[p], k_recv.at[p], has_m)

    tile(gram, kept, second_halves, PARTS, send_k)

    def seconds(j):
        return pl.ds(multiple(j * part_rows, part_rows), part_rows)

    def turn(j):
        turned[seconds(j), :] = kept[:, seconds(j)].T

    for s, j, by in hops:
        turn(j)
        send(turned.at[seconds(j), :], turn_hop.at[s], turn_hop_send.at[s], turn_hop_recv.at[s], (over, by))
    turn(sib)
    send(turned.at[seconds(sib), :], next_ref.at[lower, my_columns], turn_send.at[2], turn_recv.at[2], (b, sib))
    next_ref[lower, my_columns] = kept[:, seconds(f)].T

    def firsts_of(j):
        return pl.ds(multiple(j * share, part_rows), part_rows)

    upper = pl.ds(0, part_rows)

    def rest_of_next():
        tile(gram, kept_rest, first_halves, 1, lambda h: None, summed=True)
        for s, j, by in hops:
            turned_rest[seconds(j), :] = kept_rest[:, seconds(j)].T
            post(turned_rest.at[seconds(j), :], rest_hop.at[s], rest_hop_send.at[s], rest_hop_recv.at[s], (over, by))
        turned_rest[seconds(sib), :] = kept_rest[:, seconds(sib)].T
        post(
            turned_rest.at[seconds(sib), :],
            next_ref.at[upper, my_columns],
            rest_send.at[2],
            rest_recv.at[2],
            (b, sib),
        )
        next_ref[upper, my_columns] = kept_rest[:, seconds(f)].T

    def relay_rest_of_next():
        for s, j, to in ((0, f, far), (1, far, sib)):
            receive(rest_hop.at[s], rest_hop_send.at[s], rest_hop_recv.at[s], (over, j))
            post(rest_hop.at[s], next_ref.at[upper, group(j)], rest_send.at[s], rest_recv.at[s], (over, to))

    def rest_of_prev():
        for qi in range(4):
            for i in range(2):
                sem = 6 + 2 * qi + i
                spot = mrows_rest.at[pl.ds(LEAD + i * quarter_rows, quarter_rows), cols(everyone[qi])]
                receive(spot, rest_send.at[sem], rest_recv.at[sem], (before, f))
        mrows_rest[pl.ds(0, LEAD), :] = mrows[pl.ds(part_rows, LEAD), :]
        add_products(mgram, mrows_rest, slice(None), True)
        row_values(minv, mlagged, part_rows, 1)
        tile(mgram, mkept_rest, all_columns, 1, lambda h: None)
        for s, j, by in hops:
            turn_rest(j)
            post(mturned_rest.at[group(j), :], mrest_hop.at[s], rest_hop_send.at[s], rest_hop_recv.at[s], (over, by))
        turn_rest(sib)
        post(mturned_rest.at[group(sib), :], prev_ref.at[:, my_second], rest_send.at[5], rest_recv.at[5], (b, sib))
        prev_ref[:, my_second] = own_transposed(mkept_rest)

    def relay_rest_of_prev():
        for s, j, to in ((0, f, far), (1, far, sib)):
            receive(mrest_hop.at[s], rest_hop_send.at[s], rest_hop_recv.at[s], (over, j))
            post(mrest_hop.at[s], prev_ref.at[:, seconds_of(j)], rest_send.at[3 + s], rest_recv.at[3 + s], (over, to))

    def turn_rest(j):
        for i in range(share // LANE):
            part = pl.ds(multiple(j * share + i * LANE, LANE), LANE)
            mturned_rest[part, :] = mkept_rest[:, part].T

    def seconds_of(j):
        return pl.ds(multiple(j * share + part_rows, part_rows), part_rows)

    my_second = seconds_of(f)
    for s, j, to in ((0, f, far), (1, far, sib)):
        receive(mturn_hop.at[s], turn_hop_send.at[2 + s], turn_hop_recv.at[2 + s], (over, j))
        send(mturn_hop.at[s], prev_ref.at[:, firsts_of(j)], turn_send.at[3 + s], turn_recv.at[3 + s], (over, to))

    when(is_end, rest_of_next)
    when(is_near, rest_of_prev)

    own_group(far_half)
    add_products(same_gram, rows, far_half, False)
    row_values(inv_ref, lagged, share)

    def between(h):
        if h == 0:
            for s, j, to in ((0, f, far), (1, far, sib)):
                receive(turn_hop.at[s], turn_hop_send.at[s], turn_hop_recv.at[s], (over, j))
                send(turn_hop.at[s], next_ref.at[lower, group(j)], turn_send.at[s], turn_recv.at[s], (over, to))
            when(is_end, relay_rest_of_next)
            when(is_near, relay_rest_of_prev)

    tile(same_gram, same_ref, all_columns, PARTS, between)

    def await_mk():
        for p in range(PARTS):
            receive(mk_spot(p), mk_send.at[p], mk_recv.at[p], (after, f))

    def await_k():
        for p in range(4 * PARTS):
            receive(k_spot(p), k_send.at[p], k_recv.at[p], (before, f))

    when(has_m, await_mk)
    when(has_n, await_k)

    def await_rest(i, dst, source):
        receive(dst, rest_send.at[i], rest_recv.at[i], (b, source))

    for i, j in enumerate((far, cross, sib)):
        when(is_end, functools.partial(await_rest, i, next_ref.at[upper, group(j)], j))
        when(is_near, functools.partial(await_rest, 3 + i, prev_ref.at[:, seconds_of(j)], j))
    for s in range(2):
        leaves(rest_hop.at[s], rest_hop_send.at[s], rest_hop_recv.at[s], is_seam)
        leaves(rest_hop.at[s], rest_send.at[s], rest_recv.at[s], is_end)
        leaves(mrest_hop.at[s], rest_send.at[3 + s], rest_recv.at[3 + s], is_near)
    leaves(turned_rest.at[seconds(sib), :], rest_send.at[2], rest_recv.at[2], is_end)
    leaves(mturned_rest.at[group(sib), :], rest_send.at[5], rest_recv.at[5], is_near)
    for i, j in enumerate((far, cross, sib)):
        receive(next_ref.at[lower, group(j)], turn_send.at[i], turn_recv.at[i], (b, j))
        receive(prev_ref.at[:, firsts_of(j)], turn_send.at[3 + i], turn_recv.at[3 + i], (b, j))
    for condition, copy in sent:
        if condition is None:
            copy.wait_send()
        else:
            when(condition, copy.wait_send)


def per_device(blocks, series, scales, width):
    block, quarter = series.shape
    dims, share, wide = 4 * quarter, block // 4, block + LANE
    part_rows = share // 2
    inv = (1.0 / scales.astype(jnp.float32)).reshape(block // LANE, LANE)
    out = jax.ShapeDtypeStruct((share, block), jnp.float32)
    raw = lambda *shape: pltpu.VMEM(shape, series.dtype)
    wider = lambda *shape: pltpu.VMEM(shape, jnp.float32)
    hops = 2 * CHUNKS
    pairs = (4, 1, hops, hops, hops, 4, 2, 6, 6, 4, 14, 2, PIECES, PIECES, 4 * PARTS, PARTS)
    counts = [n for n in pairs for _ in range(2)] + [hops]
    return pl.pallas_call(
        functools.partial(tiles_kernel, blocks),
        out_shape=(out, out, out),
        in_specs=[
            pl.BlockSpec(memory_space=pltpu.VMEM),
            pl.BlockSpec(memory_space=pltpu.VMEM),
            pl.BlockSpec(memory_space=pltpu.SMEM),
        ],
        out_specs=(pl.BlockSpec(memory_space=pltpu.VMEM),) * 3,
        scratch_shapes=[
            raw(wide, dims),
            raw(LEAD + share, dims),
            raw(LEAD + share, dims),
            raw(LEAD + part_rows, dims),
            raw(LEAD + part_rows, dims),
            wider(block // LANE, LANE),
            wider(block // LANE, LANE),
            wider(8 + LEAD + share, wide),
            wider(8 + LEAD + part_rows, wide),
            wider(8 + LEAD + share, wide),
            wider(LEAD + share, wide),
            wider(4, block // LANE, LANE),
        ]
        + [wider(block // LANE, LANE)] * 5
        + [
            wider(8, wide),
            wider(share, LANE),
            wider(share, LANE),
            wider(share, block // 2),
            wider(part_rows, block),
            wider(block // 2, share),
            wider(block, part_rows),
            wider(share, block // 2),
            wider(part_rows, block),
            wider(block // 2, share),
            wider(block, part_rows),
            raw(2, CHUNKS, 2 * share // CHUNKS, quarter),
            wider(2, part_rows, share),
            wider(2, share, part_rows),
            wider(2, part_rows, share),
            wider(2, share, part_rows),
        ]
        + [pltpu.SemaphoreType.DMA((n,)) for n in counts],
        compiler_params=pltpu.CompilerParams(
            collective_id=0, has_side_effects=True, vmem_limit_bytes=48 * 1024 * 1024
        ),
    )(series, inv, width)


def solution(mesh):
    in_specs = (P("blk", "feat"), P("blk"), P())
    out_specs = (P(("blk", "feat"), None), P(("blk", "feat"), None), P(("blk", "feat"), None))
    return jax.shard_map(
        functools.partial(per_device, mesh.shape["blk"]),
        mesh=mesh,
        in_specs=in_specs,
        out_specs=out_specs,
        check_vma=False,
    )
```
